32 devices in a mesh: groups: 2 (over y), chan: 4 (over z), tm: 2 (over core), dp: 2 (over x).
Axes of the slice: x: 2, y: 2, z: 4, core: 2. Of those that a mesh axis runs over, the one named last changes fastest.
Arguments:
- features: bfloat16 [384, 4, 8, 256], P('chan', ('groups', 'dp'), 'tm'), parts along dimension 1, may hold values from -6 to 6
- kernel: bfloat16 [384, 27, 384], P('chan'), may hold values from -0.078125 to 0.078125
- cotangent: bfloat16 [384, 4, 8, 256], P('chan', ('groups', 'dp'), 'tm'), parts along dimension 1, may hold values from -6 to 6
Outputs:
- conv_out: bfloat16 [384, 4, 8, 256], P('chan', ('groups', 'dp'), 'tm'), parts along dimension 1
- feature_grad: bfloat16 [384, 4, 8, 256], P('chan', ('groups', 'dp'), 'tm'), parts along dimension 1
- kernel_grad: float32 [768, 27, 384], P(('groups', 'chan')), parts along dimension 0
The draws below stay inside these ranges and needn't reach their ends.
There are 2 independent parts, one for each index of `groups`. The reference program is written for one: setup_inputs(seed, part) draws one part's arguments, and reference() takes and returns one part's arrays. A program takes and returns all parts, laid end to end along the dimension named above; an argument that names none is the same for every part. Nothing has to cross between parts.
All inputs are finite; a program needn't handle non-finite values.
Results may differ from the reference program's by a relative error of at most 0.0051.
Values may be sent and summed in bfloat16 or wider, within the bound.
No kernel may reach another device: no remote copies, remote signals or barrier semaphores. Data moves between devices by JAX's collectives and lax.ppermute only.
A program may use at most 128 MiB of HBM per device.

```python
import math
import jax
import jax.numpy as jnp
from jax import lax

C = 384
H_ROWS = 4
WID = 64
CLIPS = 2
FRAMES = 8
PIXELS = 256


def with_spikes(entries, stream_key, source, target, shards_of, factor):
    def block_of(axis_at):
        return (jnp.arange(entries.shape[axis_at]) // (entries.shape[axis_at] // shards_of)).reshape((-1,) + (1,) * (entries.ndim - 1 - axis_at))

    first = jax.random.permutation(stream_key, shards_of)[block_of(target)]
    far = (block_of(target) + shards_of // 2) % shards_of
    return jnp.where((block_of(source) == first) | (block_of(source) == far), factor * entries, entries)


def block_levels(key, extent, shards, least, high):
    gain, own = 1.0, jax.random.fold_in(key, 6)
    for position, shards_of in shards:
        draws = jnp.exp(jax.random.uniform(jax.random.fold_in(own, position), (shards_of,), jnp.float32, least / len(shards), high / len(shards)))
        gain = gain * jnp.repeat(draws, extent[position] // shards_of).reshape([-1 if axis == position else 1 for axis in range(len(extent))])
    return gain


def gaussian(stream_key, shape, scale, limit, pieces=(), kind=jnp.bfloat16):
    loudness = block_levels(stream_key, shape, pieces, -0.22, 0.18) if pieces else 1.0
    drawn = jax.random.normal(stream_key, shape, jnp.float32) * scale * loudness
    return jnp.minimum(jnp.maximum(drawn, -limit), limit).astype(kind)


def gaussian_with(rng, extent, scale, reach, shards, heavy, kind=jnp.bfloat16):
    array = scale * jax.random.normal(rng, extent, jnp.float32)
    if shards:
        array = array * block_levels(rng, extent, shards, -0.22, 0.18)
    return jnp.clip(with_spikes(array, jax.random.fold_in(rng, 3), *heavy), -reach, reach).astype(kind)


def setup_inputs(seed: int = 0, part: int = 0) -> dict:
    streams_of = jax.random.split(jax.random.key(seed), 4)
    part_keys = jax.random.split(jax.random.fold_in(streams_of[3], part), 4)
    features = gaussian(part_keys[0], (C, CLIPS, FRAMES, PIXELS), 1.0, 6.0, ((0, 4), (1, 2), (2, 2)))
    kernel = gaussian_with(streams_of[1], (C, 27, C), (27 * C) ** -0.5, 0.078125, ((0, 4),), (0, 2, 4, 2.0))
    cotangent = gaussian(part_keys[2], (C, CLIPS, FRAMES, PIXELS), 1.0, 6.0, ((0, 4), (1, 2), (2, 2)))
    return {"features": features, "kernel": kernel, "cotangent": cotangent}


def reference(features, kernel, cotangent):
    widened = features.astype(jnp.float32)
    logistic = jax.nn.sigmoid(widened)
    activation = lax.optimization_barrier((widened * logistic).astype(jnp.bfloat16)).astype(jnp.float32)
    slope_factor = logistic * (1.0 + widened * (1.0 - logistic))
    grid_shape = (C, CLIPS, FRAMES, H_ROWS, WID)
    activation_grid = jnp.pad(activation.reshape(grid_shape), ((0, 0), (0, 0), (2, 0), (1, 1), (1, 1)))
    cotangent_wide = cotangent.astype(jnp.float32)
    cotangent_grid = jnp.pad(cotangent_wide.reshape(grid_shape), ((0, 0), (0, 0), (0, 2), (1, 1), (1, 1)))
    cotangent_rows = cotangent_wide.reshape(C, -1)
    kernel_wide = kernel.astype(jnp.float32)
    out_sum = jnp.zeros((C, CLIPS * FRAMES * PIXELS), jnp.float32)
    before_slope = jnp.zeros((C, CLIPS * FRAMES * PIXELS), jnp.float32)
    grad_parts = []
    for temporal in range(3):
        for vertical in range(3):
            for horizontal in range(3):
                tap_index = 9 * temporal + 3 * vertical + horizontal
                tap_matrix = kernel_wide[:, tap_index, :]
                shifted = activation_grid[:, :, temporal:temporal + FRAMES, vertical:vertical + H_ROWS, horizontal:horizontal + WID].reshape(C, -1)
                out_sum = out_sum + jnp.dot(tap_matrix, shifted, preferred_element_type=jnp.float32)
                grad_parts.append(jnp.dot(cotangent_rows, shifted.T, preferred_element_type=jnp.float32))
                flipped = cotangent_grid[:, :, 2 - temporal:2 - temporal + FRAMES, 2 - vertical:2 - vertical + H_ROWS, 2 - horizontal:2 - horizontal + WID].reshape(C, -1)
                before_slope = before_slope + jnp.dot(tap_matrix.T, flipped, preferred_element_type=jnp.float32)
    grad_scale = 1.0 / math.sqrt(CLIPS * FRAMES * PIXELS)
    conv_out = out_sum.reshape(features.shape).astype(jnp.bfloat16)
    feature_grad = (before_slope.reshape(features.shape) * slope_factor).astype(jnp.bfloat16)
    kernel_grad = jnp.stack(grad_parts, axis=1) * grad_scale
    return (conv_out, feature_grad, kernel_grad)
```

```python
import functools
import math

import jax
import jax.numpy as jnp
from jax import lax
from jax.experimental import pallas as pl
from jax.experimental.pallas import tpu as pltpu
from jax.sharding import PartitionSpec as P

WID = 64
SUB = 16
F32 = jnp.float32
BF16 = jnp.bfloat16
VMEM_LIMIT = 40 * 1024 * 1024


def from_behind(x, axis, by):
    size = lax.axis_size(axis)
    pairs = [(i, i + by) for i in range(size) if 0 <= i + by < size]
    return lax.ppermute(x, axis, pairs)


def padded_copies(block):
    pixels = block.shape[-1]
    column = lax.broadcasted_iota(jnp.int32, (pixels,), 0) % WID
    nothing = jnp.zeros((), block.dtype)
    widths = [(0, 0), (0, 0), (0, 0), (WID + 1, WID + 1)]
    left_cut = jnp.pad(jnp.where(column == WID - 1, nothing, block), widths)
    untouched = jnp.pad(block, widths)
    right_cut = jnp.pad(jnp.where(column == 0, nothing, block), widths)
    return (left_cut, untouched, right_cut)


def tap_window(copies, first_frame, vertical, horizontal, frames, pixels):
    source = copies[horizontal]
    offset = vertical * WID + horizontal
    return source[:, :, first_frame : first_frame + frames, offset : offset + pixels]


def stacked_taps(copies, first_frame, flipped, frames, pixels):
    pieces = []
    for vertical in range(3):
        for horizontal in range(3):
            if flipped:
                pieces.append(
                    tap_window(copies, first_frame, 2 - vertical, 2 - horizontal, frames, pixels)
                )
            else:
                pieces.append(tap_window(copies, first_frame, vertical, horizontal, frames, pixels))
    concatenated = jnp.concatenate(pieces, axis=0)
    return concatenated.reshape(concatenated.shape[0], -1)


def local_generic(features, kernel, cotangent):
    channels, clip_count, frames, pixels = features.shape
    flat_length = clip_count * frames * pixels
    widened = features.astype(F32)
    logistic = jax.nn.sigmoid(widened)
    activation = (widened * logistic).astype(BF16)
    slope_factor = logistic * (1.0 + widened * (1.0 - logistic))
    earlier = from_behind(activation[:, :, frames - 2 :, :], "tm", 1)
    extended = jnp.concatenate([earlier, activation], axis=2)
    upcoming = from_behind(cotangent[:, :, :2, :], "tm", -1)
    later_padded = jnp.concatenate([cotangent, upcoming], axis=2)
    cotangent_rows = cotangent.reshape(channels, -1)
    portion = lax.all_gather(extended, "chan", axis=0, tiled=True)
    out_sum = jnp.zeros((channels, flat_length), F32)
    amount = portion.shape[0]
    copies = padded_copies(portion)
    grad_parts = []
    for temporal in range(3):
        stacked = stacked_taps(copies, temporal, False, frames, pixels)
        weights = kernel[:, 9 * temporal : 9 * temporal + 9, :].reshape(channels, 9 * amount)
        out_sum = out_sum + jnp.dot(weights, stacked, preferred_element_type=F32)
        grad_parts.append(
            lax.dot_general(
                cotangent_rows, stacked, (((1,), (1,)), ((), ())), preferred_element_type=F32
            ).reshape(channels, 9, amount)
        )
    grad_sum = jnp.concatenate(grad_parts, axis=1)
    conv_out = out_sum.reshape(features.shape).astype(BF16)
    position_count = lax.axis_size("dp") * lax.axis_size("tm") * flat_length
    kernel_grad = lax.psum(grad_sum, ("tm", "dp")) * (1.0 / math.sqrt(position_count))
    padded_later = padded_copies(later_padded)
    summed = jnp.zeros((amount, flat_length), F32)
    for temporal in range(3):
        weights = jnp.transpose(
            kernel[:, 9 * temporal : 9 * temporal + 9, :], (2, 1, 0)
        ).reshape(amount, 9 * channels)
        stacked = stacked_taps(padded_later, 2 - temporal, True, frames, pixels)
        summed = summed + jnp.dot(weights, stacked, preferred_element_type=F32)
    before_slope = lax.psum_scatter(
        summed.reshape(amount, clip_count, frames, pixels), "chan", scatter_dimension=0, tiled=True
    )
    feature_grad = (before_slope * slope_factor).astype(BF16)
    return (conv_out, feature_grad, kernel_grad)


def rotate(x, axis, by):
    size = lax.axis_size(axis)
    return lax.ppermute(x, axis, [(i, (i + by) % size) for i in range(size)])


def shifted(frame, down, right):
    pixels = frame.shape[-1]
    if down == 0 and right == 0:
        return frame
    cell = lax.broadcasted_iota(jnp.int32, (1, pixels), 1)
    row, column = cell // WID + down, cell % WID + right
    inside = (row >= 0) & (row < pixels // WID) & (column >= 0) & (column < WID)
    moved = pltpu.roll(frame, (-(down * WID + right)) % pixels, 1)
    return jnp.where(inside, moved, 0.0)


def params(**more):
    return pltpu.CompilerParams(vmem_limit_bytes=VMEM_LIMIT, **more)


def cost(flops, bytes_accessed):
    return pl.CostEstimate(
        flops=int(flops), bytes_accessed=int(bytes_accessed), transcendentals=0
    )


def whole():
    return pl.BlockSpec(memory_space=pltpu.VMEM)


def activate_kernel(features, cotangent, activation, pair):
    frames, pixels = features.shape[2:]
    v = features[:, 0].astype(F32)
    act = v / (1.0 + jnp.exp(-v))
    cot = cotangent[:, 0].astype(F32)
    for t in range(frames):
        lanes = slice(t * pixels, (t + 1) * pixels)
        piece = act[:, t, :].astype(BF16)
        activation[:, lanes] = piece
        pair[0, :, lanes] = piece
        pair[1, :, lanes] = cot[:, t, :].astype(BF16)


def share_kernel(pixels, weights, mine, other, own, *rest):
    sends, (stack, total) = rest[:-2], rest[-2:]
    rows, length = mine.shape[1:]
    frames = length // pixels
    me, z = lax.axis_index("tm"), lax.axis_index("chan")
    count = len(sends) + 1
    for t in range(frames + 2):
        if t < frames:
            frame = mine[1, :, t * pixels : (t + 1) * pixels].astype(F32)
        else:
            frame = other[1, :, (t - frames) * pixels : (t - frames + 1) * pixels].astype(F32)
            frame = jnp.where(me == 0, frame, 0.0)
        for i in range(3):
            for j in range(3):
                at = (3 * i + j) * rows
                stack[at : at + rows, t * pixels : (t + 1) * pixels] = shifted(
                    frame, 1 - i, 1 - j
                ).astype(BF16)
    taps = 9 * rows
    for t in range(frames):
        acc = None
        for a in range(3):
            term = lax.dot_general(
                weights[a * taps : (a + 1) * taps, :],
                stack[:, (t + 2 - a) * pixels : (t + 3 - a) * pixels],
                (((0,), (0,)), ((), ())),
                preferred_element_type=F32,
            )
            acc = term if acc is None else acc + term
        total[:, t * pixels : (t + 1) * pixels] = acc
    own[...] = total[pl.ds(pl.multiple_of(z * rows, SUB), rows), :]
    for d, send in enumerate(sends, 1):
        to = lax.rem(z + d, count)
        send[...] = total[pl.ds(pl.multiple_of(to * rows, SUB), rows), :].astype(BF16)


def gather_kernel(pixels, *refs):
    mine, other, out = refs[0], refs[1], refs[-1]
    blocks = refs[2:-1]
    rows, length = mine.shape[1:]
    me, z = lax.axis_index("tm"), lax.axis_index("chan")
    count = len(blocks) // 2 + 1
    front = 2 * pixels
    out[:, :front] = jnp.zeros((out.shape[0], front), BF16)
    here = pl.ds(pl.multiple_of(front + me * length, pixels), length)
    there = pl.ds(pl.multiple_of(front + (1 - me) * length, pixels), length)
    at = pl.ds(pl.multiple_of(z * rows, SUB), rows)
    out[at, here] = mine[0]
    out[at, there] = other[0]
    for d in range(1, count):
        at = pl.ds(pl.multiple_of(lax.rem(z + count - d, count) * rows, SUB), rows)
        out[at, here] = blocks[d - 1][...]
        out[at, there] = blocks[count - 2 + d][...]


def grad_kernel(pixels, chunk, mine, other, act, out, stack):
    rows, length = mine.shape[1:]
    frames = length // pixels
    me = lax.axis_index("tm")
    at = pl.ds(pl.multiple_of(me * (rows // 2) + chunk * SUB, SUB), SUB)
    here = mine[1, at, :]
    there = other[1, at, :]
    first = jnp.where(me == 0, here, there)
    second = jnp.where(me == 0, there, here)
    for t in range(2 * frames):
        source = first if t < frames else second
        lanes = slice((t % frames) * pixels, (t % frames + 1) * pixels)
        frame = source[:, lanes].astype(F32)
        for i in range(3):
            for j in range(3):
                row = (3 * i + j) * SUB
                stack[row : row + SUB, t * pixels : (t + 1) * pixels] = shifted(
                    frame, 1 - i, 1 - j
                ).astype(BF16)
    channels = act.shape[0]
    for a in range(3):
        skip = (2 - a) * pixels
        out[:, a * channels : (a + 1) * channels] = lax.dot_general(
            stack[:, skip:],
            act[:, 2 * pixels : 2 * pixels + 2 * length - skip],
            (((1,), (1,)), ((), ())),
            preferred_element_type=F32,
        ).astype(BF16)


def conv_kernel(pixels, weights, act, out):
    rows, _, frames, _ = out.shape
    me = lax.axis_index("tm")
    taps = 9 * rows
    for t in range(frames):
        z = None
        for a in range(3):
            at = pl.multiple_of((me * frames + t + a) * pixels, pixels)
            term = jnp.dot(
                weights[a * taps : (a + 1) * taps, :],
                act[:, pl.ds(at, pixels)],
                preferred_element_type=F32,
            )
            z = term if z is None else z + term
        acc = None
        for i in range(3):
            for j in range(3):
                at = (3 * i + j) * rows
                moved = shifted(z[at : at + rows, :], i - 1, j - 1)
                acc = moved if acc is None else acc + moved
        out[:, 0, t, :] = acc.astype(BF16)


def feature_kernel(pixels, features, own, *rest):
    out, received = rest[-1], rest[:-1]
    frames = features.shape[2]
    total = own[...]
    for part in received:
        total = total + part[...].astype(F32)
    v = features[:, 0].astype(F32)
    s = 1.0 / (1.0 + jnp.exp(-v))
    slope = s * (1.0 + v * (1.0 - s))
    for t in range(frames):
        piece = total[:, t * pixels : (t + 1) * pixels] * slope[:, t, :]
        out[:, 0, t, :] = piece.astype(BF16)


def finish_kernel(scale, has_base, *refs):
    refs = refs[1:] if has_base else refs
    mine, got, other, other_got, out = refs
    me, half = lax.axis_index("tm"), pl.program_id(0)
    channels = out.shape[2]

    def write(left, right):
        for a in range(3):
            lanes = slice(a * channels, (a + 1) * channels)
            for tap in range(9):
                at = slice(tap * SUB, (tap + 1) * SUB)
                total = left[at, lanes].astype(F32) + right[at, lanes].astype(F32)
                out[:, 9 * a + tap, :] = total * scale

    @pl.when(me == half)
    def _():
        write(mine, got)

    @pl.when(me != half)
    def _():
        write(other, other_got)


def local_fast(features, kernel, cotangent):
    rows, _, frames, pixels = features.shape
    length = frames * pixels
    count = lax.axis_size("chan")
    channels = rows * count
    taps = kernel.shape[1]
    chunks = rows // 2 // SUB
    flops = 2 * rows * taps * channels * length
    sds = jax.ShapeDtypeStruct

    weights = jnp.transpose(kernel, (1, 0, 2)).reshape(taps * rows, channels)

    activation, pair = pl.pallas_call(
        activate_kernel,
        out_shape=(sds((rows, length), BF16), sds((2, rows, length), BF16)),
        in_specs=[whole()] * 2,
        out_specs=(whole(), whole()),
        compiler_params=params(),
        cost_estimate=cost(0, 10 * rows * length),
        name="activate",
    )(features, cotangent)

    blocks = [rotate(activation, "chan", d) for d in range(1, count)]
    other_pair = rotate(pair, "tm", 1)

    shares = pl.pallas_call(
        functools.partial(share_kernel, pixels),
        out_shape=(sds((rows, length), F32),) + (sds((rows, length), BF16),) * (count - 1),
        in_specs=[whole()] * 3,
        out_specs=(whole(),) * count,
        scratch_shapes=[
            pltpu.VMEM((9 * rows, (frames + 2) * pixels), BF16),
            pltpu.VMEM((channels, length), F32),
        ],
        compiler_params=params(),
        cost_estimate=cost(flops, 4 * taps * rows * channels),
        name="shares",
    )(weights, pair, other_pair)
    own_share, sends = shares[0], shares[1:]

    other_blocks = [rotate(b, "tm", 1) for b in blocks]
    act = pl.pallas_call(
        functools.partial(gather_kernel, pixels),
        out_shape=sds((channels, 2 * pixels + 2 * length), BF16),
        in_specs=[whole()] * (2 * count),
        out_specs=whole(),
        compiler_params=params(),
        cost_estimate=cost(0, 8 * channels * length),
        name="gathered",
    )(pair, other_pair, *blocks, *other_blocks)

    terms, got, other_terms, other_got = [], [], [], []
    for q in range(chunks):
        term = pl.pallas_call(
            functools.partial(grad_kernel, pixels, q),
            out_shape=sds((9 * SUB, 3 * channels), BF16),
            in_specs=[whole()] * 3,
            out_specs=whole(),
            scratch_shapes=[pltpu.VMEM((9 * SUB, 2 * length), BF16)],
            compiler_params=params(),
            cost_estimate=cost(flops // chunks, 4 * channels * length),
            name=f"grad_terms_{q}",
        )(pair, other_pair, act)
        terms.append(term)
        got.append(rotate(term, "dp", 1))

    received = [rotate(s, "chan", d) for d, s in enumerate(sends, 1)]

    conv_out = pl.pallas_call(
        functools.partial(conv_kernel, pixels),
        out_shape=sds(features.shape, BF16),
        in_specs=[whole()] * 2,
        out_specs=whole(),
        compiler_params=params(),
        cost_estimate=cost(flops, 2 * taps * rows * channels),
        name="conv",
    )(weights, act)

    feature_grad = pl.pallas_call(
        functools.partial(feature_kernel, pixels),
        out_shape=sds(features.shape, BF16),
        in_specs=[whole()] * (count + 1),
        out_specs=whole(),
        compiler_params=params(),
        cost_estimate=cost(0, 14 * rows * length),
        name="feature_grad",
    )(features, own_share, *received)

    scale = 1.0 / math.sqrt(lax.axis_size("dp") * lax.axis_size("tm") * length)
    kernel_grad = None
    for q in range(chunks):
        base = () if kernel_grad is None else (kernel_grad,)
        kernel_grad = pl.pallas_call(
            functools.partial(finish_kernel, scale, bool(base)),
            grid=(2,),
            out_shape=sds((rows, taps, channels), F32),
            in_specs=[pl.BlockSpec(memory_space=pl.ANY)] * len(base)
            + [pl.BlockSpec((9 * SUB, 3 * channels), lambda g: (0, 0))] * 4,
            out_specs=pl.BlockSpec(
                (SUB, taps, channels), functools.partial(lambda q, g: (g * chunks + q, 0, 0), q)
            ),
            input_output_aliases={0: 0} if base else {},
            compiler_params=params(),
            cost_estimate=cost(0, 4 * SUB * 2 * taps * channels * 2),
            name=f"kernel_grad_{q}",
        )(*base, terms[q], got[q], rotate(terms[q], "tm", 1), rotate(got[q], "tm", 1))
    return (conv_out, feature_grad, kernel_grad)


def local(features, kernel, cotangent):
    rows, clips, _, pixels = features.shape
    fits = (
        clips == 1
        and lax.axis_size("tm") == 2
        and lax.axis_size("dp") == 2
        and rows % (2 * SUB) == 0
        and pixels % 128 == 0
        and kernel.shape[1] == 27
    )
    return (local_fast if fits else local_generic)(features, kernel, cotangent)


def solution(mesh):
    return jax.shard_map(
        local,
        mesh=mesh,
        in_specs=(
            P("chan", ("groups", "dp"), "tm", None),
            P("chan", None, None),
            P("chan", ("groups", "dp"), "tm", None),
        ),
        out_specs=(
            P("chan", ("groups", "dp"), "tm", None),
            P("chan", ("groups", "dp"), "tm", None),
            P(("groups", "chan"), None, None),
        ),
        check_vma=False,
    )
```

```python
import functools
import math

import jax
import jax.numpy as jnp
from jax import lax
from jax.experimental import pallas as pl
from jax.experimental.pallas import tpu as pltpu
from jax.sharding import PartitionSpec as P

WID = 64
SUB = 16
F32 = jnp.float32
BF16 = jnp.bfloat16
VMEM_LIMIT = 24 * 1024 * 1024
TOKEN = (8, 128)


def from_behind(x, axis, by):
    size = lax.axis_size(axis)
    pairs = [(i, i + by) for i in range(size) if 0 <= i + by < size]
    return lax.ppermute(x, axis, pairs)


def padded_copies(block):
    pixels = block.shape[-1]
    column = lax.broadcasted_iota(jnp.int32, (pixels,), 0) % WID
    nothing = jnp.zeros((), block.dtype)
    widths = [(0, 0), (0, 0), (0, 0), (WID + 1, WID + 1)]
    left_cut = jnp.pad(jnp.where(column == WID - 1, nothing, block), widths)
    untouched = jnp.pad(block, widths)
    right_cut = jnp.pad(jnp.where(column == 0, nothing, block), widths)
    return (left_cut, untouched, right_cut)


def tap_window(copies, first_frame, vertical, horizontal, frames, pixels):
    source = copies[horizontal]
    offset = vertical * WID + horizontal
    return source[:, :, first_frame : first_frame + frames, offset : offset + pixels]


def stacked_taps(copies, first_frame, flipped, frames, pixels):
    pieces = []
    for vertical in range(3):
        for horizontal in range(3):
            if flipped:
                pieces.append(
                    tap_window(copies, first_frame, 2 - vertical, 2 - horizontal, frames, pixels)
                )
            else:
                pieces.append(tap_window(copies, first_frame, vertical, horizontal, frames, pixels))
    concatenated = jnp.concatenate(pieces, axis=0)
    return concatenated.reshape(concatenated.shape[0], -1)


def local_generic(features, kernel, cotangent):
    channels, clip_count, frames, pixels = features.shape
    flat_length = clip_count * frames * pixels
    widened = features.astype(F32)
    logistic = jax.nn.sigmoid(widened)
    activation = (widened * logistic).astype(BF16)
    slope_factor = logistic * (1.0 + widened * (1.0 - logistic))
    earlier = from_behind(activation[:, :, frames - 2 :, :], "tm", 1)
    extended = jnp.concatenate([earlier, activation], axis=2)
    upcoming = from_behind(cotangent[:, :, :2, :], "tm", -1)
    later_padded = jnp.concatenate([cotangent, upcoming], axis=2)
    cotangent_rows = cotangent.reshape(channels, -1)
    portion = lax.all_gather(extended, "chan", axis=0, tiled=True)
    out_sum = jnp.zeros((channels, flat_length), F32)
    amount = portion.shape[0]
    copies = padded_copies(portion)
    grad_parts = []
    for temporal in range(3):
        stacked = stacked_taps(copies, temporal, False, frames, pixels)
        weights = kernel[:, 9 * temporal : 9 * temporal + 9, :].reshape(channels, 9 * amount)
        out_sum = out_sum + jnp.dot(weights, stacked, preferred_element_type=F32)
        grad_parts.append(
            lax.dot_general(
                cotangent_rows, stacked, (((1,), (1,)), ((), ())), preferred_element_type=F32
            ).reshape(channels, 9, amount)
        )
    grad_sum = jnp.concatenate(grad_parts, axis=1)
    conv_out = out_sum.reshape(features.shape).astype(BF16)
    position_count = lax.axis_size("dp") * lax.axis_size("tm") * flat_length
    kernel_grad = lax.psum(grad_sum, ("tm", "dp")) * (1.0 / math.sqrt(position_count))
    padded_later = padded_copies(later_padded)
    summed = jnp.zeros((amount, flat_length), F32)
    for temporal in range(3):
        weights = jnp.transpose(
            kernel[:, 9 * temporal : 9 * temporal + 9, :], (2, 1, 0)
        ).reshape(amount, 9 * channels)
        stacked = stacked_taps(padded_later, 2 - temporal, True, frames, pixels)
        summed = summed + jnp.dot(weights, stacked, preferred_element_type=F32)
    before_slope = lax.psum_scatter(
        summed.reshape(amount, clip_count, frames, pixels), "chan", scatter_dimension=0, tiled=True
    )
    feature_grad = (before_slope * slope_factor).astype(BF16)
    return (conv_out, feature_grad, kernel_grad)


def rotate(x, axis, by):
    size = lax.axis_size(axis)
    return lax.ppermute(x, axis, [(i, (i + by) % size) for i in range(size)])


def shifted(frame, down, right):
    pixels = frame.shape[-1]
    if down == 0 and right == 0:
        return frame
    cell = lax.broadcasted_iota(jnp.int32, (1, pixels), 1)
    row, column = cell // WID + down, cell % WID + right
    inside = (row >= 0) & (row < pixels // WID) & (column >= 0) & (column < WID)
    moved = pltpu.roll(frame, (-(down * WID + right)) % pixels, 1)
    return jnp.where(inside, moved, 0.0)


def after(x, *others):
    anywhere = pl.BlockSpec(memory_space=pl.ANY)
    return pl.pallas_call(
        lambda *refs: None,
        out_shape=jax.ShapeDtypeStruct(x.shape, x.dtype),
        in_specs=[anywhere] * (1 + len(others)),
        out_specs=anywhere,
        input_output_aliases={0: 0},
        cost_estimate=cost(0, 0),
        name="hand_on",
    )(x, *others)


def run(kernel, args, waits=(), **options):
    options.setdefault("in_specs", [whole()] * len(args))
    options["in_specs"] = list(options["in_specs"]) + [
        pl.BlockSpec(memory_space=pl.ANY) for _ in waits
    ]
    count = len(args)

    def body(*refs):
        kernel(*refs[:count], *refs[count + len(waits) :])

    return pl.pallas_call(
        body, compiler_params=pltpu.CompilerParams(vmem_limit_bytes=VMEM_LIMIT), **options
    )(*args, *waits)


def cost(flops, bytes_accessed):
    return pl.CostEstimate(flops=1, bytes_accessed=1, transcendentals=0)


def whole():
    return pl.BlockSpec(memory_space=pltpu.VMEM)


def activate_kernel(features, activation):
    frames, pixels = features.shape[2:]
    v = features[:, 0].astype(F32)
    act = v / (1.0 + jnp.exp(-v))
    for t in range(frames):
        activation[:, t * pixels : (t + 1) * pixels] = act[:, t, :].astype(BF16)


def block_terms(pixels, stack, here, there, act, out, rhs):
    rows, length = here.shape
    me = lax.axis_index("tm")
    front = 2 * pixels
    act[:, :front] = jnp.zeros((rows, front), BF16)
    act[:, pl.ds(pl.multiple_of(front + me * length, pixels), length)] = here[...]
    act[:, pl.ds(pl.multiple_of(front + (1 - me) * length, pixels), length)] = there[...]
    for a in range(3):
        rhs[a * rows : (a + 1) * rows, :] = act[:, a * pixels : a * pixels + 2 * length]
    terms = lax.dot_general(
        stack[...], rhs[...], (((1,), (1,)), ((), ())), preferred_element_type=F32
    )
    main, tail = packed_rows(terms.shape[0])
    moved = [terms[main:, a * rows : (a + 1) * rows] for a in range(3)]
    if main > 3 * tail:
        moved.append(jnp.zeros((main - 3 * tail, rows), F32))
    out[...] = jnp.concatenate([terms[:main], jnp.concatenate(moved, axis=0)], axis=1).astype(BF16)


def packed_rows(total):
    unit = total // 9
    return 7 * unit, 2 * unit


def own_terms_kernel(pixels, mine, other, cot, cot_other, out, stack, act, later, rhs, flat):
    rows, _, frames, _ = cot.shape
    half = rows // 2
    me = lax.axis_index("tm")
    for at, source in ((me, cot), (1 - me, cot_other)):
        wide = source[:, 0].astype(F32)
        for t in range(frames):
            lanes = pl.ds(pl.multiple_of((at * frames + t) * pixels, pixels), pixels)
            flat[:, lanes] = wide[:, t, :]
    own = pl.ds(pl.multiple_of(me * frames * pixels, pixels), frames * pixels)
    later[:, : frames * pixels] = flat[:, own].astype(BF16)
    after_own = flat[:, frames * pixels : (frames + 2) * pixels]
    later[:, frames * pixels :] = jnp.where(me == 0, after_own, 0.0).astype(BF16)
    for t in range(2 * frames):
        at = pl.ds(pl.multiple_of(me * half, 8), half)
        frame = flat[at, t * pixels : (t + 1) * pixels]
        for i in range(3):
            for j in range(3):
                row = (3 * i + j) * half
                stack[row : row + half, t * pixels : (t + 1) * pixels] = shifted(
                    frame, 1 - i, 1 - j
                ).astype(BF16)
    block_terms(pixels, stack, mine, other, act, out, rhs)


def terms_kernel(pixels, stack, here, there, out, act, rhs):
    block_terms(pixels, stack, here, there, act, out, rhs)


def share_kernel(pixels, distances, weights, later, *rest):
    outs, (stack, total) = rest[:-2], rest[-2:]
    rows = later.shape[0]
    frames = later.shape[1] // pixels - 2
    z = lax.axis_index("chan")
    count = weights.shape[1] // rows
    for t in range(frames + 2):
        frame = later[:, t * pixels : (t + 1) * pixels].astype(F32)
        for i in range(3):
            for j in range(3):
                at = (3 * i + j) * rows
                stack[at : at + rows, t * pixels : (t + 1) * pixels] = shifted(
                    frame, 1 - i, 1 - j
                ).astype(BF16)
    taps = 9 * rows
    for t in range(frames):
        acc = None
        for a in range(3):
            term = lax.dot_general(
                weights[a * taps : (a + 1) * taps, :],
                stack[:, (t + 2 - a) * pixels : (t + 3 - a) * pixels],
                (((0,), (0,)), ((), ())),
                preferred_element_type=F32,
            )
            acc = term if acc is None else acc + term
        total[:, t * pixels : (t + 1) * pixels] = acc
    for d, out in zip(distances, outs):
        to = lax.rem(z + (d + count), count)
        out[...] = total[pl.ds(pl.multiple_of(to * rows, SUB), rows), :].astype(out.dtype)


def add_kernel(left, right, out):
    out[...] = (left[...] + right[...].astype(F32)).astype(out.dtype)


def conv_kernel(pixels, weights, *refs):
    blocks, (out, token, act) = refs[:-3], refs[-3:]
    token[...] = jnp.zeros(TOKEN, F32)
    rows, _, frames, _ = out.shape
    count = len(blocks)
    me, z = lax.axis_index("tm"), lax.axis_index("chan")
    window = pl.ds(pl.multiple_of(me * frames * pixels, pixels), (frames + 2) * pixels)
    for d, block in enumerate(blocks):
        at = lax.rem(z + count - d, count) * rows
        act[pl.ds(pl.multiple_of(at, SUB), rows), :] = block[:, window]
    taps = 9 * rows
    for t in range(frames):
        z_t = None
        for a in range(3):
            term = jnp.dot(
                weights[a * taps : (a + 1) * taps, :],
                act[:, (t + a) * pixels : (t + a + 1) * pixels],
                preferred_element_type=F32,
            )
            z_t = term if z_t is None else z_t + term
        acc = None
        for i in range(3):
            for j in range(3):
                at = (3 * i + j) * rows
                moved = shifted(z_t[at : at + rows, :], i - 1, j - 1)
                acc = moved if acc is None else acc + moved
        out[:, 0, t, :] = acc.astype(BF16)


def feature_kernel(pixels, features, own, *rest):
    (out, token), received = rest[-2:], rest[:-2]
    token[...] = jnp.zeros(TOKEN, F32)
    frames = features.shape[2]
    total = own[...]
    for part in received:
        total = total + part[...].astype(F32)
    v = features[:, 0].astype(F32)
    s = 1.0 / (1.0 + jnp.exp(-v))
    slope = s * (1.0 + v * (1.0 - s))
    for t in range(frames):
        piece = total[:, t * pixels : (t + 1) * pixels] * slope[:, t, :]
        out[:, 0, t, :] = piece.astype(BF16)


def sum_kernel(main, count, *refs):
    out, ins = refs[-1], refs[:-1]
    for d in range(len(ins) - count):
        at = slice(d * main, (d + 1) * main)
        if d < count:
            out[at, :] = ins[d][...].astype(F32) + ins[count + d][...].astype(F32)
        else:
            out[at, :] = ins[count + d][...].astype(F32)


def term_place(rows, step, u, a):
    half = rows // 2
    tap, kept = step * 3 + u, 7
    if tap < kept:
        return tap * half, a * rows
    return (a * (9 - kept) + tap - kept) * half, 3 * rows


def lay_kernel(scale, main, early, late, other_early, other_late, out):
    rows, channels = out.shape[2:]
    count, half = channels // rows, rows // 2
    me, z = lax.axis_index("tm"), lax.axis_index("chan")

    def write(at_z, first, second, start):
        for step in range(3):
            for u in range(3):
                for a in range(3):
                    base, lane = term_place(rows, step, u, a)
                    pieces = []
                    for s in range(count):
                        d = (at_z - s) % count
                        if d == count - 1:
                            pieces.append(jnp.zeros((half, rows), F32))
                            continue
                        source = second if d == count - 2 else first
                        at = base + (0 if d == count - 2 else d * main)
                        pieces.append(source[at : at + half, lane : lane + rows] * scale)
                    total = jnp.concatenate(pieces, axis=1)
                    out[a, step * 3 + u, pl.ds(pl.multiple_of(start, 8), half), :] = total

    for at_z in range(count):

        @pl.when(z == at_z)
        def _(at_z=at_z):
            write(at_z, early, late, me * half)
            write(at_z, other_early, other_late, (1 - me) * half)


def finish_kernel(scale, main, laid, term, got, other_term, other_got, out):
    rows, channels = out.shape[2:]
    count, half = channels // rows, rows // 2
    me, z, now = lax.axis_index("tm"), lax.axis_index("chan"), pl.program_id(0)

    def write(at_z, step, left, right, start):
        before = ((at_z + 1) % count) * rows
        at = pl.ds(pl.multiple_of(start, 8), half)
        for u in range(3):
            for a in range(3):
                base, lane = term_place(rows, step, u, a)
                source = (slice(base, base + half), slice(lane, lane + rows))
                piece = (left[source].astype(F32) + right[source].astype(F32)) * scale
                around = laid[a, u, at, :]
                pieces = [around[:, :before], piece, around[:, before + rows :]]
                pieces = [p for p in pieces if p.shape[1]]
                out[a, u, at, :] = jnp.concatenate(pieces, axis=1)

    for at_z in range(count):
        for step in range(3):

            @pl.when((z == at_z) & (now == step))
            def _(at_z=at_z, step=step):
                write(at_z, step, term, got, me * half)
                write(at_z, step, other_term, other_got, (1 - me) * half)


def local_fast(features, kernel, cotangent):
    rows, _, frames, pixels = features.shape
    length = frames * pixels
    count = lax.axis_size("chan")
    channels = rows * count
    taps = kernel.shape[1]
    half = rows // 2
    flops = 2 * rows * taps * channels * length
    sds = jax.ShapeDtypeStruct

    weights = jnp.transpose(kernel, (1, 0, 2)).reshape(taps * rows, channels)
    cot_other = rotate(cotangent, "tm", 1)
    activation = run(
        activate_kernel,
        (features,),
        out_shape=sds((rows, length), BF16),
        out_specs=whole(),
        cost_estimate=cost(0, 10 * rows * length),
        name="activate",
    )
    block = rotate(activation, "chan", 1)
    up = count // 2
    down = count - 1 - up

    main, _ = packed_rows(9 * half)
    term_shape = sds((main, channels), BF16)
    act_shape = sds((rows, 2 * pixels + 2 * length), BF16)
    stack_shape = sds((9 * half, 2 * length), BF16)
    later_shape = sds((rows, length + 2 * pixels), BF16)
    rhs = pltpu.VMEM((3 * rows, 2 * length), BF16)
    term_cost = cost(flops // count, 4 * rows * 9 * length)
    own_term, stack, own_act, later = run(
        functools.partial(own_terms_kernel, pixels),
        (activation, rotate(activation, "tm", 1), cotangent, cot_other),
        out_shape=(term_shape, stack_shape, act_shape, later_shape),
        out_specs=(whole(),) * 4,
        scratch_shapes=[rhs, pltpu.VMEM((rows, 2 * length), F32)],
        cost_estimate=term_cost,
        name="own_terms",
    )
    terms, acts, got = [own_term], [own_act], [rotate(own_term, "dp", 1)]

    distances = (0,) + tuple(range(1, up + 1)) + tuple(-d for d in range(1, down + 1))
    carried = (up, -down)

    def shares_after(last):
        parts = run(
            functools.partial(share_kernel, pixels, distances),
            (weights, later),
            waits=(last,),
            out_shape=tuple(
                sds((rows, length), BF16 if d in carried else F32) for d in distances
            ),
            out_specs=(whole(),) * count,
            scratch_shapes=[
                pltpu.VMEM((9 * rows, (frames + 2) * pixels), BF16),
                pltpu.VMEM((channels, length), F32),
            ],
            cost_estimate=cost(flops, 4 * taps * rows * channels),
            name="shares",
        )
        return dict(zip(distances, parts))

    def carry_on(carry, sign, d, waits):
        return run(
            add_kernel,
            (shares[sign * d], carry),
            waits=waits,
            out_shape=sds((rows, length), BF16),
            out_specs=whole(),
            cost_estimate=cost(0, 8 * rows * length),
            name="carry_share",
        )

    last = own_term
    shares = None
    for d in range(1, count):
        here = after(block, last, *got[d - 2 : d - 1])
        if d < count - 1:
            block = rotate(here, "chan", 1)
        term, act = run(
            functools.partial(terms_kernel, pixels),
            (stack, here, rotate(here, "tm", 1)),
            out_shape=(term_shape, act_shape),
            out_specs=(whole(),) * 2,
            scratch_shapes=[rhs],
            cost_estimate=term_cost,
            name=f"terms_{d}",
        )
        terms.append(term)
        acts.append(act)
        got.append(rotate(term, "dp", 1))
        last = term
        if d == 1:
            shares = shares_after(last)
            last = shares[0]
            carries = {s: rotate(shares[s * r], "chan", s) for s, r in ((1, up), (-1, down))}
            steps = [(1, d) for d in range(up - 1, 0, -1)]
            steps += [(-1, d) for d in range(down - 1, 0, -1)]
        elif steps:
            sign, distance = steps.pop(0)
            last = carry_on(carries[sign], sign, distance, (last,))
            carries[sign] = rotate(last, "chan", sign)

    def sums(first, stop, waits, alone=()):
        return run(
            functools.partial(sum_kernel, main, stop - first),
            (*terms[first:stop], *got[first:stop], *alone),
            waits=waits,
            out_shape=sds(((stop - first + len(alone)) * main, channels), F32),
            out_specs=whole(),
            cost_estimate=cost(0, 8 * main * channels * (stop - first)),
            name="sums",
        )

    early = sums(0, count - 2, (last,), (terms[-1],))
    other_early = rotate(early, "tm", 1)
    conv_out, token = run(
        functools.partial(conv_kernel, pixels),
        (weights, *acts),
        waits=(early,),
        out_shape=(sds(features.shape, BF16), sds(TOKEN, F32)),
        out_specs=(whole(),) * 2,
        scratch_shapes=[pltpu.VMEM((channels, (frames + 2) * pixels), BF16)],
        cost_estimate=cost(flops, 2 * taps * rows * channels),
        name="conv",
    )
    late = sums(count - 2, count - 1, (token,))
    other_late = rotate(late, "tm", 1)
    feature_grad, token = run(
        functools.partial(feature_kernel, pixels),
        (features, shares[0], *carries.values()),
        waits=(late,),
        out_shape=(sds(features.shape, BF16), sds(TOKEN, F32)),
        out_specs=(whole(),) * 2,
        cost_estimate=cost(0, 14 * rows * length),
        name="feature_grad",
    )

    scale = 1.0 / math.sqrt(lax.axis_size("dp") * lax.axis_size("tm") * length)
    grad_shape = sds((3, 9, rows, channels), F32)
    laid = run(
        functools.partial(lay_kernel, scale, main),
        (early, late, other_early, other_late),
        waits=(token,),
        out_shape=grad_shape,
        out_specs=whole(),
        cost_estimate=cost(0, 8 * taps * rows * channels),
        name="laid",
    )
    grad_block = pl.BlockSpec((3, 3, rows, channels), lambda g: (0, g, 0, 0))
    kernel_grad = run(
        functools.partial(finish_kernel, scale, main),
        (laid, early, got[-1], other_early, rotate(got[-1], "tm", 1)),
        grid=(3,),
        out_shape=grad_shape,
        in_specs=[
            grad_block,
            pl.BlockSpec((main, channels), lambda g: (count - 2, 0)),
            pl.BlockSpec((main, channels), lambda g: (0, 0)),
            pl.BlockSpec((main, channels), lambda g: (count - 2, 0)),
            pl.BlockSpec((main, channels), lambda g: (0, 0)),
        ],
        out_specs=grad_block,
        cost_estimate=cost(0, 8 * taps * rows * channels),
        name="kernel_grad",
    )
    kernel_grad = jnp.transpose(kernel_grad.reshape(taps, rows, channels), (1, 0, 2))
    return (conv_out, feature_grad, kernel_grad)


def local(features, kernel, cotangent):
    rows, clips, _, pixels = features.shape
    fits = (
        clips == 1
        and lax.axis_size("tm") == 2
        and lax.axis_size("dp") == 2
        and rows % (2 * SUB) == 0
        and pixels % 128 == 0
        and kernel.shape[1] == 27
        and lax.axis_size("chan") == 4
    )
    return (local_fast if fits else local_generic)(features, kernel, cotangent)


def solution(mesh):
    return jax.shard_map(
        local,
        mesh=mesh,
        in_specs=(
            P("chan", ("groups", "dp"), "tm", None),
            P("chan", None, None),
            P("chan", ("groups", "dp"), "tm", None),
        ),
        out_specs=(
            P("chan", ("groups", "dp"), "tm", None),
            P("chan", ("groups", "dp"), "tm", None),
            P(("groups", "chan"), None, None),
        ),
        check_vma=False,
    )
```

```python
import functools
import math

import jax
import jax.numpy as jnp
from jax import lax
from jax.experimental import pallas as pl
from jax.experimental.pallas import tpu as pltpu
from jax.sharding import PartitionSpec as P

WID = 64
SUB = 16
F32 = jnp.float32
BF16 = jnp.bfloat16
VMEM_LIMIT = 24 * 1024 * 1024
TOKEN = (8, 128)
FEATURE_COST = 1024 * 1024


def from_behind(x, axis, by):
    size = lax.axis_size(axis)
    pairs = [(i, i + by) for i in range(size) if 0 <= i + by < size]
    return lax.ppermute(x, axis, pairs)


def padded_copies(block):
    pixels = block.shape[-1]
    column = lax.broadcasted_iota(jnp.int32, (pixels,), 0) % WID
    nothing = jnp.zeros((), block.dtype)
    widths = [(0, 0), (0, 0), (0, 0), (WID + 1, WID + 1)]
    left_cut = jnp.pad(jnp.where(column == WID - 1, nothing, block), widths)
    untouched = jnp.pad(block, widths)
    right_cut = jnp.pad(jnp.where(column == 0, nothing, block), widths)
    return (left_cut, untouched, right_cut)


def tap_window(copies, first_frame, vertical, horizontal, frames, pixels):
    source = copies[horizontal]
    offset = vertical * WID + horizontal
    return source[:, :, first_frame : first_frame + frames, offset : offset + pixels]


def stacked_taps(copies, first_frame, flipped, frames, pixels):
    pieces = []
    for vertical in range(3):
        for horizontal in range(3):
            if flipped:
                pieces.append(
                    tap_window(copies, first_frame, 2 - vertical, 2 - horizontal, frames, pixels)
                )
            else:
                pieces.append(tap_window(copies, first_frame, vertical, horizontal, frames, pixels))
    concatenated = jnp.concatenate(pieces, axis=0)
    return concatenated.reshape(concatenated.shape[0], -1)


def local_generic(features, kernel, cotangent):
    channels, clip_count, frames, pixels = features.shape
    flat_length = clip_count * frames * pixels
    widened = features.astype(F32)
    logistic = jax.nn.sigmoid(widened)
    activation = (widened * logistic).astype(BF16)
    slope_factor = logistic * (1.0 + widened * (1.0 - logistic))
    earlier = from_behind(activation[:, :, frames - 2 :, :], "tm", 1)
    extended = jnp.concatenate([earlier, activation], axis=2)
    upcoming = from_behind(cotangent[:, :, :2, :], "tm", -1)
    later_padded = jnp.concatenate([cotangent, upcoming], axis=2)
    cotangent_rows = cotangent.reshape(channels, -1)
    portion = lax.all_gather(extended, "chan", axis=0, tiled=True)
    out_sum = jnp.zeros((channels, flat_length), F32)
    amount = portion.shape[0]
    copies = padded_copies(portion)
    grad_parts = []
    for temporal in range(3):
        stacked = stacked_taps(copies, temporal, False, frames, pixels)
        weights = kernel[:, 9 * temporal : 9 * temporal + 9, :].reshape(channels, 9 * amount)
        out_sum = out_sum + jnp.dot(weights, stacked, preferred_element_type=F32)
        grad_parts.append(
            lax.dot_general(
                cotangent_rows, stacked, (((1,), (1,)), ((), ())), preferred_element_type=F32
            ).reshape(channels, 9, amount)
        )
    grad_sum = jnp.concatenate(grad_parts, axis=1)
    conv_out = out_sum.reshape(features.shape).astype(BF16)
    position_count = lax.axis_size("dp") * lax.axis_size("tm") * flat_length
    kernel_grad = lax.psum(grad_sum, ("tm", "dp")) * (1.0 / math.sqrt(position_count))
    padded_later = padded_copies(later_padded)
    summed = jnp.zeros((amount, flat_length), F32)
    for temporal in range(3):
        weights = jnp.transpose(
            kernel[:, 9 * temporal : 9 * temporal + 9, :], (2, 1, 0)
        ).reshape(amount, 9 * channels)
        stacked = stacked_taps(padded_later, 2 - temporal, True, frames, pixels)
        summed = summed + jnp.dot(weights, stacked, preferred_element_type=F32)
    before_slope = lax.psum_scatter(
        summed.reshape(amount, clip_count, frames, pixels), "chan", scatter_dimension=0, tiled=True
    )
    feature_grad = (before_slope * slope_factor).astype(BF16)
    return (conv_out, feature_grad, kernel_grad)


def rotate(x, axis, by):
    size = lax.axis_size(axis)
    return lax.ppermute(x, axis, [(i, (i + by) % size) for i in range(size)])


def shifted(frame, down, right):
    pixels = frame.shape[-1]
    if down == 0 and right == 0:
        return frame
    cell = lax.broadcasted_iota(jnp.int32, (1, pixels), 1)
    row, column = cell // WID + down, cell % WID + right
    inside = (row >= 0) & (row < pixels // WID) & (column >= 0) & (column < WID)
    moved = pltpu.roll(frame, (-(down * WID + right)) % pixels, 1)
    return jnp.where(inside, moved, 0.0)


def after(x, *others):
    anywhere = pl.BlockSpec(memory_space=pl.ANY)
    return pl.pallas_call(
        lambda *refs: None,
        out_shape=jax.ShapeDtypeStruct(x.shape, x.dtype),
        in_specs=[anywhere] * (1 + len(others)),
        out_specs=anywhere,
        input_output_aliases={0: 0},
        compiler_params=pltpu.CompilerParams(vmem_limit_bytes=1024 * 1024),
        cost_estimate=cost(0, 0),
        name="hand_on",
    )(x, *others)


def run(kernel, args, waits=(), **options):
    options.setdefault("in_specs", [whole()] * len(args))
    options["in_specs"] = list(options["in_specs"]) + [
        pl.BlockSpec(memory_space=pl.ANY) for _ in waits
    ]
    count = len(args)

    def body(*refs):
        kernel(*refs[:count], *refs[count + len(waits) :])

    return pl.pallas_call(
        body, compiler_params=pltpu.CompilerParams(vmem_limit_bytes=VMEM_LIMIT), **options
    )(*args, *waits)


def cost(flops, bytes_accessed, bytes_like=1):
    return pl.CostEstimate(flops=1, bytes_accessed=bytes_like, transcendentals=0)


def whole():
    return pl.BlockSpec(memory_space=pltpu.VMEM)


def activate_kernel(features, activation):
    frames, pixels = features.shape[2:]
    v = features[:, 0].astype(F32)
    act = v / (1.0 + jnp.exp(-v))
    for t in range(frames):
        activation[:, t * pixels : (t + 1) * pixels] = act[:, t, :].astype(BF16)


def in_slot(channels, rows, slot):
    lane = lax.broadcasted_iota(jnp.int32, (1, channels), 1)
    return (lane >= slot * rows) & (lane < (slot + 1) * rows)


def packed_rows(total):
    unit = total // 9
    return 7 * unit, 2 * unit


def block_terms(pixels, back, stack, here, there, act, out, rhs):
    rows, length = here.shape
    channels = out.shape[1]
    count = channels // rows
    me = lax.axis_index("tm")
    shard = lax.rem(lax.axis_index("chan") + count - back, count)
    front = 2 * pixels
    act[:, :front] = jnp.zeros((rows, front), BF16)
    act[:, pl.ds(pl.multiple_of(front + me * length, pixels), length)] = here[...]
    act[:, pl.ds(pl.multiple_of(front + (1 - me) * length, pixels), length)] = there[...]
    for a in range(3):
        at = pl.multiple_of(lax.rem(shard + a, count) * rows, SUB)
        rhs[pl.ds(at, rows), :] = act[:, a * pixels : a * pixels + 2 * length]
    last = lax.rem(shard + 3, count)
    rhs[pl.ds(pl.multiple_of(last * rows, SUB), rows), :] = jnp.zeros((rows, 2 * length), BF16)
    terms = lax.dot_general(
        stack[...], rhs[...], (((1,), (1,)), ((), ())), preferred_element_type=F32
    )
    main, tail = packed_rows(terms.shape[0])
    free = in_slot(channels, rows, last)
    for a in range(3):
        at = slice(a * tail, (a + 1) * tail)
        moved = pltpu.roll(terms[main:], (3 - a) * rows, 1)
        out[at, :] = jnp.where(free, moved, terms[at]).astype(BF16)
    out[3 * tail :, :] = terms[3 * tail : main].astype(BF16)


def own_terms_kernel(pixels, mine, other, cot, cot_other, out, stack, act, later, rhs, flat):
    rows, _, frames, _ = cot.shape
    half = rows // 2
    me = lax.axis_index("tm")
    for at, source in ((me, cot), (1 - me, cot_other)):
        wide = source[:, 0].astype(F32)
        for t in range(frames):
            lanes = pl.ds(pl.multiple_of((at * frames + t) * pixels, pixels), pixels)
            flat[:, lanes] = wide[:, t, :]
    own = pl.ds(pl.multiple_of(me * frames * pixels, pixels), frames * pixels)
    later[:, : frames * pixels] = flat[:, own].astype(BF16)
    after_own = flat[:, frames * pixels : (frames + 2) * pixels]
    later[:, frames * pixels :] = jnp.where(me == 0, after_own, 0.0).astype(BF16)
    for t in range(2 * frames):
        at = pl.ds(pl.multiple_of(me * half, 8), half)
        frame = flat[at, t * pixels : (t + 1) * pixels]
        for i in range(3):
            for j in range(3):
                row = (3 * i + j) * half
                stack[row : row + half, t * pixels : (t + 1) * pixels] = shifted(
                    frame, 1 - i, 1 - j
                ).astype(BF16)
    block_terms(pixels, 0, stack, mine, other, act, out, rhs)


def terms_kernel(pixels, back, stack, here, there, out, act, rhs):
    block_terms(pixels, back, stack, here, there, act, out, rhs)


def share_kernel(pixels, distances, weights, later, *rest):
    outs, (stack, total) = rest[:-2], rest[-2:]
    rows = later.shape[0]
    frames = later.shape[1] // pixels - 2
    z = lax.axis_index("chan")
    count = weights.shape[1] // rows
    for t in range(frames + 2):
        frame = later[:, t * pixels : (t + 1) * pixels].astype(F32)
        for i in range(3):
            for j in range(3):
                at = (3 * i + j) * rows
                stack[at : at + rows, t * pixels : (t + 1) * pixels] = shifted(
                    frame, 1 - i, 1 - j
                ).astype(BF16)
    taps = 9 * rows
    for t in range(frames):
        acc = None
        for a in range(3):
            term = lax.dot_general(
                weights[a * taps : (a + 1) * taps, :],
                stack[:, (t + 2 - a) * pixels : (t + 3 - a) * pixels],
                (((0,), (0,)), ((), ())),
                preferred_element_type=F32,
            )
            acc = term if acc is None else acc + term
        total[:, t * pixels : (t + 1) * pixels] = acc
    for d, out in zip(distances, outs):
        to = lax.rem(z + (d + count), count)
        out[...] = total[pl.ds(pl.multiple_of(to * rows, SUB), rows), :].astype(out.dtype)


def add_kernel(left, right, out):
    out[...] = (left[...] + right[...].astype(F32)).astype(out.dtype)


def conv_kernel(pixels, weights, *refs):
    blocks, (out, token, act) = refs[:-3], refs[-3:]
    token[...] = jnp.zeros(TOKEN, F32)
    rows, _, frames, _ = out.shape
    count = len(blocks)
    me, z = lax.axis_index("tm"), lax.axis_index("chan")
    window = pl.ds(pl.multiple_of(me * frames * pixels, pixels), (frames + 2) * pixels)
    for d, block in enumerate(blocks):
        at = lax.rem(z + count - d, count) * rows
        act[pl.ds(pl.multiple_of(at, SUB), rows), :] = block[:, window]
    taps = 9 * rows
    for t in range(frames):
        z_t = None
        for a in range(3):
            term = jnp.dot(
                weights[a * taps : (a + 1) * taps, :],
                act[:, (t + a) * pixels : (t + a + 1) * pixels],
                preferred_element_type=F32,
            )
            z_t = term if z_t is None else z_t + term
        acc = None
        for i in range(3):
            for j in range(3):
                at = (3 * i + j) * rows
                moved = shifted(z_t[at : at + rows, :], i - 1, j - 1)
                acc = moved if acc is None else acc + moved
        out[:, 0, t, :] = acc.astype(BF16)


def feature_kernel(pixels, features, own, *rest):
    (out, token), received = rest[-2:], rest[:-2]
    token[...] = jnp.zeros(TOKEN, F32)
    frames = features.shape[2]
    total = own[...]
    for part in received:
        total = total + part[...].astype(F32)
    v = features[:, 0].astype(F32)
    s = 1.0 / (1.0 + jnp.exp(-v))
    slope = s * (1.0 + v * (1.0 - s))
    for t in range(frames):
        piece = total[:, t * pixels : (t + 1) * pixels] * slope[:, t, :]
        out[:, 0, t, :] = piece.astype(BF16)


def sum_kernel(main, *refs):
    out, ins = refs[-1], refs[:-1]
    count = len(ins) // 2
    z = lax.axis_index("chan")
    for d in range(count):
        at = pl.multiple_of(lax.rem(z + count - d, count) * main, SUB)
        total = ins[d][...].astype(F32) + ins[count + d][...].astype(F32)
        out[pl.ds(at, main), :] = total.astype(BF16)


def finish_kernel(scale, main, sums, other_sums, out):
    _, _, rows, channels = out.shape
    count, half = channels // rows, rows // 2
    me, now = lax.axis_index("tm"), pl.program_id(0)

    def write(moved, source, start):
        for a in range(3):
            base = a * 2 * half + (now - 7) * half if moved else now * half
            step = 3 if moved else a
            total = None
            for s in range(count):
                at = pl.ds(pl.multiple_of(s * main + base, SUB), half)
                piece = source[at, :].astype(F32)
                mask = in_slot(channels, rows, (s + step) % count)
                total = piece if total is None else jnp.where(mask, piece, total)
            total = total * scale
            if step:
                total = pltpu.roll(total, channels - step * rows, 1)
            out[a, 0, pl.ds(pl.multiple_of(start, 8), half), :] = total

    for moved in (False, True):

        @pl.when((now >= 7) == moved)
        def _(moved=moved):
            write(moved, sums, me * half)
            write(moved, other_sums, (1 - me) * half)


def local_fast(features, kernel, cotangent):
    rows, _, frames, pixels = features.shape
    length = frames * pixels
    count = lax.axis_size("chan")
    channels = rows * count
    taps = kernel.shape[1]
    half = rows // 2
    flops = 2 * rows * taps * channels * length
    sds = jax.ShapeDtypeStruct

    weights = jnp.transpose(kernel, (1, 0, 2)).reshape(taps * rows, channels)
    cot_other = rotate(cotangent, "tm", 1)
    activation = run(
        activate_kernel,
        (features,),
        out_shape=sds((rows, length), BF16),
        out_specs=whole(),
        cost_estimate=cost(0, 10 * rows * length),
        name="activate",
    )
    block = rotate(activation, "chan", 1)
    up = count // 2
    down = count - 1 - up

    main, _ = packed_rows(9 * half)
    term_shape = sds((main, channels), BF16)
    act_shape = sds((rows, 2 * pixels + 2 * length), BF16)
    stack_shape = sds((9 * half, 2 * length), BF16)
    later_shape = sds((rows, length + 2 * pixels), BF16)
    rhs = pltpu.VMEM((channels, 2 * length), BF16)
    term_cost = cost(flops // count, 4 * rows * 9 * length)
    own_term, stack, own_act, later = run(
        functools.partial(own_terms_kernel, pixels),
        (activation, rotate(activation, "tm", 1), cotangent, cot_other),
        out_shape=(term_shape, stack_shape, act_shape, later_shape),
        out_specs=(whole(),) * 4,
        scratch_shapes=[rhs, pltpu.VMEM((rows, 2 * length), F32)],
        cost_estimate=term_cost,
        name="own_terms",
    )
    terms, acts, got = [own_term], [own_act], [rotate(own_term, "dp", 1)]

    distances = (0,) + tuple(range(1, up + 1)) + tuple(-d for d in range(1, down + 1))
    carried = (up, -down)

    def shares_after(last):
        parts = run(
            functools.partial(share_kernel, pixels, distances),
            (weights, later),
            waits=(last,),
            out_shape=tuple(
                sds((rows, length), BF16 if d in carried else F32) for d in distances
            ),
            out_specs=(whole(),) * count,
            scratch_shapes=[
                pltpu.VMEM((9 * rows, (frames + 2) * pixels), BF16),
                pltpu.VMEM((channels, length), F32),
            ],
            cost_estimate=cost(flops, 4 * taps * rows * channels),
            name="shares",
        )
        return dict(zip(distances, parts))

    def carry_on(carry, sign, d, waits):
        return run(
            add_kernel,
            (shares[sign * d], carry),
            waits=waits,
            out_shape=sds((rows, length), BF16),
            out_specs=whole(),
            cost_estimate=cost(0, 8 * rows * length),
            name="carry_share",
        )

    last = own_term
    shares = None
    for d in range(1, count):
        here = after(block, last, *got[d - 2 : d - 1])
        if d < count - 1:
            block = rotate(here, "chan", 1)
        term, act = run(
            functools.partial(terms_kernel, pixels, d),
            (stack, here, rotate(here, "tm", 1)),
            out_shape=(term_shape, act_shape),
            out_specs=(whole(),) * 2,
            scratch_shapes=[rhs],
            cost_estimate=term_cost,
            name=f"terms_{d}",
        )
        terms.append(term)
        acts.append(act)
        got.append(rotate(term, "dp", 1))
        last = term
        if d == 1:
            shares = shares_after(last)
            last = shares[0]
            carries = {s: rotate(shares[s * r], "chan", s) for s, r in ((1, up), (-1, down))}
            steps = [(1, d) for d in range(up - 1, 0, -1)]
            steps += [(-1, d) for d in range(down - 1, 0, -1)]
        elif steps:
            sign, distance = steps.pop(0)
            last = carry_on(carries[sign], sign, distance, (last,))
            carries[sign] = rotate(last, "chan", sign)

    conv_out, token = run(
        functools.partial(conv_kernel, pixels),
        (weights, *acts),
        waits=(last,),
        out_shape=(sds(features.shape, BF16), sds(TOKEN, F32)),
        out_specs=(whole(),) * 2,
        scratch_shapes=[pltpu.VMEM((channels, (frames + 2) * pixels), BF16)],
        cost_estimate=cost(0, 0),
        name="conv",
    )
    feature_grad, token = run(
        functools.partial(feature_kernel, pixels),
        (features, shares[0], *carries.values()),
        waits=(token, got[-2]),
        out_shape=(sds(features.shape, BF16), sds(TOKEN, F32)),
        out_specs=(whole(),) * 2,
        cost_estimate=cost(0, 0, FEATURE_COST),
        name="feature_grad",
    )
    sums = run(
        functools.partial(sum_kernel, main),
        (*terms, *got),
        waits=(token,),
        out_shape=sds((count * main, channels), BF16),
        out_specs=whole(),
        cost_estimate=cost(0, 0),
        name="sums",
    )

    scale = 1.0 / math.sqrt(lax.axis_size("dp") * lax.axis_size("tm") * length)
    packed = pl.BlockSpec((count * main, channels), lambda g: (0, 0))
    kernel_grad = run(
        functools.partial(finish_kernel, scale, main),
        (sums, rotate(sums, "tm", 1)),
        grid=(9,),
        out_shape=sds((3, 9, rows, channels), F32),
        in_specs=[packed] * 2,
        out_specs=pl.BlockSpec((3, 1, rows, channels), lambda g: (0, g, 0, 0)),
        cost_estimate=cost(0, 0),
        name="kernel_grad",
    )
    kernel_grad = jnp.transpose(kernel_grad.reshape(taps, rows, channels), (1, 0, 2))
    return (conv_out, feature_grad, kernel_grad)


def local(features, kernel, cotangent):
    rows, clips, _, pixels = features.shape
    fits = (
        clips == 1
        and lax.axis_size("tm") == 2
        and lax.axis_size("dp") == 2
        and rows % (2 * SUB) == 0
        and pixels % 128 == 0
        and kernel.shape[1] == 27
        and lax.axis_size("chan") == 4
    )
    return (local_fast if fits else local_generic)(features, kernel, cotangent)


def solution(mesh):
    return jax.shard_map(
        local,
        mesh=mesh,
        in_specs=(
            P("chan", ("groups", "dp"), "tm", None),
            P("chan", None, None),
            P("chan", ("groups", "dp"), "tm", None),
        ),
        out_specs=(
            P("chan", ("groups", "dp"), "tm", None),
            P("chan", ("groups", "dp"), "tm", None),
            P(("groups", "chan"), None, None),
        ),
        check_vma=False,
    )
```

```python
import functools
import math

import jax
import jax.numpy as jnp
from jax import lax
from jax.experimental import pallas as pl
from jax.experimental.pallas import tpu as pltpu
from jax.sharding import PartitionSpec as P

WID = 64
SUB = 16
F32 = jnp.float32
BF16 = jnp.bfloat16
VMEM_LIMIT = 24 * 1024 * 1024
TOKEN = (8, 128)
FEATURE_COST = 1024 * 1024


def from_behind(x, axis, by):
    size = lax.axis_size(axis)
    pairs = [(i, i + by) for i in range(size) if 0 <= i + by < size]
    return lax.ppermute(x, axis, pairs)


def padded_copies(block):
    pixels = block.shape[-1]
    column = lax.broadcasted_iota(jnp.int32, (pixels,), 0) % WID
    nothing = jnp.zeros((), block.dtype)
    widths = [(0, 0), (0, 0), (0, 0), (WID + 1, WID + 1)]
    left_cut = jnp.pad(jnp.where(column == WID - 1, nothing, block), widths)
    untouched = jnp.pad(block, widths)
    right_cut = jnp.pad(jnp.where(column == 0, nothing, block), widths)
    return (left_cut, untouched, right_cut)


def tap_window(copies, first_frame, vertical, horizontal, frames, pixels):
    source = copies[horizontal]
    offset = vertical * WID + horizontal
    return source[:, :, first_frame : first_frame + frames, offset : offset + pixels]


def stacked_taps(copies, first_frame, flipped, frames, pixels):
    pieces = []
    for vertical in range(3):
        for horizontal in range(3):
            if flipped:
                pieces.append(
                    tap_window(copies, first_frame, 2 - vertical, 2 - horizontal, frames, pixels)
                )
            else:
                pieces.append(tap_window(copies, first_frame, vertical, horizontal, frames, pixels))
    concatenated = jnp.concatenate(pieces, axis=0)
    return concatenated.reshape(concatenated.shape[0], -1)


def local_generic(features, kernel, cotangent):
    channels, clip_count, frames, pixels = features.shape
    flat_length = clip_count * frames * pixels
    widened = features.astype(F32)
    logistic = jax.nn.sigmoid(widened)
    activation = (widened * logistic).astype(BF16)
    slope_factor = logistic * (1.0 + widened * (1.0 - logistic))
    earlier = from_behind(activation[:, :, frames - 2 :, :], "tm", 1)
    extended = jnp.concatenate([earlier, activation], axis=2)
    upcoming = from_behind(cotangent[:, :, :2, :], "tm", -1)
    later_padded = jnp.concatenate([cotangent, upcoming], axis=2)
    cotangent_rows = cotangent.reshape(channels, -1)
    portion = lax.all_gather(extended, "chan", axis=0, tiled=True)
    out_sum = jnp.zeros((channels, flat_length), F32)
    amount = portion.shape[0]
    copies = padded_copies(portion)
    grad_parts = []
    for temporal in range(3):
        stacked = stacked_taps(copies, temporal, False, frames, pixels)
        weights = kernel[:, 9 * temporal : 9 * temporal + 9, :].reshape(channels, 9 * amount)
        out_sum = out_sum + jnp.dot(weights, stacked, preferred_element_type=F32)
        grad_parts.append(
            lax.dot_general(
                cotangent_rows, stacked, (((1,), (1,)), ((), ())), preferred_element_type=F32
            ).reshape(channels, 9, amount)
        )
    grad_sum = jnp.concatenate(grad_parts, axis=1)
    conv_out = out_sum.reshape(features.shape).astype(BF16)
    position_count = lax.axis_size("dp") * lax.axis_size("tm") * flat_length
    kernel_grad = lax.psum(grad_sum, ("tm", "dp")) * (1.0 / math.sqrt(position_count))
    padded_later = padded_copies(later_padded)
    summed = jnp.zeros((amount, flat_length), F32)
    for temporal in range(3):
        weights = jnp.transpose(
            kernel[:, 9 * temporal : 9 * temporal + 9, :], (2, 1, 0)
        ).reshape(amount, 9 * channels)
        stacked = stacked_taps(padded_later, 2 - temporal, True, frames, pixels)
        summed = summed + jnp.dot(weights, stacked, preferred_element_type=F32)
    before_slope = lax.psum_scatter(
        summed.reshape(amount, clip_count, frames, pixels), "chan", scatter_dimension=0, tiled=True
    )
    feature_grad = (before_slope * slope_factor).astype(BF16)
    return (conv_out, feature_grad, kernel_grad)


def rotate(x, axis, by):
    size = lax.axis_size(axis)
    return lax.ppermute(x, axis, [(i, (i + by) % size) for i in range(size)])


def shifted(frame, down, right):
    pixels = frame.shape[-1]
    if down == 0 and right == 0:
        return frame
    cell = lax.broadcasted_iota(jnp.int32, (1, pixels), 1)
    row, column = cell // WID + down, cell % WID + right
    inside = (row >= 0) & (row < pixels // WID) & (column >= 0) & (column < WID)
    moved = pltpu.roll(frame, (-(down * WID + right)) % pixels, 1)
    return jnp.where(inside, moved, 0.0)


def after(x, *others):
    anywhere = pl.BlockSpec(memory_space=pl.ANY)
    return pl.pallas_call(
        lambda *refs: None,
        out_shape=jax.ShapeDtypeStruct(x.shape, x.dtype),
        in_specs=[anywhere] * (1 + len(others)),
        out_specs=anywhere,
        input_output_aliases={0: 0},
        compiler_params=pltpu.CompilerParams(vmem_limit_bytes=1024 * 1024),
        cost_estimate=cost(),
        name="hand_on",
    )(x, *others)


def run(kernel, args, waits=(), **options):
    options.setdefault("in_specs", [whole()] * len(args))
    options.setdefault("cost_estimate", cost())
    options["in_specs"] = list(options["in_specs"]) + [
        pl.BlockSpec(memory_space=pl.ANY) for _ in waits
    ]
    count = len(args)

    def body(*refs):
        kernel(*refs[:count], *refs[count + len(waits) :])

    return pl.pallas_call(
        body, compiler_params=pltpu.CompilerParams(vmem_limit_bytes=VMEM_LIMIT), **options
    )(*args, *waits)


def cost(bytes_like=1):
    return pl.CostEstimate(flops=1, bytes_accessed=bytes_like, transcendentals=0)


def whole():
    return pl.BlockSpec(memory_space=pltpu.VMEM)


def activate_kernel(features, features_other, full):
    _, _, frames, pixels = features.shape
    me = lax.axis_index("tm")
    for core, source in ((me, features), (1 - me, features_other)):
        v = source[:, 0].astype(F32)
        act = v / (1.0 + jnp.exp(-v))
        for t in range(frames):
            at = pl.multiple_of((core * frames + t) * pixels, pixels)
            full[:, pl.ds(at, pixels)] = act[:, t, :].astype(BF16)


def in_slot(channels, rows, slot):
    lane = lax.broadcasted_iota(jnp.int32, (1, channels), 1)
    return (lane >= slot * rows) & (lane < (slot + 1) * rows)


def packed_rows(total):
    unit = total // 9
    return 7 * unit, 2 * unit


def fill_stack(pixels, flat, stack, which):
    total, lanes = stack.shape
    rows = flat.shape[0]
    unit = rows // 2
    frames = flat.shape[1] // pixels
    stack[:, frames * pixels :] = jnp.zeros((total, lanes - frames * pixels), BF16)
    for half in range(2):

        @pl.when(which == half)
        def _(half=half):
            for t in range(frames):
                at = slice(t * pixels, (t + 1) * pixels)
                for q in range(9):
                    tap, part = divmod(9 * half + q, 2)
                    i, j = divmod(tap, 3)
                    frame = flat[part * unit : (part + 1) * unit, at]
                    stack[q * unit : (q + 1) * unit, at] = shifted(frame, 1 - i, 1 - j).astype(BF16)


def block_terms(pixels, shard, stack, sources, out, rhs):
    channels = out.shape[1]
    rows, lanes = sources[0][1].shape
    count = channels // rows
    for flag, source in sources:

        @pl.when(flag)
        def _(source=source):
            for a in range(3):
                skip = (2 - a) * pixels
                at = pl.ds(pl.multiple_of(lax.rem(shard + a, count) * rows, SUB), rows)
                if skip:
                    rhs[at, :skip] = jnp.zeros((rows, skip), BF16)
                rhs[at, skip:] = source[:, : lanes - skip]

    last = lax.rem(shard + 3, count)
    rhs[pl.ds(pl.multiple_of(last * rows, SUB), rows), :] = jnp.zeros((rows, lanes), BF16)
    terms = lax.dot_general(
        stack[:, :lanes], rhs[...], (((1,), (1,)), ((), ())), preferred_element_type=F32
    )
    main, tail = packed_rows(terms.shape[0])
    free = in_slot(channels, rows, last)
    for a in range(3):
        at = slice(a * tail, (a + 1) * tail)
        moved = pltpu.roll(terms[main:], (3 - a) * rows, 1)
        out[at, :] = jnp.where(free, moved, terms[at]).astype(BF16)
    out[3 * tail :, :] = terms[3 * tail : main].astype(BF16)


def own_terms_kernel(pixels, full, cot, cot_other, out, stack, flat, rhs):
    _, _, frames, _ = cot.shape
    me = lax.axis_index("tm")
    for core, source in ((me, cot), (1 - me, cot_other)):
        wide = source[:, 0].astype(F32)
        for t in range(frames):
            at = pl.multiple_of((core * frames + t) * pixels, pixels)
            flat[:, pl.ds(at, pixels)] = wide[:, t, :]
    fill_stack(pixels, flat, stack, me)
    block_terms(pixels, lax.axis_index("chan"), stack, [(me >= 0, full)], out, rhs)


def arrivals(count, z):
    both = [(hops, below) for hops in range(1, count) for below in (True, False)]
    return [(h, below) for h, below in both if 0 <= (z - h if below else z + h) < count]


def terms_kernel(pixels, count, k, hops, stack, *refs):
    blocks, (out, rhs) = refs[:-2], refs[-2:]
    me, z = lax.axis_index("tm"), lax.axis_index("chan")
    shard = z
    flags = [z < 0] * len(blocks)
    for at_z in range(count):
        hop, below = arrivals(count, at_z)[k]
        shard = jnp.where(z == at_z, at_z - hop if below else at_z + hop, shard)
        n = 2 * hops.index(hop)
        carrier = me == (0 if below else 1)
        flags[n] = flags[n] | ((z == at_z) & carrier)
        flags[n + 1] = flags[n + 1] | ((z == at_z) & jnp.logical_not(carrier))
    block_terms(pixels, shard, stack, list(zip(flags, blocks)), out, rhs)


def write_share(pixels, target, start, weights, mine, other, out):
    half = mine.shape[0]
    rows, length = out.shape
    me = lax.axis_index("tm")
    for shard in range(weights.shape[1] // rows):

        @pl.when(target == shard)
        def _(shard=shard):
            total = None
            for a in range(3):
                lanes = pl.ds(pl.multiple_of(start + (2 - a) * pixels, pixels), length)
                for which, stack in ((me, mine), (1 - me, other)):
                    at = pl.multiple_of((2 * a + which) * half, SUB)
                    term = lax.dot_general(
                        weights[pl.ds(at, half), shard * rows : (shard + 1) * rows],
                        stack[:, lanes],
                        (((0,), (0,)), ((), ())),
                        preferred_element_type=F32,
                    )
                    total = term if total is None else total + term
            out[...] = total


def share_target(hops):
    return lax.axis_index("chan") + jnp.where(lax.axis_index("tm") == 0, hops, -hops)


def far_share_kernel(pixels, hops, weights, mine, flat, out, other):
    fill_stack(pixels, flat, other, 1 - lax.axis_index("tm"))
    write_share(pixels, share_target(hops), 0, weights, mine, other, out)


def share_kernel(pixels, hops, weights, mine, other, out):
    write_share(pixels, share_target(hops), 0, weights, mine, other, out)


def near_share_kernel(pixels, hops, weights, mine, other, out, own):
    write_share(pixels, share_target(hops), 0, weights, mine, other, out)
    start = lax.axis_index("tm") * own.shape[1]
    write_share(pixels, lax.axis_index("chan"), start, weights, mine, other, own)


def message_kernel(count, step, came, share, out):
    me, z = lax.axis_index("tm"), lax.axis_index("chan")
    behind = jnp.where(me == 0, z, count - 1 - z)

    @pl.when(behind <= step - 2)
    def _():
        out[...] = (came[...].astype(F32) + share[...]).astype(BF16)

    @pl.when(behind > step - 2)
    def _():
        out[...] = came[...]


def conv_kernel(pixels, weights, full, *refs):
    blocks, (out, token, act) = refs[:-3], refs[-3:]
    token[...] = jnp.zeros(TOKEN, F32)
    rows, _, frames, _ = out.shape
    count = weights.shape[1] // rows
    length, front = frames * pixels, 2 * pixels
    me, z = lax.axis_index("tm"), lax.axis_index("chan")

    def place(flag, shard, source):
        at = pl.ds(pl.multiple_of(shard * rows, SUB), rows)

        @pl.when(flag & (me == 0))
        def _():
            act[at, :front] = jnp.zeros((rows, front), BF16)
            act[at, front:] = source[:, :length]

        @pl.when(flag & (me == 1))
        def _():
            act[at, :] = source[:, length - front :]

    place(me >= 0, z, full)
    for n in range(count - 1):
        hops = n + 1
        for core, source in ((0, blocks[2 * n]), (1, blocks[2 * n + 1])):
            below = me == core
            place(below & (z - hops >= 0), z - hops, source)
            place(jnp.logical_not(below) & (z + hops < count), z + hops, source)

    taps = 9 * rows
    for t in range(frames):
        z_t = None
        for a in range(3):
            term = jnp.dot(
                weights[a * taps : (a + 1) * taps, :],
                act[:, (t + a) * pixels : (t + a + 1) * pixels],
                preferred_element_type=F32,
            )
            z_t = term if z_t is None else z_t + term
        acc = None
        for i in range(3):
            for j in range(3):
                at = (3 * i + j) * rows
                moved = shifted(z_t[at : at + rows, :], i - 1, j - 1)
                acc = moved if acc is None else acc + moved
        out[:, 0, t, :] = acc.astype(BF16)


def feature_kernel(pixels, features, own, came, came_other, out, token):
    token[...] = jnp.zeros(TOKEN, F32)
    frames = features.shape[2]
    length = frames * pixels
    mine = pl.ds(pl.multiple_of(lax.axis_index("tm") * length, pixels), length)
    total = own[...] + came[:, mine].astype(F32) + came_other[:, mine].astype(F32)
    v = features[:, 0].astype(F32)
    s = 1.0 / (1.0 + jnp.exp(-v))
    slope = s * (1.0 + v * (1.0 - s))
    for t in range(frames):
        piece = total[:, t * pixels : (t + 1) * pixels] * slope[:, t, :]
        out[:, 0, t, :] = piece.astype(BF16)


def shard_at(count, k):
    z = lax.axis_index("chan")
    if k == 0:
        return z
    shard = z
    for at_z in range(count):
        hop, below = arrivals(count, at_z)[k - 1]
        shard = jnp.where(z == at_z, at_z - hop if below else at_z + hop, shard)
    return shard


def sum_kernel(main, *refs):
    out, ins = refs[-1], refs[:-1]
    count = len(ins) // 2
    for k in range(count):
        at = pl.multiple_of(shard_at(count, k) * main, SUB)
        total = ins[k][...].astype(F32) + ins[count + k][...].astype(F32)
        out[pl.ds(at, main), :] = total.astype(BF16)


def finish_kernel(scale, main, count, sums, other_sums, out, laid, sems):
    channels = out.shape[2]
    rows, half = channels // count, out.shape[1] // 2
    unit = rows // 2
    me = lax.axis_index("tm")
    copies = []
    for which, source in ((me, sums), (1 - me, other_sums)):
        start = pl.multiple_of(which * half, 8)
        for a in range(3):
            for q in range(9):
                base = q * unit if q < 7 else a * 2 * unit + (q - 7) * unit
                step = a if q < 7 else 3
                total = None
                for s in range(count):
                    piece = source[s * main + base : s * main + base + unit, :].astype(F32)
                    mask = in_slot(channels, rows, (s + step) % count)
                    total = piece if total is None else jnp.where(mask, piece, total)
                total = total * scale
                if step:
                    total = pltpu.roll(total, channels - step * rows, 1)
                laid[a, pl.ds(start + q * unit, unit), :] = total
            at = pl.ds(start, half)
            copy = pltpu.make_async_copy(laid.at[a, at], out.at[a, at], sems.at[len(copies)])
            copy.start()
            copies.append(copy)
    for copy in copies:
        copy.wait()


def local_fast(features, kernel, cotangent):
    rows, _, frames, pixels = features.shape
    length = frames * pixels
    count = lax.axis_size("chan")
    channels = rows * count
    taps = kernel.shape[1]
    half = 9 * rows // 2
    main, _ = packed_rows(half)
    sds = jax.ShapeDtypeStruct
    chip = sds((rows, 2 * length), BF16)
    term_shape = sds((main, channels), BF16)
    stack_shape = sds((half, 2 * length + 2 * pixels), BF16)
    share_shape = sds((rows, 2 * length), F32)
    rhs = pltpu.VMEM((channels, 2 * length), BF16)

    def hop(x):
        pairs = [(2 * z, 2 * z + 2) for z in range(count - 1)]
        pairs += [(2 * z + 1, 2 * z - 1) for z in range(1, count)]
        return lax.ppermute(x, ("chan", "tm"), pairs)

    weights = jnp.transpose(kernel, (1, 0, 2)).reshape(taps * rows, channels)
    features_other = rotate(features, "tm", 1)
    cot_other = rotate(cotangent, "tm", 1)
    full = run(
        activate_kernel,
        (features, features_other),
        out_shape=chip,
        out_specs=whole(),
        name="activate",
    )
    came = [hop(full)]
    own_term, stack, flat = run(
        functools.partial(own_terms_kernel, pixels),
        (full, cotangent, cot_other),
        out_shape=(term_shape, stack_shape, sds((rows, 2 * length), F32)),
        out_specs=(whole(),) * 3,
        scratch_shapes=[rhs],
        name="own_terms",
    )
    terms, got = [own_term], [rotate(own_term, "dp", 1)]
    share, stack_other = run(
        functools.partial(far_share_kernel, pixels, count - 1),
        (weights, stack, flat),
        waits=(own_term,),
        out_shape=(share_shape, stack_shape),
        out_specs=(whole(),) * 2,
        name="far_share",
    )
    blocks = []
    for step in range(2, count + 1):
        here = after(came[-1], share, *got[step - 3 : step - 2] if step > 2 else ())
        blocks += [here, rotate(here, "tm", 1)]
        message = run(
            functools.partial(message_kernel, count, step),
            (here, share),
            out_shape=chip,
            out_specs=whole(),
            name=f"message_{step}",
        )
        came.append(hop(message))
        hops = sorted({arrivals(count, z)[step - 2][0] for z in range(count)})
        held = [b for h in hops for b in blocks[2 * h - 2 : 2 * h]]
        term = run(
            functools.partial(terms_kernel, pixels, count, step - 2, hops),
            (stack, *held),
            out_shape=term_shape,
            out_specs=whole(),
            scratch_shapes=[rhs],
            name=f"terms_{step - 1}",
        )
        terms.append(term)
        got.append(rotate(term, "dp", 1))
        left = count - step
        if left > 1:
            share = run(
                functools.partial(share_kernel, pixels, left),
                (weights, stack, stack_other),
                waits=(term,),
                out_shape=share_shape,
                out_specs=whole(),
                name=f"share_{left}",
            )
        elif left == 1:
            share, own_share = run(
                functools.partial(near_share_kernel, pixels, left),
                (weights, stack, stack_other),
                waits=(term,),
                out_shape=(share_shape, sds((rows, length), F32)),
                out_specs=(whole(),) * 2,
                name="near_share",
            )

    conv_out, token = run(
        functools.partial(conv_kernel, pixels),
        (weights, full, *blocks),
        waits=(terms[-1],),
        out_shape=(sds(features.shape, BF16), sds(TOKEN, F32)),
        out_specs=(whole(),) * 2,
        scratch_shapes=[pltpu.VMEM((channels, (frames + 2) * pixels), BF16)],
        name="conv",
    )
    sums_of_shares = after(came[-1], token)
    feature_grad, token = run(
        functools.partial(feature_kernel, pixels),
        (features, own_share, sums_of_shares, rotate(sums_of_shares, "tm", 1)),
        waits=(got[-2],),
        out_shape=(sds(features.shape, BF16), sds(TOKEN, F32)),
        out_specs=(whole(),) * 2,
        cost_estimate=cost(FEATURE_COST),
        name="feature_grad",
    )
    sums = run(
        functools.partial(sum_kernel, main),
        (*terms, *got),
        waits=(token,),
        out_shape=sds((count * main, channels), BF16),
        out_specs=whole(),
        name="sums",
    )
    scale = 1.0 / math.sqrt(lax.axis_size("dp") * lax.axis_size("tm") * length)
    grad_shape = (3, 9 * rows, channels)
    kernel_grad = run(
        functools.partial(finish_kernel, scale, main, count),
        (sums, rotate(sums, "tm", 1)),
        out_shape=sds(grad_shape, F32),
        out_specs=pl.BlockSpec(memory_space=pl.ANY),
        scratch_shapes=[pltpu.VMEM(grad_shape, F32), pltpu.SemaphoreType.DMA((6,))],
        name="kernel_grad",
    )
    kernel_grad = jnp.transpose(kernel_grad.reshape(taps, rows, channels), (1, 0, 2))
    return (conv_out, feature_grad, kernel_grad)


def local(features, kernel, cotangent):
    rows, clips, _, pixels = features.shape
    fits = (
        clips == 1
        and lax.axis_size("tm") == 2
        and lax.axis_size("dp") == 2
        and rows % (2 * SUB) == 0
        and pixels % 128 == 0
        and kernel.shape[1] == 27
        and lax.axis_size("chan") == 4
    )
    return (local_fast if fits else local_generic)(features, kernel, cotangent)


def solution(mesh):
    return jax.shard_map(
        local,
        mesh=mesh,
        in_specs=(
            P("chan", ("groups", "dp"), "tm", None),
            P("chan", None, None),
            P("chan", ("groups", "dp"), "tm", None),
        ),
        out_specs=(
            P("chan", ("groups", "dp"), "tm", None),
            P("chan", ("groups", "dp"), "tm", None),
            P(("groups", "chan"), None, None),
        ),
        check_vma=False,
    )
```

```python
import functools
import math

import jax
import jax.numpy as jnp
from jax import lax
from jax.experimental import pallas as pl
from jax.experimental.pallas import tpu as pltpu
from jax.sharding import PartitionSpec as P

WID = 64
SUB = 16
F32 = jnp.float32
BF16 = jnp.bfloat16
VMEM_LIMIT = 24 * 1024 * 1024
TOKEN = (8, 128)
FEATURE_COST = 1024 * 1024


def from_behind(x, axis, by):
    size = lax.axis_size(axis)
    pairs = [(i, i + by) for i in range(size) if 0 <= i + by < size]
    return lax.ppermute(x, axis, pairs)


def padded_copies(block):
    pixels = block.shape[-1]
    column = lax.broadcasted_iota(jnp.int32, (pixels,), 0) % WID
    nothing = jnp.zeros((), block.dtype)
    widths = [(0, 0), (0, 0), (0, 0), (WID + 1, WID + 1)]
    left_cut = jnp.pad(jnp.where(column == WID - 1, nothing, block), widths)
    untouched = jnp.pad(block, widths)
    right_cut = jnp.pad(jnp.where(column == 0, nothing, block), widths)
    return (left_cut, untouched, right_cut)


def tap_window(copies, first_frame, vertical, horizontal, frames, pixels):
    source = copies[horizontal]
    offset = vertical * WID + horizontal
    return source[:, :, first_frame : first_frame + frames, offset : offset + pixels]


def stacked_taps(copies, first_frame, flipped, frames, pixels):
    pieces = []
    for vertical in range(3):
        for horizontal in range(3):
            if flipped:
                pieces.append(
                    tap_window(copies, first_frame, 2 - vertical, 2 - horizontal, frames, pixels)
                )
            else:
                pieces.append(tap_window(copies, first_frame, vertical, horizontal, frames, pixels))
    concatenated = jnp.concatenate(pieces, axis=0)
    return concatenated.reshape(concatenated.shape[0], -1)


def local_generic(features, kernel, cotangent):
    channels, clip_count, frames, pixels = features.shape
    flat_length = clip_count * frames * pixels
    widened = features.astype(F32)
    logistic = jax.nn.sigmoid(widened)
    activation = (widened * logistic).astype(BF16)
    slope_factor = logistic * (1.0 + widened * (1.0 - logistic))
    earlier = from_behind(activation[:, :, frames - 2 :, :], "tm", 1)
    extended = jnp.concatenate([earlier, activation], axis=2)
    upcoming = from_behind(cotangent[:, :, :2, :], "tm", -1)
    later_padded = jnp.concatenate([cotangent, upcoming], axis=2)
    cotangent_rows = cotangent.reshape(channels, -1)
    portion = lax.all_gather(extended, "chan", axis=0, tiled=True)
    out_sum = jnp.zeros((channels, flat_length), F32)
    amount = portion.shape[0]
    copies = padded_copies(portion)
    grad_parts = []
    for temporal in range(3):
        stacked = stacked_taps(copies, temporal, False, frames, pixels)
        weights = kernel[:, 9 * temporal : 9 * temporal + 9, :].reshape(channels, 9 * amount)
        out_sum = out_sum + jnp.dot(weights, stacked, preferred_element_type=F32)
        grad_parts.append(
            lax.dot_general(
                cotangent_rows, stacked, (((1,), (1,)), ((), ())), preferred_element_type=F32
            ).reshape(channels, 9, amount)
        )
    grad_sum = jnp.concatenate(grad_parts, axis=1)
    conv_out = out_sum.reshape(features.shape).astype(BF16)
    position_count = lax.axis_size("dp") * lax.axis_size("tm") * flat_length
    kernel_grad = lax.psum(grad_sum, ("tm", "dp")) * (1.0 / math.sqrt(position_count))
    padded_later = padded_copies(later_padded)
    summed = jnp.zeros((amount, flat_length), F32)
    for temporal in range(3):
        weights = jnp.transpose(
            kernel[:, 9 * temporal : 9 * temporal + 9, :], (2, 1, 0)
        ).reshape(amount, 9 * channels)
        stacked = stacked_taps(padded_later, 2 - temporal, True, frames, pixels)
        summed = summed + jnp.dot(weights, stacked, preferred_element_type=F32)
    before_slope = lax.psum_scatter(
        summed.reshape(amount, clip_count, frames, pixels), "chan", scatter_dimension=0, tiled=True
    )
    feature_grad = (before_slope * slope_factor).astype(BF16)
    return (conv_out, feature_grad, kernel_grad)


def rotate(x, axis, by):
    size = lax.axis_size(axis)
    return lax.ppermute(x, axis, [(i, (i + by) % size) for i in range(size)])


def shifted(frame, down, right):
    pixels = frame.shape[-1]
    if down == 0 and right == 0:
        return frame
    cell = lax.broadcasted_iota(jnp.int32, (1, pixels), 1)
    row, column = cell // WID + down, cell % WID + right
    inside = (row >= 0) & (row < pixels // WID) & (column >= 0) & (column < WID)
    moved = pltpu.roll(frame, (-(down * WID + right)) % pixels, 1)
    return jnp.where(inside, moved, 0.0)


def after(x, *others):
    anywhere = pl.BlockSpec(memory_space=pl.ANY)
    return pl.pallas_call(
        lambda *refs: None,
        out_shape=jax.ShapeDtypeStruct(x.shape, x.dtype),
        in_specs=[anywhere] * (1 + len(others)),
        out_specs=anywhere,
        input_output_aliases={0: 0},
        compiler_params=pltpu.CompilerParams(vmem_limit_bytes=1024 * 1024),
        cost_estimate=cost(),
        name="hand_on",
    )(x, *others)


def run(kernel, args, waits=(), **options):
    options.setdefault("in_specs", [whole()] * len(args))
    options.setdefault("cost_estimate", cost())
    options["in_specs"] = list(options["in_specs"]) + [
        pl.BlockSpec(memory_space=pl.ANY) for _ in waits
    ]
    count = len(args)

    def body(*refs):
        kernel(*refs[:count], *refs[count + len(waits) :])

    return pl.pallas_call(
        body, compiler_params=pltpu.CompilerParams(vmem_limit_bytes=VMEM_LIMIT), **options
    )(*args, *waits)


def cost(bytes_like=1):
    return pl.CostEstimate(flops=1, bytes_accessed=bytes_like, transcendentals=0)


def whole():
    return pl.BlockSpec(memory_space=pltpu.VMEM)


def activate_kernel(features, activation):
    frames, pixels = features.shape[2:]
    v = features[:, 0].astype(F32)
    act = v / (1.0 + jnp.exp(-v))
    for t in range(frames):
        activation[:, t * pixels : (t + 1) * pixels] = act[:, t, :].astype(BF16)


def shard_at(count, k):
    z = lax.axis_index("chan")
    return (z, lax.rem(z + 2, count), z + 1 - 2 * lax.rem(z, 2), count - 1 - z)[k]


def in_slot(channels, rows, slot):
    lane = lax.broadcasted_iota(jnp.int32, (1, channels), 1)
    return (lane >= slot * rows) & (lane < (slot + 1) * rows)


def packed_rows(total):
    unit = total // 9
    return 7 * unit, 2 * unit


def fill_stack(pixels, flat, stack, which):
    rows = flat.shape[0]
    unit = rows // 2
    frames = flat.shape[1] // pixels
    for half in range(2):

        @pl.when(which == half)
        def _(half=half):
            for t in range(frames):
                at = slice(t * pixels, (t + 1) * pixels)
                for q in range(9):
                    tap, part = divmod(9 * half + q, 2)
                    i, j = divmod(tap, 3)
                    frame = flat[part * unit : (part + 1) * unit, at]
                    stack[q * unit : (q + 1) * unit, at] = shifted(frame, 1 - i, 1 - j).astype(BF16)


def block_terms(pixels, k, stack, here, there, out, rhs):
    channels = out.shape[1]
    rows, length = here.shape
    lanes, count = 2 * length, channels // rows
    shard = shard_at(count, k)
    for core in range(2):

        @pl.when(lax.axis_index("tm") == core)
        def _(first=(here, there)[core], second=(there, here)[core]):
            for a in range(3):
                skip = (2 - a) * pixels
                at = pl.ds(pl.multiple_of(lax.rem(shard + a, count) * rows, SUB), rows)
                if skip:
                    rhs[at, :skip] = jnp.zeros((rows, skip), BF16)
                rhs[at, skip : skip + length] = first[...]
                rhs[at, skip + length :] = second[:, : length - skip]

    last = lax.rem(shard + 3, count)
    rhs[pl.ds(pl.multiple_of(last * rows, SUB), rows), :] = jnp.zeros((rows, lanes), BF16)
    terms = lax.dot_general(
        stack[...], rhs[...], (((1,), (1,)), ((), ())), preferred_element_type=F32
    )
    main, tail = packed_rows(terms.shape[0])
    free = in_slot(channels, rows, last)
    for a in range(3):
        at = slice(a * tail, (a + 1) * tail)
        moved = pltpu.roll(terms[main:], (3 - a) * rows, 1)
        out[at, :] = jnp.where(free, moved, terms[at]).astype(BF16)
    out[3 * tail :, :] = terms[3 * tail : main].astype(BF16)


def own_terms_kernel(pixels, mine, other, cot, cot_other, out, stack, later, rhs, flat):
    _, _, frames, _ = cot.shape
    length = frames * pixels
    me = lax.axis_index("tm")
    for core, source in ((me, cot), (1 - me, cot_other)):
        wide = source[:, 0].astype(F32)
        for t in range(frames):
            at = pl.multiple_of((core * frames + t) * pixels, pixels)
            flat[:, pl.ds(at, pixels)] = wide[:, t, :]
    own = pl.ds(pl.multiple_of(me * length, pixels), length)
    later[:, :length] = flat[:, own].astype(BF16)
    after_own = flat[:, length : length + 2 * pixels]
    later[:, length:] = jnp.where(me == 0, after_own, 0.0).astype(BF16)
    fill_stack(pixels, flat, stack, me)
    block_terms(pixels, 0, stack, mine, other, out, rhs)


def terms_kernel(pixels, k, stack, here, there, out, rhs):
    block_terms(pixels, k, stack, here, there, out, rhs)


def share_kernel(pixels, weights, later, own, kept, sent, stack, total):
    rows = later.shape[0]
    length = own.shape[1]
    frames = length // pixels
    count = weights.shape[1] // rows
    for t in range(frames + 2):
        at = slice(t * pixels, (t + 1) * pixels)
        frame = later[:, at].astype(F32)
        for i in range(3):
            for j in range(3):
                row = (3 * i + j) * rows
                stack[row : row + rows, at] = shifted(frame, 1 - i, 1 - j).astype(BF16)
    taps = 9 * rows
    acc = None
    for a in range(3):
        term = lax.dot_general(
            weights[a * taps : (a + 1) * taps, :],
            stack[:, (2 - a) * pixels : (2 - a) * pixels + length],
            (((0,), (0,)), ((), ())),
            preferred_element_type=F32,
        )
        acc = term if acc is None else acc + term
    total[...] = acc

    def part(k):
        return total[pl.ds(pl.multiple_of(shard_at(count, k) * rows, SUB), rows), :]

    own[...] = part(0)
    kept[...] = part(1)
    sent[0] = part(2).astype(BF16)
    sent[1] = part(3).astype(BF16)


def add_kernel(kept, came, out):
    out[...] = (kept[...] + came[1].astype(F32)).astype(out.dtype)


def conv_kernel(pixels, weights, *refs):
    blocks, (out, token, act) = refs[:-3], refs[-3:]
    token[...] = jnp.zeros(TOKEN, F32)
    rows, _, frames, _ = out.shape
    count = weights.shape[1] // rows
    length, front = frames * pixels, 2 * pixels
    me = lax.axis_index("tm")
    for k in range(count):
        here, there = blocks[2 * k], blocks[2 * k + 1]
        at = pl.ds(pl.multiple_of(shard_at(count, k) * rows, SUB), rows)
        earlier = there[:, length - front :]
        act[at, :front] = jnp.where(me == 0, jnp.zeros_like(earlier), earlier)
        act[at, front:] = here[...]

    taps = 9 * rows
    for t in range(frames):
        z_t = None
        for a in range(3):
            term = jnp.dot(
                weights[a * taps : (a + 1) * taps, :],
                act[:, (t + a) * pixels : (t + a + 1) * pixels],
                preferred_element_type=F32,
            )
            z_t = term if z_t is None else z_t + term
        acc = None
        for i in range(3):
            for j in range(3):
                at = (3 * i + j) * rows
                moved = shifted(z_t[at : at + rows, :], i - 1, j - 1)
                acc = moved if acc is None else acc + moved
        out[:, 0, t, :] = acc.astype(BF16)


def feature_kernel(pixels, features, own, first, second, out, token):
    token[...] = jnp.zeros(TOKEN, F32)
    frames = features.shape[2]
    total = own[...] + first[0].astype(F32) + second[...].astype(F32)
    v = features[:, 0].astype(F32)
    s = 1.0 / (1.0 + jnp.exp(-v))
    slope = s * (1.0 + v * (1.0 - s))
    for t in range(frames):
        piece = total[:, t * pixels : (t + 1) * pixels] * slope[:, t, :]
        out[:, 0, t, :] = piece.astype(BF16)


def sum_kernel(main, *refs):
    out, ins = refs[-1], refs[:-1]
    count = len(ins) // 2
    for k in range(count):
        at = pl.multiple_of(shard_at(count, k) * main, SUB)
        total = ins[k][...].astype(F32) + ins[count + k][...].astype(F32)
        out[pl.ds(at, main), :] = total.astype(BF16)


def finish_kernel(scale, main, count, sums, other_sums, out, laid, sems):
    channels = out.shape[2]
    rows, half = channels // count, out.shape[1] // 2
    unit = rows // 2
    me = lax.axis_index("tm")
    copies = []
    for which, source in ((me, sums), (1 - me, other_sums)):
        start = pl.multiple_of(which * half, 8)
        for a in range(3):
            for q in range(9):
                base = q * unit if q < 7 else a * 2 * unit + (q - 7) * unit
                step = a if q < 7 else 3
                total = None
                for s in range(count):
                    piece = source[s * main + base : s * main + base + unit, :].astype(F32)
                    mask = in_slot(channels, rows, (s + step) % count)
                    total = piece if total is None else jnp.where(mask, piece, total)
                total = total * scale
                if step:
                    total = pltpu.roll(total, channels - step * rows, 1)
                laid[a, pl.ds(start + q * unit, unit), :] = total
            at = pl.ds(start, half)
            copy = pltpu.make_async_copy(laid.at[a, at], out.at[a, at], sems.at[len(copies)])
            copy.start()
            copies.append(copy)
    for copy in copies:
        copy.wait()


def local_fast(features, kernel, cotangent):
    rows, _, frames, pixels = features.shape
    length = frames * pixels
    count = lax.axis_size("chan")
    channels = rows * count
    taps = kernel.shape[1]
    half = 9 * rows // 2
    main, _ = packed_rows(half)
    sds = jax.ShapeDtypeStruct
    block_shape = sds((rows, length), BF16)
    term_shape = sds((main, channels), BF16)
    stack_shape = sds((half, 2 * length), BF16)
    rhs = pltpu.VMEM((channels, 2 * length), BF16)

    def swap(x, far):
        return lax.ppermute(x, "chan", [(z, z ^ far) for z in range(count)])

    weights = jnp.transpose(kernel, (1, 0, 2)).reshape(taps * rows, channels)
    cot_other = rotate(cotangent, "tm", 1)
    activation = run(
        activate_kernel,
        (features,),
        out_shape=block_shape,
        out_specs=whole(),
        name="activate",
    )
    other = rotate(activation, "tm", 1)
    far, near = swap(activation, 2), swap(activation, 1)
    own_term, stack, later = run(
        functools.partial(own_terms_kernel, pixels),
        (activation, other, cotangent, cot_other),
        out_shape=(term_shape, stack_shape, sds((rows, length + 2 * pixels), BF16)),
        out_specs=(whole(),) * 3,
        scratch_shapes=[rhs, pltpu.VMEM((rows, 2 * length), F32)],
        name="own_terms",
    )
    terms, got = [own_term], [rotate(own_term, "dp", 1)]
    own_share, kept, sent = run(
        functools.partial(share_kernel, pixels),
        (weights, later),
        waits=(own_term,),
        out_shape=(
            sds((rows, length), F32),
            sds((rows, length), F32),
            sds((2, rows, length), BF16),
        ),
        out_specs=(whole(),) * 3,
        scratch_shapes=[
            pltpu.VMEM((9 * rows, (frames + 2) * pixels), BF16),
            pltpu.VMEM((channels, length), F32),
        ],
        name="shares",
    )
    first_share = swap(sent, 1)
    blocks = [activation, other]

    def terms_of(k, here, waits=()):
        blocks.extend((here, rotate(here, "tm", 1)))
        term = run(
            functools.partial(terms_kernel, pixels, k),
            (stack, *blocks[-2:]),
            waits=waits,
            out_shape=term_shape,
            out_specs=whole(),
            scratch_shapes=[rhs],
            name=f"terms_{k}",
        )
        terms.append(term)
        got.append(rotate(term, "dp", 1))
        return term

    far = after(far, own_share, near)
    near = after(near, far)
    last = swap(far, 1)
    term = terms_of(1, far, (got[0],))
    term = terms_of(2, near, (term,))
    carry = run(
        add_kernel,
        (kept, first_share),
        waits=(term,),
        out_shape=block_shape,
        out_specs=whole(),
        name="carry_share",
    )
    second_share = swap(carry, 2)
    term = terms_of(3, after(last, carry, got[1]))

    conv_out, token = run(
        functools.partial(conv_kernel, pixels),
        (weights, *blocks),
        waits=(term,),
        out_shape=(sds(features.shape, BF16), sds(TOKEN, F32)),
        out_specs=(whole(),) * 2,
        scratch_shapes=[pltpu.VMEM((channels, (frames + 2) * pixels), BF16)],
        name="conv",
    )
    feature_grad, token = run(
        functools.partial(feature_kernel, pixels),
        (features, own_share, first_share, second_share),
        waits=(token, got[2]),
        out_shape=(sds(features.shape, BF16), sds(TOKEN, F32)),
        out_specs=(whole(),) * 2,
        cost_estimate=cost(FEATURE_COST),
        name="feature_grad",
    )
    sums = run(
        functools.partial(sum_kernel, main),
        (*terms, *got),
        waits=(token,),
        out_shape=sds((count * main, channels), BF16),
        out_specs=whole(),
        name="sums",
    )
    scale = 1.0 / math.sqrt(lax.axis_size("dp") * lax.axis_size("tm") * length)
    grad_shape = (3, 9 * rows, channels)
    kernel_grad = run(
        functools.partial(finish_kernel, scale, main, count),
        (sums, rotate(sums, "tm", 1)),
        out_shape=sds(grad_shape, F32),
        out_specs=pl.BlockSpec(memory_space=pl.ANY),
        scratch_shapes=[pltpu.VMEM(grad_shape, F32), pltpu.SemaphoreType.DMA((6,))],
        name="kernel_grad",
    )
    kernel_grad = jnp.transpose(kernel_grad.reshape(taps, rows, channels), (1, 0, 2))
    return (conv_out, feature_grad, kernel_grad)


def local(features, kernel, cotangent):
    rows, clips, _, pixels = features.shape
    fits = (
        clips == 1
        and lax.axis_size("tm") == 2
        and lax.axis_size("dp") == 2
        and rows % (2 * SUB) == 0
        and pixels % 128 == 0
        and kernel.shape[1] == 27
        and lax.axis_size("chan") == 4
    )
    return (local_fast if fits else local_generic)(features, kernel, cotangent)


def solution(mesh):
    return jax.shard_map(
        local,
        mesh=mesh,
        in_specs=(
            P("chan", ("groups", "dp"), "tm", None),
            P("chan", None, None),
            P("chan", ("groups", "dp"), "tm", None),
        ),
        out_specs=(
            P("chan", ("groups", "dp"), "tm", None),
            P("chan", ("groups", "dp"), "tm", None),
            P(("groups", "chan"), None, None),
        ),
        check_vma=False,
    )
```

```python
import functools
import math

import jax
import jax.numpy as jnp
from jax import lax
from jax.experimental import pallas as pl
from jax.experimental.pallas import tpu as pltpu
from jax.sharding import PartitionSpec as P

WID = 64
SUB = 16
F32 = jnp.float32
BF16 = jnp.bfloat16
VMEM_LIMIT = 24 * 1024 * 1024
TOKEN = (8, 128)
FEATURE_COST = 3 * 10**9


def from_behind(x, axis, by):
    size = lax.axis_size(axis)
    pairs = [(i, i + by) for i in range(size) if 0 <= i + by < size]
    return lax.ppermute(x, axis, pairs)


def padded_copies(block):
    pixels = block.shape[-1]
    column = lax.broadcasted_iota(jnp.int32, (pixels,), 0) % WID
    nothing = jnp.zeros((), block.dtype)
    widths = [(0, 0), (0, 0), (0, 0), (WID + 1, WID + 1)]
    left_cut = jnp.pad(jnp.where(column == WID - 1, nothing, block), widths)
    untouched = jnp.pad(block, widths)
    right_cut = jnp.pad(jnp.where(column == 0, nothing, block), widths)
    return (left_cut, untouched, right_cut)


def tap_window(copies, first_frame, vertical, horizontal, frames, pixels):
    source = copies[horizontal]
    offset = vertical * WID + horizontal
    return source[:, :, first_frame : first_frame + frames, offset : offset + pixels]


def stacked_taps(copies, first_frame, flipped, frames, pixels):
    pieces = []
    for vertical in range(3):
        for horizontal in range(3):
            if flipped:
                pieces.append(
                    tap_window(copies, first_frame, 2 - vertical, 2 - horizontal, frames, pixels)
                )
            else:
                pieces.append(tap_window(copies, first_frame, vertical, horizontal, frames, pixels))
    concatenated = jnp.concatenate(pieces, axis=0)
    return concatenated.reshape(concatenated.shape[0], -1)


def local_generic(features, kernel, cotangent):
    channels, clip_count, frames, pixels = features.shape
    flat_length = clip_count * frames * pixels
    widened = features.astype(F32)
    logistic = jax.nn.sigmoid(widened)
    activation = (widened * logistic).astype(BF16)
    slope_factor = logistic * (1.0 + widened * (1.0 - logistic))
    earlier = from_behind(activation[:, :, frames - 2 :, :], "tm", 1)
    extended = jnp.concatenate([earlier, activation], axis=2)
    upcoming = from_behind(cotangent[:, :, :2, :], "tm", -1)
    later_padded = jnp.concatenate([cotangent, upcoming], axis=2)
    cotangent_rows = cotangent.reshape(channels, -1)
    portion = lax.all_gather(extended, "chan", axis=0, tiled=True)
    out_sum = jnp.zeros((channels, flat_length), F32)
    amount = portion.shape[0]
    copies = padded_copies(portion)
    grad_parts = []
    for temporal in range(3):
        stacked = stacked_taps(copies, temporal, False, frames, pixels)
        weights = kernel[:, 9 * temporal : 9 * temporal + 9, :].reshape(channels, 9 * amount)
        out_sum = out_sum + jnp.dot(weights, stacked, preferred_element_type=F32)
        grad_parts.append(
            lax.dot_general(
                cotangent_rows, stacked, (((1,), (1,)), ((), ())), preferred_element_type=F32
            ).reshape(channels, 9, amount)
        )
    grad_sum = jnp.concatenate(grad_parts, axis=1)
    conv_out = out_sum.reshape(features.shape).astype(BF16)
    position_count = lax.axis_size("dp") * lax.axis_size("tm") * flat_length
    kernel_grad = lax.psum(grad_sum, ("tm", "dp")) * (1.0 / math.sqrt(position_count))
    padded_later = padded_copies(later_padded)
    summed = jnp.zeros((amount, flat_length), F32)
    for temporal in range(3):
        weights = jnp.transpose(
            kernel[:, 9 * temporal : 9 * temporal + 9, :], (2, 1, 0)
        ).reshape(amount, 9 * channels)
        stacked = stacked_taps(padded_later, 2 - temporal, True, frames, pixels)
        summed = summed + jnp.dot(weights, stacked, preferred_element_type=F32)
    before_slope = lax.psum_scatter(
        summed.reshape(amount, clip_count, frames, pixels), "chan", scatter_dimension=0, tiled=True
    )
    feature_grad = (before_slope * slope_factor).astype(BF16)
    return (conv_out, feature_grad, kernel_grad)


def rotate(x, axis, by):
    size = lax.axis_size(axis)
    return lax.ppermute(x, axis, [(i, (i + by) % size) for i in range(size)])


def shifted(frame, down, right):
    pixels = frame.shape[-1]
    if down == 0 and right == 0:
        return frame
    cell = lax.broadcasted_iota(jnp.int32, (1, pixels), 1)
    row, column = cell // WID + down, cell % WID + right
    inside = (row >= 0) & (row < pixels // WID) & (column >= 0) & (column < WID)
    moved = pltpu.roll(frame, (-(down * WID + right)) % pixels, 1)
    return jnp.where(inside, moved, 0.0)


def after(x, *others):
    anywhere = pl.BlockSpec(memory_space=pl.ANY)
    return pl.pallas_call(
        lambda *refs: None,
        out_shape=jax.ShapeDtypeStruct(x.shape, x.dtype),
        in_specs=[anywhere] * (1 + len(others)),
        out_specs=anywhere,
        input_output_aliases={0: 0},
        compiler_params=pltpu.CompilerParams(vmem_limit_bytes=1024 * 1024),
        cost_estimate=cost(),
        name="hand_on",
    )(x, *others)


def run(kernel, args, waits=(), **options):
    options.setdefault("in_specs", [whole()] * len(args))
    options.setdefault("cost_estimate", cost())
    options["in_specs"] = list(options["in_specs"]) + [
        pl.BlockSpec(memory_space=pl.ANY) for _ in waits
    ]
    count = len(args)

    def body(*refs):
        kernel(*refs[:count], *refs[count + len(waits) :])

    return pl.pallas_call(
        body, compiler_params=pltpu.CompilerParams(vmem_limit_bytes=VMEM_LIMIT), **options
    )(*args, *waits)


def cost(flops=1):
    return pl.CostEstimate(flops=flops, bytes_accessed=1, transcendentals=0)


def whole():
    return pl.BlockSpec(memory_space=pltpu.VMEM)


def activate_kernel(features, activation):
    frames, pixels = features.shape[2:]
    v = features[:, 0].astype(F32)
    act = v / (1.0 + jnp.exp(-v))
    for t in range(frames):
        activation[:, t * pixels : (t + 1) * pixels] = act[:, t, :].astype(BF16)


def shard_at(count, k):
    z = lax.axis_index("chan")
    return (z, lax.rem(z + 2, count), z + 1 - 2 * lax.rem(z, 2), count - 1 - z)[k]


def in_slot(channels, rows, slot):
    lane = lax.broadcasted_iota(jnp.int32, (1, channels), 1)
    return (lane >= slot * rows) & (lane < (slot + 1) * rows)


def packed_rows(total):
    unit = total // 9
    return 7 * unit, 2 * unit


def fill_stack(pixels, flat, stack, which):
    rows = flat.shape[0]
    unit = rows // 2
    frames = flat.shape[1] // pixels
    for half in range(2):

        @pl.when(which == half)
        def _(half=half):
            for t in range(frames):
                at = slice(t * pixels, (t + 1) * pixels)
                for q in range(9):
                    tap, part = divmod(9 * half + q, 2)
                    i, j = divmod(tap, 3)
                    frame = flat[part * unit : (part + 1) * unit, at]
                    stack[q * unit : (q + 1) * unit, at] = shifted(frame, 1 - i, 1 - j).astype(BF16)


def block_terms(pixels, k, stack, here, there, out, rhs):
    channels = out.shape[1]
    rows, length = here.shape
    lanes, count = 2 * length, channels // rows
    shard = shard_at(count, k)
    for core in range(2):

        @pl.when(lax.axis_index("tm") == core)
        def _(first=(here, there)[core], second=(there, here)[core]):
            for a in range(3):
                skip = (2 - a) * pixels
                at = pl.ds(pl.multiple_of(lax.rem(shard + a, count) * rows, SUB), rows)
                if skip:
                    rhs[at, :skip] = jnp.zeros((rows, skip), BF16)
                rhs[at, skip : skip + length] = first[...]
                rhs[at, skip + length :] = second[:, : length - skip]

    last = lax.rem(shard + 3, count)
    rhs[pl.ds(pl.multiple_of(last * rows, SUB), rows), :] = jnp.zeros((rows, lanes), BF16)
    terms = lax.dot_general(
        stack[...], rhs[...], (((1,), (1,)), ((), ())), preferred_element_type=F32
    )
    main, tail = packed_rows(terms.shape[0])
    free = in_slot(channels, rows, last)
    for a in range(3):
        at = slice(a * tail, (a + 1) * tail)
        moved = pltpu.roll(terms[main:], (3 - a) * rows, 1)
        out[at, :] = jnp.where(free, moved, terms[at]).astype(BF16)
    out[3 * tail :, :] = terms[3 * tail : main].astype(BF16)


def own_terms_kernel(pixels, mine, other, flat, out, stack, rhs):
    fill_stack(pixels, flat, stack, lax.axis_index("tm"))
    block_terms(pixels, 0, stack, mine, other, out, rhs)


def terms_kernel(pixels, k, stack, here, there, out, rhs):
    block_terms(pixels, k, stack, here, there, out, rhs)


def share_kernel(pixels, weights, cot, cot_other, own, kept, sent, flat, held, mine, stack, total, sems):
    loads = [
        pltpu.make_async_copy(source, target, sems.at[n])
        for n, (source, target) in enumerate(((cot, mine), (weights, held)))
    ]
    for load in loads:
        load.start()
    rows, length = own.shape
    frames = length // pixels
    count = held.shape[1] // rows
    me = lax.axis_index("tm")

    def flatten(core, source):
        wide = source[:, 0].astype(F32)
        for t in range(frames):
            at = pl.multiple_of((core * frames + t) * pixels, pixels)
            flat[:, pl.ds(at, pixels)] = wide[:, t, :]

    flatten(1 - me, cot_other)
    loads[0].wait()
    flatten(me, mine)
    for t in range(frames + 2):
        at = slice(t * pixels, (t + 1) * pixels)
        if t < frames:
            frame = flat[:, pl.ds(pl.multiple_of((me * frames + t) * pixels, pixels), pixels)]
        else:
            frame = jnp.where(me == 0, flat[:, at], 0.0)
        for i in range(3):
            for j in range(3):
                row = (3 * i + j) * rows
                stack[row : row + rows, at] = shifted(frame, 1 - i, 1 - j).astype(BF16)
    loads[1].wait()
    taps = 9 * rows
    acc = None
    for a in range(3):
        term = lax.dot_general(
            held[a * taps : (a + 1) * taps, :],
            stack[:, (2 - a) * pixels : (2 - a) * pixels + length],
            (((0,), (0,)), ((), ())),
            preferred_element_type=F32,
        )
        acc = term if acc is None else acc + term
    total[...] = acc

    def part(k):
        return total[pl.ds(pl.multiple_of(shard_at(count, k) * rows, SUB), rows), :]

    own[...] = part(0)
    kept[...] = part(1)
    sent[0] = part(2).astype(BF16)
    sent[1] = part(3).astype(BF16)


def add_kernel(kept, came, out):
    out[...] = (kept[...] + came[1].astype(F32)).astype(out.dtype)


def conv_kernel(pixels, weights, *refs):
    blocks, (out, token, act) = refs[:-3], refs[-3:]
    token[...] = jnp.zeros(TOKEN, F32)
    rows, _, frames, _ = out.shape
    count = weights.shape[1] // rows
    length, front = frames * pixels, 2 * pixels
    me = lax.axis_index("tm")
    for k in range(count):
        here, there = blocks[2 * k], blocks[2 * k + 1]
        at = pl.ds(pl.multiple_of(shard_at(count, k) * rows, SUB), rows)
        earlier = there[:, length - front :]
        act[at, :front] = jnp.where(me == 0, jnp.zeros_like(earlier), earlier)
        act[at, front:] = here[...]

    taps = 9 * rows
    for t in range(frames):
        z_t = None
        for a in range(3):
            term = jnp.dot(
                weights[a * taps : (a + 1) * taps, :],
                act[:, (t + a) * pixels : (t + a + 1) * pixels],
                preferred_element_type=F32,
            )
            z_t = term if z_t is None else z_t + term
        acc = None
        for i in range(3):
            for j in range(3):
                at = (3 * i + j) * rows
                moved = shifted(z_t[at : at + rows, :], i - 1, j - 1)
                acc = moved if acc is None else acc + moved
        out[:, 0, t, :] = acc.astype(BF16)


def feature_kernel(pixels, features, own, first, second, out, token):
    token[...] = jnp.zeros(TOKEN, F32)
    frames = features.shape[2]
    total = own[...] + first[0].astype(F32) + second[...].astype(F32)
    v = features[:, 0].astype(F32)
    s = 1.0 / (1.0 + jnp.exp(-v))
    slope = s * (1.0 + v * (1.0 - s))
    for t in range(frames):
        piece = total[:, t * pixels : (t + 1) * pixels] * slope[:, t, :]
        out[:, 0, t, :] = piece.astype(BF16)


def sum_kernel(main, *refs):
    out, ins = refs[-1], refs[:-1]
    count = len(ins) // 2
    for k in range(count):
        total = ins[k][...].astype(F32) + ins[count + k][...].astype(F32)
        out[k * main : (k + 1) * main, :] = total.astype(BF16)


def finish_kernel(scale, main, early, other_early, late, other_late, out, laid, sems):
    channels = out.shape[2]
    first = early.shape[0] // main
    count = first + late.shape[0] // main
    rows, half = channels // count, out.shape[1] // 2
    unit = rows // 2
    me = lax.axis_index("tm")
    shards = [shard_at(count, k) for k in range(count)]
    copies = []
    for which, one, two in ((me, early, late), (1 - me, other_early, other_late)):
        start = pl.multiple_of(which * half, 8)
        for a in range(3):
            for q in range(9):
                base = q * unit if q < 7 else a * 2 * unit + (q - 7) * unit
                step = a if q < 7 else 3
                total = None
                for k, shard in enumerate(shards):
                    source, place = (one, k) if k < first else (two, k - first)
                    at = place * main + base
                    piece = source[at : at + unit, :].astype(F32)
                    mask = in_slot(channels, rows, lax.rem(shard + step, count))
                    total = piece if total is None else jnp.where(mask, piece, total)
                total = total * scale
                if step:
                    total = pltpu.roll(total, channels - step * rows, 1)
                laid[a, pl.ds(start + q * unit, unit), :] = total
            at = pl.ds(start, half)
            copy = pltpu.make_async_copy(laid.at[a, at], out.at[a, at], sems.at[len(copies)])
            copy.start()
            copies.append(copy)
    for copy in copies:
        copy.wait()


def in_place(x):
    return pltpu.with_memory_space_constraint(x, pltpu.HBM)


def local_fast(features, kernel, cotangent):
    rows, _, frames, pixels = features.shape
    length = frames * pixels
    count = lax.axis_size("chan")
    channels = rows * count
    taps = kernel.shape[1]
    half = 9 * rows // 2
    main, _ = packed_rows(half)
    sds = jax.ShapeDtypeStruct
    block_shape = sds((rows, length), BF16)
    term_shape = sds((main, channels), BF16)
    stack_shape = sds((half, 2 * length), BF16)
    rhs = pltpu.VMEM((channels, 2 * length), BF16)

    def swap(x, far):
        return lax.ppermute(x, "chan", [(z, z ^ far) for z in range(count)])

    weights = jnp.transpose(kernel, (1, 0, 2)).reshape(taps * rows, channels)
    cot_other = rotate(cotangent, "tm", 1)
    activation = run(
        activate_kernel,
        (features,),
        out_shape=block_shape,
        out_specs=whole(),
        name="activate",
    )
    other = rotate(activation, "tm", 1)
    far, near = swap(activation, 2), swap(activation, 1)
    own_share, kept, sent, flat = run(
        functools.partial(share_kernel, pixels),
        (in_place(weights), in_place(cotangent), cot_other),
        in_specs=[pl.BlockSpec(memory_space=pltpu.HBM)] * 2 + [whole()],
        out_shape=(
            sds((rows, length), F32),
            sds((rows, length), F32),
            sds((2, rows, length), BF16),
            sds((rows, 2 * length), F32),
        ),
        out_specs=(whole(),) * 4,
        scratch_shapes=[
            pltpu.VMEM((taps * rows, channels), BF16),
            pltpu.VMEM(cotangent.shape, BF16),
            pltpu.VMEM((9 * rows, (frames + 2) * pixels), BF16),
            pltpu.VMEM((channels, length), F32),
            pltpu.SemaphoreType.DMA((2,)),
        ],
        name="shares",
    )
    first_share = swap(sent, 1)
    own_term, stack = run(
        functools.partial(own_terms_kernel, pixels),
        (activation, other, flat),
        out_shape=(term_shape, stack_shape),
        out_specs=(whole(),) * 2,
        scratch_shapes=[rhs],
        name="own_terms",
    )
    terms, got = [own_term], [rotate(own_term, "dp", 1)]

    blocks = [activation, other]

    def terms_of(k, here, waits=()):
        blocks.extend((here, rotate(here, "tm", 1)))
        term = run(
            functools.partial(terms_kernel, pixels, k),
            (stack, *blocks[-2:]),
            waits=waits,
            out_shape=term_shape,
            out_specs=whole(),
            scratch_shapes=[rhs],
            name=f"terms_{k}",
        )
        terms.append(term)
        got.append(rotate(term, "dp", 1))
        return term

    far = after(far, own_term, near)
    near = after(near, far)
    last = swap(far, 1)
    term = terms_of(1, far, (got[0],))
    carry = run(
        add_kernel,
        (kept, first_share),
        waits=(term,),
        out_shape=block_shape,
        out_specs=whole(),
        name="carry_share",
    )
    second_share = swap(carry, 2)
    term = terms_of(2, near, (carry,))
    term = terms_of(3, after(last, term, got[1]))

    def sums(first, stop, waits=()):
        return run(
            functools.partial(sum_kernel, main),
            (*terms[first:stop], *got[first:stop]),
            waits=waits,
            out_shape=sds(((stop - first) * main, channels), BF16),
            out_specs=whole(),
            name=f"sums_{first}",
        )

    conv_out, token = run(
        functools.partial(conv_kernel, pixels),
        (weights, *blocks),
        waits=(term, got[2]),
        out_shape=(sds(features.shape, BF16), sds(TOKEN, F32)),
        out_specs=(whole(),) * 2,
        scratch_shapes=[pltpu.VMEM((channels, (frames + 2) * pixels), BF16)],
        name="conv",
    )
    early = sums(0, 2)
    feature_grad, token = run(
        functools.partial(feature_kernel, pixels),
        (features, own_share, first_share, second_share),
        waits=(token, early),
        out_shape=(sds(features.shape, BF16), sds(TOKEN, F32)),
        out_specs=(whole(),) * 2,
        cost_estimate=cost(FEATURE_COST),
        name="feature_grad",
    )
    late = sums(2, count, (token,))
    scale = 1.0 / math.sqrt(lax.axis_size("dp") * lax.axis_size("tm") * length)
    grad_shape = (3, 9 * rows, channels)
    kernel_grad = run(
        functools.partial(finish_kernel, scale, main),
        (early, rotate(early, "tm", 1), late, rotate(late, "tm", 1)),
        out_shape=sds(grad_shape, F32),
        out_specs=pl.BlockSpec(memory_space=pl.ANY),
        scratch_shapes=[pltpu.VMEM(grad_shape, F32), pltpu.SemaphoreType.DMA((6,))],
        name="kernel_grad",
    )
    kernel_grad = jnp.transpose(kernel_grad.reshape(taps, rows, channels), (1, 0, 2))
    return (conv_out, feature_grad, kernel_grad)


def local(features, kernel, cotangent):
    rows, clips, _, pixels = features.shape
    fits = (
        clips == 1
        and lax.axis_size("tm") == 2
        and lax.axis_size("dp") == 2
        and rows % (2 * SUB) == 0
        and pixels % 128 == 0
        and kernel.shape[1] == 27
        and lax.axis_size("chan") == 4
    )
    return (local_fast if fits else local_generic)(features, kernel, cotangent)


def solution(mesh):
    return jax.shard_map(
        local,
        mesh=mesh,
        in_specs=(
            P("chan", ("groups", "dp"), "tm", None),
            P("chan", None, None),
            P("chan", ("groups", "dp"), "tm", None),
        ),
        out_specs=(
            P("chan", ("groups", "dp"), "tm", None),
            P("chan", ("groups", "dp"), "tm", None),
            P(("groups", "chan"), None, None),
        ),
        check_vma=False,
    )
```

```python
import functools
import math

import jax
import jax.numpy as jnp
from jax import lax
from jax.experimental import pallas as pl
from jax.experimental.pallas import tpu as pltpu
from jax.sharding import PartitionSpec as P

WID = 64
SUB = 16
F32 = jnp.float32
BF16 = jnp.bfloat16
VMEM_LIMIT = 24 * 1024 * 1024
TOKEN = (8, 128)
FEATURE_COST = 3 * 10**9


def from_behind(x, axis, by):
    size = lax.axis_size(axis)
    pairs = [(i, i + by) for i in range(size) if 0 <= i + by < size]
    return lax.ppermute(x, axis, pairs)


def padded_copies(block):
    pixels = block.shape[-1]
    column = lax.broadcasted_iota(jnp.int32, (pixels,), 0) % WID
    nothing = jnp.zeros((), block.dtype)
    widths = [(0, 0), (0, 0), (0, 0), (WID + 1, WID + 1)]
    left_cut = jnp.pad(jnp.where(column == WID - 1, nothing, block), widths)
    untouched = jnp.pad(block, widths)
    right_cut = jnp.pad(jnp.where(column == 0, nothing, block), widths)
    return (left_cut, untouched, right_cut)


def tap_window(copies, first_frame, vertical, horizontal, frames, pixels):
    source = copies[horizontal]
    offset = vertical * WID + horizontal
    return source[:, :, first_frame : first_frame + frames, offset : offset + pixels]


def stacked_taps(copies, first_frame, flipped, frames, pixels):
    pieces = []
    for vertical in range(3):
        for horizontal in range(3):
            if flipped:
                pieces.append(
                    tap_window(copies, first_frame, 2 - vertical, 2 - horizontal, frames, pixels)
                )
            else:
                pieces.append(tap_window(copies, first_frame, vertical, horizontal, frames, pixels))
    concatenated = jnp.concatenate(pieces, axis=0)
    return concatenated.reshape(concatenated.shape[0], -1)


def local_generic(features, kernel, cotangent):
    channels, clip_count, frames, pixels = features.shape
    flat_length = clip_count * frames * pixels
    widened = features.astype(F32)
    logistic = jax.nn.sigmoid(widened)
    activation = (widened * logistic).astype(BF16)
    slope_factor = logistic * (1.0 + widened * (1.0 - logistic))
    earlier = from_behind(activation[:, :, frames - 2 :, :], "tm", 1)
    extended = jnp.concatenate([earlier, activation], axis=2)
    upcoming = from_behind(cotangent[:, :, :2, :], "tm", -1)
    later_padded = jnp.concatenate([cotangent, upcoming], axis=2)
    cotangent_rows = cotangent.reshape(channels, -1)
    portion = lax.all_gather(extended, "chan", axis=0, tiled=True)
    out_sum = jnp.zeros((channels, flat_length), F32)
    amount = portion.shape[0]
    copies = padded_copies(portion)
    grad_parts = []
    for temporal in range(3):
        stacked = stacked_taps(copies, temporal, False, frames, pixels)
        weights = kernel[:, 9 * temporal : 9 * temporal + 9, :].reshape(channels, 9 * amount)
        out_sum = out_sum + jnp.dot(weights, stacked, preferred_element_type=F32)
        grad_parts.append(
            lax.dot_general(
                cotangent_rows, stacked, (((1,), (1,)), ((), ())), preferred_element_type=F32
            ).reshape(channels, 9, amount)
        )
    grad_sum = jnp.concatenate(grad_parts, axis=1)
    conv_out = out_sum.reshape(features.shape).astype(BF16)
    position_count = lax.axis_size("dp") * lax.axis_size("tm") * flat_length
    kernel_grad = lax.psum(grad_sum, ("tm", "dp")) * (1.0 / math.sqrt(position_count))
    padded_later = padded_copies(later_padded)
    summed = jnp.zeros((amount, flat_length), F32)
    for temporal in range(3):
        weights = jnp.transpose(
            kernel[:, 9 * temporal : 9 * temporal + 9, :], (2, 1, 0)
        ).reshape(amount, 9 * channels)
        stacked = stacked_taps(padded_later, 2 - temporal, True, frames, pixels)
        summed = summed + jnp.dot(weights, stacked, preferred_element_type=F32)
    before_slope = lax.psum_scatter(
        summed.reshape(amount, clip_count, frames, pixels), "chan", scatter_dimension=0, tiled=True
    )
    feature_grad = (before_slope * slope_factor).astype(BF16)
    return (conv_out, feature_grad, kernel_grad)


def rotate(x, axis, by):
    size = lax.axis_size(axis)
    return lax.ppermute(x, axis, [(i, (i + by) % size) for i in range(size)])


def shifted(frame, down, right):
    pixels = frame.shape[-1]
    if down == 0 and right == 0:
        return frame
    cell = lax.broadcasted_iota(jnp.int32, (1, pixels), 1)
    row, column = cell // WID + down, cell % WID + right
    inside = (row >= 0) & (row < pixels // WID) & (column >= 0) & (column < WID)
    moved = pltpu.roll(frame, (-(down * WID + right)) % pixels, 1)
    return jnp.where(inside, moved, 0.0)


def after(x, *others):
    anywhere = pl.BlockSpec(memory_space=pl.ANY)
    return pl.pallas_call(
        lambda *refs: None,
        out_shape=jax.ShapeDtypeStruct(x.shape, x.dtype),
        in_specs=[anywhere] * (1 + len(others)),
        out_specs=anywhere,
        input_output_aliases={0: 0},
        compiler_params=pltpu.CompilerParams(vmem_limit_bytes=1024 * 1024),
        cost_estimate=cost(),
        name="hand_on",
    )(x, *others)


def run(kernel, args, waits=(), **options):
    options.setdefault("in_specs", [whole()] * len(args))
    options.setdefault("cost_estimate", cost())
    options["in_specs"] = list(options["in_specs"]) + [
        pl.BlockSpec(memory_space=pl.ANY) for _ in waits
    ]
    count = len(args)

    def body(*refs):
        kernel(*refs[:count], *refs[count + len(waits) :])

    return pl.pallas_call(
        body, compiler_params=pltpu.CompilerParams(vmem_limit_bytes=VMEM_LIMIT), **options
    )(*args, *waits)


def cost(flops=1):
    return pl.CostEstimate(flops=flops, bytes_accessed=1, transcendentals=0)


def whole():
    return pl.BlockSpec(memory_space=pltpu.VMEM)


def activate_kernel(features, cotangent, activation, flat, feat, cot, sems):
    loads = [
        pltpu.make_async_copy(source, target, sems.at[n])
        for n, (source, target) in enumerate(((features, feat), (cotangent, cot)))
    ]
    for load in loads:
        load.start()
    frames, pixels = feat.shape[2:]
    loads[0].wait()
    v = feat[:, 0].astype(F32)
    act = v / (1.0 + jnp.exp(-v))
    for t in range(frames):
        activation[:, t * pixels : (t + 1) * pixels] = act[:, t, :].astype(BF16)
    loads[1].wait()
    flatten(pixels, cot, flat, 0)


def flatten(pixels, source, flat, first):
    wide = source[:, 0].astype(F32)
    for t in range(wide.shape[1]):
        at = (first + t) * pixels
        at = at if isinstance(at, int) else pl.multiple_of(at, pixels)
        flat[:, pl.ds(at, pixels)] = wide[:, t, :]


def shard_at(count, k):
    z = lax.axis_index("chan")
    return (z, z + 1 - 2 * lax.rem(z, 2), lax.rem(z + 2, count), count - 1 - z)[k]


def in_slot(channels, rows, slot):
    lane = lax.broadcasted_iota(jnp.int32, (1, channels), 1)
    return (lane >= slot * rows) & (lane < (slot + 1) * rows)


def packed_rows(total):
    unit = total // 9
    return 7 * unit, 2 * unit


def fill_stack(pixels, flat, stack, which):
    rows = flat.shape[0]
    unit = rows // 2
    frames = flat.shape[1] // pixels
    for half in range(2):

        @pl.when(which == half)
        def _(half=half):
            for t in range(frames):
                at = slice(t * pixels, (t + 1) * pixels)
                for q in range(9):
                    tap, part = divmod(9 * half + q, 2)
                    i, j = divmod(tap, 3)
                    frame = flat[part * unit : (part + 1) * unit, at]
                    stack[q * unit : (q + 1) * unit, at] = shifted(frame, 1 - i, 1 - j).astype(BF16)


def block_terms(pixels, k, stack, here, there, out, rhs):
    channels = out.shape[1]
    rows, length = here.shape
    lanes, count = 2 * length, channels // rows
    shard = shard_at(count, k)
    for core in range(2):

        @pl.when(lax.axis_index("tm") == core)
        def _(first=(here, there)[core], second=(there, here)[core]):
            for a in range(3):
                skip = (2 - a) * pixels
                at = pl.ds(pl.multiple_of(lax.rem(shard + a, count) * rows, SUB), rows)
                if skip:
                    rhs[at, :skip] = jnp.zeros((rows, skip), BF16)
                rhs[at, skip : skip + length] = first[...]
                rhs[at, skip + length :] = second[:, : length - skip]

    last = lax.rem(shard + 3, count)
    rhs[pl.ds(pl.multiple_of(last * rows, SUB), rows), :] = jnp.zeros((rows, lanes), BF16)
    terms = lax.dot_general(
        stack[...], rhs[...], (((1,), (1,)), ((), ())), preferred_element_type=F32
    )
    main, tail = packed_rows(terms.shape[0])
    free = in_slot(channels, rows, last)
    for a in range(3):
        at = slice(a * tail, (a + 1) * tail)
        moved = pltpu.roll(terms[main:], (3 - a) * rows, 1)
        out[at, :] = jnp.where(free, moved, terms[at]).astype(BF16)
    out[3 * tail :, :] = terms[3 * tail : main].astype(BF16)


def own_terms_kernel(
    pixels, mine, other, flat_own, cot_other, weights, out, stack, flat, held, rhs, sems
):
    load = pltpu.make_async_copy(weights, held, sems.at[0])
    load.start()
    length = flat_own.shape[1]
    me = lax.axis_index("tm")
    flat[:, pl.ds(pl.multiple_of(me * length, pixels), length)] = flat_own[...]
    flatten(pixels, cot_other, flat, (1 - me) * (length // pixels))
    fill_stack(pixels, flat, stack, me)
    block_terms(pixels, 0, stack, mine, other, out, rhs)
    load.wait()


def terms_kernel(pixels, k, stack, here, there, out, rhs):
    block_terms(pixels, k, stack, here, there, out, rhs)


def share_kernel(pixels, weights, flat, own, kept, sent, stack, total):
    rows, length = own.shape
    frames = length // pixels
    count = weights.shape[1] // rows
    me = lax.axis_index("tm")
    for t in range(frames + 2):
        at = slice(t * pixels, (t + 1) * pixels)
        if t < frames:
            frame = flat[:, pl.ds(pl.multiple_of((me * frames + t) * pixels, pixels), pixels)]
        else:
            frame = jnp.where(me == 0, flat[:, at], 0.0)
        for i in range(3):
            for j in range(3):
                row = (3 * i + j) * rows
                stack[row : row + rows, at] = shifted(frame, 1 - i, 1 - j).astype(BF16)
    taps = 9 * rows
    acc = None
    for a in range(3):
        term = lax.dot_general(
            weights[a * taps : (a + 1) * taps, :],
            stack[:, (2 - a) * pixels : (2 - a) * pixels + length],
            (((0,), (0,)), ((), ())),
            preferred_element_type=F32,
        )
        acc = term if acc is None else acc + term
    total[...] = acc

    def part(k):
        return total[pl.ds(pl.multiple_of(shard_at(count, k) * rows, SUB), rows), :]

    own[...] = part(0)
    kept[...] = part(2)
    sent[0] = part(1).astype(BF16)
    sent[1] = part(3).astype(BF16)


def add_kernel(kept, came, out):
    out[...] = (kept[...] + came[1].astype(F32)).astype(out.dtype)


def conv_kernel(pixels, weights, *refs):
    blocks, (out, token, act) = refs[:-3], refs[-3:]
    token[...] = jnp.zeros(TOKEN, F32)
    rows, _, frames, _ = out.shape
    count = weights.shape[1] // rows
    length, front = frames * pixels, 2 * pixels
    me = lax.axis_index("tm")
    for k in range(count):
        here, there = blocks[2 * k], blocks[2 * k + 1]
        at = pl.ds(pl.multiple_of(shard_at(count, k) * rows, SUB), rows)
        earlier = there[:, length - front :]
        act[at, :front] = jnp.where(me == 0, jnp.zeros_like(earlier), earlier)
        act[at, front:] = here[...]

    taps = 9 * rows
    for t in range(frames):
        z_t = None
        for a in range(3):
            term = jnp.dot(
                weights[a * taps : (a + 1) * taps, :],
                act[:, (t + a) * pixels : (t + a + 1) * pixels],
                preferred_element_type=F32,
            )
            z_t = term if z_t is None else z_t + term
        acc = None
        for i in range(3):
            for j in range(3):
                at = (3 * i + j) * rows
                moved = shifted(z_t[at : at + rows, :], i - 1, j - 1)
                acc = moved if acc is None else acc + moved
        out[:, 0, t, :] = acc.astype(BF16)


def feature_kernel(pixels, features, own, first, second, out, token):
    token[...] = jnp.zeros(TOKEN, F32)
    frames = features.shape[2]
    total = own[...] + first[0].astype(F32) + second[...].astype(F32)
    v = features[:, 0].astype(F32)
    s = 1.0 / (1.0 + jnp.exp(-v))
    slope = s * (1.0 + v * (1.0 - s))
    for t in range(frames):
        piece = total[:, t * pixels : (t + 1) * pixels] * slope[:, t, :]
        out[:, 0, t, :] = piece.astype(BF16)


def sum_kernel(main, *refs):
    out, ins = refs[-1], refs[:-1]
    count = len(ins) // 2
    for k in range(count):
        total = ins[k][...].astype(F32) + ins[count + k][...].astype(F32)
        out[k * main : (k + 1) * main, :] = total.astype(BF16)


def finish_kernel(scale, main, whose, early, late, *refs):
    out, laid, sems = refs[-3:]
    channels = out.shape[2]
    first = early.shape[0] // main
    count = first + late.shape[0] // main
    rows, half = channels // count, out.shape[1] // 2
    unit = rows // 2
    which = lax.rem(lax.axis_index("tm") + whose, 2)
    at = pl.ds(pl.multiple_of(which * half, 8), half)
    shards = [shard_at(count, k) for k in range(count)]
    copies = []
    for a in range(3):
        for q in range(9):
            base = q * unit if q < 7 else a * 2 * unit + (q - 7) * unit
            step = a if q < 7 else 3
            total = None
            for k, shard in enumerate(shards):
                source, place = (early, k) if k < first else (late, k - first)
                piece = source[place * main + base : place * main + base + unit, :].astype(F32)
                mask = in_slot(channels, rows, lax.rem(shard + step, count))
                total = piece if total is None else jnp.where(mask, piece, total)
            total = total * scale
            if step:
                total = pltpu.roll(total, channels - step * rows, 1)
            laid[a, q * unit : (q + 1) * unit, :] = total
        copy = pltpu.make_async_copy(laid.at[a], out.at[a, at], sems.at[a])
        copy.start()
        copies.append(copy)
    for copy in copies:
        copy.wait()


def in_place(x):
    return pltpu.with_memory_space_constraint(x, pltpu.HBM)


def local_fast(features, kernel, cotangent):
    rows, _, frames, pixels = features.shape
    length = frames * pixels
    count = lax.axis_size("chan")
    channels = rows * count
    taps = kernel.shape[1]
    half = 9 * rows // 2
    main, _ = packed_rows(half)
    sds = jax.ShapeDtypeStruct
    block_shape = sds((rows, length), BF16)
    term_shape = sds((main, channels), BF16)
    stack_shape = sds((half, 2 * length), BF16)
    rhs = pltpu.VMEM((channels, 2 * length), BF16)

    def swap(x, far):
        return lax.ppermute(x, "chan", [(z, z ^ far) for z in range(count)])

    weights = jnp.transpose(kernel, (1, 0, 2)).reshape(taps * rows, channels)
    hbm = pl.BlockSpec(memory_space=pltpu.HBM)
    cot_other = rotate(cotangent, "tm", 1)
    activation, flat_own = run(
        activate_kernel,
        (in_place(features), in_place(cotangent)),
        in_specs=[hbm] * 2,
        out_shape=(block_shape, sds((rows, length), F32)),
        out_specs=(whole(),) * 2,
        scratch_shapes=[
            pltpu.VMEM(features.shape, BF16),
            pltpu.VMEM(features.shape, BF16),
            pltpu.SemaphoreType.DMA((2,)),
        ],
        name="activate",
    )
    other = rotate(activation, "tm", 1)
    near, far = swap(activation, 1), swap(activation, 2)
    own_term, stack, flat, weights = run(
        functools.partial(own_terms_kernel, pixels),
        (activation, other, flat_own, cot_other, in_place(weights)),
        in_specs=[whole()] * 4 + [hbm],
        out_shape=(
            term_shape,
            stack_shape,
            sds((rows, 2 * length), F32),
            sds(weights.shape, BF16),
        ),
        out_specs=(whole(),) * 4,
        scratch_shapes=[rhs, pltpu.SemaphoreType.DMA((1,))],
        name="own_terms",
    )
    terms, got = [own_term], [rotate(own_term, "dp", 1)]
    blocks = [activation, other]

    def terms_of(k, here, waits=()):
        blocks.extend((here, rotate(here, "tm", 1)))
        term = run(
            functools.partial(terms_kernel, pixels, k),
            (stack, *blocks[-2:]),
            waits=waits,
            out_shape=term_shape,
            out_specs=whole(),
            scratch_shapes=[rhs],
            name=f"terms_{k}",
        )
        terms.append(term)
        got.append(rotate(term, "dp", 1))
        return term

    near = after(near, own_term)
    own_share, kept, sent = run(
        functools.partial(share_kernel, pixels),
        (weights, flat),
        waits=(near,),
        out_shape=(
            sds((rows, length), F32),
            sds((rows, length), F32),
            sds((2, rows, length), BF16),
        ),
        out_specs=(whole(),) * 3,
        scratch_shapes=[
            pltpu.VMEM((9 * rows, (frames + 2) * pixels), BF16),
            pltpu.VMEM((channels, length), F32),
        ],
        name="shares",
    )
    first_share = swap(sent, 1)
    term = terms_of(1, near, (own_share, got[0]))
    far = after(far, term)
    last = swap(far, 1)
    term = terms_of(2, far)
    carry = run(
        add_kernel,
        (kept, first_share),
        waits=(term,),
        out_shape=block_shape,
        out_specs=whole(),
        name="carry_share",
    )
    second_share = swap(carry, 2)
    term = terms_of(3, after(last, carry, got[1]))

    def sums(first, stop, waits=()):
        return run(
            functools.partial(sum_kernel, main),
            (*terms[first:stop], *got[first:stop]),
            waits=waits,
            out_shape=sds(((stop - first) * main, channels), BF16),
            out_specs=whole(),
            name=f"sums_{first}",
        )

    conv_out, token = run(
        functools.partial(conv_kernel, pixels),
        (weights, *blocks),
        waits=(term, got[2]),
        out_shape=(sds(features.shape, BF16), sds(TOKEN, F32)),
        out_specs=(whole(),) * 2,
        scratch_shapes=[pltpu.VMEM((channels, (frames + 2) * pixels), BF16)],
        name="conv",
    )
    early = sums(0, 2)
    feature_grad, token = run(
        functools.partial(feature_kernel, pixels),
        (features, own_share, first_share, second_share),
        waits=(token, early),
        out_shape=(sds(features.shape, BF16), sds(TOKEN, F32)),
        out_specs=(whole(),) * 2,
        cost_estimate=cost(FEATURE_COST),
        name="feature_grad",
    )
    late = sums(2, count, (token,))
    scale = 1.0 / math.sqrt(lax.axis_size("dp") * lax.axis_size("tm") * length)

    def finish(whose, sums, base=()):
        anywhere = pl.BlockSpec(memory_space=pl.ANY)
        return run(
            functools.partial(finish_kernel, scale, main, whose),
            (*sums, *base),
            in_specs=[whole()] * 2 + [anywhere] * len(base),
            out_shape=sds((3, 9 * rows, channels), F32),
            out_specs=anywhere,
            input_output_aliases={2: 0} if base else {},
            scratch_shapes=[pltpu.VMEM((3, half, channels), F32), pltpu.SemaphoreType.DMA((3,))],
            name=f"kernel_grad_{whose}",
        )

    kernel_grad = finish(0, (early, late))
    kernel_grad = finish(1, (rotate(early, "tm", 1), rotate(late, "tm", 1)), (kernel_grad,))
    kernel_grad = jnp.transpose(kernel_grad.reshape(taps, rows, channels), (1, 0, 2))
    return (conv_out, feature_grad, kernel_grad)


def local(features, kernel, cotangent):
    rows, clips, _, pixels = features.shape
    fits = (
        clips == 1
        and lax.axis_size("tm") == 2
        and lax.axis_size("dp") == 2
        and rows % (2 * SUB) == 0
        and pixels % 128 == 0
        and kernel.shape[1] == 27
        and lax.axis_size("chan") == 4
    )
    return (local_fast if fits else local_generic)(features, kernel, cotangent)


def solution(mesh):
    return jax.shard_map(
        local,
        mesh=mesh,
        in_specs=(
            P("chan", ("groups", "dp"), "tm", None),
            P("chan", None, None),
            P("chan", ("groups", "dp"), "tm", None),
        ),
        out_specs=(
            P("chan", ("groups", "dp"), "tm", None),
            P("chan", ("groups", "dp"), "tm", None),
            P(("groups", "chan"), None, None),
        ),
        check_vma=False,
    )
```

```python
import functools
import math

import jax
import jax.numpy as jnp
from jax import lax
from jax.experimental import pallas as pl
from jax.experimental.pallas import tpu as pltpu
from jax.sharding import PartitionSpec as P

WID = 64
SUB = 16
F32 = jnp.float32
BF16 = jnp.bfloat16
VMEM_LIMIT = 24 * 1024 * 1024
TOKEN = (8, 128)
FEATURE_COST = 3 * 10**9
FAR_COST = 2 * 10**9


def from_behind(x, axis, by):
    size = lax.axis_size(axis)
    pairs = [(i, i + by) for i in range(size) if 0 <= i + by < size]
    return lax.ppermute(x, axis, pairs)


def padded_copies(block):
    pixels = block.shape[-1]
    column = lax.broadcasted_iota(jnp.int32, (pixels,), 0) % WID
    nothing = jnp.zeros((), block.dtype)
    widths = [(0, 0), (0, 0), (0, 0), (WID + 1, WID + 1)]
    left_cut = jnp.pad(jnp.where(column == WID - 1, nothing, block), widths)
    untouched = jnp.pad(block, widths)
    right_cut = jnp.pad(jnp.where(column == 0, nothing, block), widths)
    return (left_cut, untouched, right_cut)


def tap_window(copies, first_frame, vertical, horizontal, frames, pixels):
    source = copies[horizontal]
    offset = vertical * WID + horizontal
    return source[:, :, first_frame : first_frame + frames, offset : offset + pixels]


def stacked_taps(copies, first_frame, flipped, frames, pixels):
    pieces = []
    for vertical in range(3):
        for horizontal in range(3):
            if flipped:
                pieces.append(
                    tap_window(copies, first_frame, 2 - vertical, 2 - horizontal, frames, pixels)
                )
            else:
                pieces.append(tap_window(copies, first_frame, vertical, horizontal, frames, pixels))
    concatenated = jnp.concatenate(pieces, axis=0)
    return concatenated.reshape(concatenated.shape[0], -1)


def local_generic(features, kernel, cotangent):
    channels, clip_count, frames, pixels = features.shape
    flat_length = clip_count * frames * pixels
    widened = features.astype(F32)
    logistic = jax.nn.sigmoid(widened)
    activation = (widened * logistic).astype(BF16)
    slope_factor = logistic * (1.0 + widened * (1.0 - logistic))
    earlier = from_behind(activation[:, :, frames - 2 :, :], "tm", 1)
    extended = jnp.concatenate([earlier, activation], axis=2)
    upcoming = from_behind(cotangent[:, :, :2, :], "tm", -1)
    later_padded = jnp.concatenate([cotangent, upcoming], axis=2)
    cotangent_rows = cotangent.reshape(channels, -1)
    portion = lax.all_gather(extended, "chan", axis=0, tiled=True)
    out_sum = jnp.zeros((channels, flat_length), F32)
    amount = portion.shape[0]
    copies = padded_copies(portion)
    grad_parts = []
    for temporal in range(3):
        stacked = stacked_taps(copies, temporal, False, frames, pixels)
        weights = kernel[:, 9 * temporal : 9 * temporal + 9, :].reshape(channels, 9 * amount)
        out_sum = out_sum + jnp.dot(weights, stacked, preferred_element_type=F32)
        grad_parts.append(
            lax.dot_general(
                cotangent_rows, stacked, (((1,), (1,)), ((), ())), preferred_element_type=F32
            ).reshape(channels, 9, amount)
        )
    grad_sum = jnp.concatenate(grad_parts, axis=1)
    conv_out = out_sum.reshape(features.shape).astype(BF16)
    position_count = lax.axis_size("dp") * lax.axis_size("tm") * flat_length
    kernel_grad = lax.psum(grad_sum, ("tm", "dp")) * (1.0 / math.sqrt(position_count))
    padded_later = padded_copies(later_padded)
    summed = jnp.zeros((amount, flat_length), F32)
    for temporal in range(3):
        weights = jnp.transpose(
            kernel[:, 9 * temporal : 9 * temporal + 9, :], (2, 1, 0)
        ).reshape(amount, 9 * channels)
        stacked = stacked_taps(padded_later, 2 - temporal, True, frames, pixels)
        summed = summed + jnp.dot(weights, stacked, preferred_element_type=F32)
    before_slope = lax.psum_scatter(
        summed.reshape(amount, clip_count, frames, pixels), "chan", scatter_dimension=0, tiled=True
    )
    feature_grad = (before_slope * slope_factor).astype(BF16)
    return (conv_out, feature_grad, kernel_grad)


def rotate(x, axis, by):
    size = lax.axis_size(axis)
    return lax.ppermute(x, axis, [(i, (i + by) % size) for i in range(size)])


def shifted(frame, down, right):
    pixels = frame.shape[-1]
    if down == 0 and right == 0:
        return frame
    cell = lax.broadcasted_iota(jnp.int32, (1, pixels), 1)
    row, column = cell // WID + down, cell % WID + right
    inside = (row >= 0) & (row < pixels // WID) & (column >= 0) & (column < WID)
    moved = pltpu.roll(frame, (-(down * WID + right)) % pixels, 1)
    return jnp.where(inside, moved, 0.0)


def after(x, *others, flops=1):
    anywhere = pl.BlockSpec(memory_space=pl.ANY)
    return pl.pallas_call(
        lambda *refs: None,
        out_shape=jax.ShapeDtypeStruct(x.shape, x.dtype),
        in_specs=[anywhere] * (1 + len(others)),
        out_specs=anywhere,
        input_output_aliases={0: 0},
        compiler_params=pltpu.CompilerParams(vmem_limit_bytes=1024 * 1024),
        cost_estimate=cost(flops),
        name="hand_on",
    )(x, *others)


def run(kernel, args, waits=(), **options):
    options.setdefault("in_specs", [whole()] * len(args))
    options.setdefault("cost_estimate", cost())
    options["in_specs"] = list(options["in_specs"]) + [
        pl.BlockSpec(memory_space=pl.ANY) for _ in waits
    ]
    count = len(args)

    def body(*refs):
        kernel(*refs[:count], *refs[count + len(waits) :])

    return pl.pallas_call(
        body, compiler_params=pltpu.CompilerParams(vmem_limit_bytes=VMEM_LIMIT), **options
    )(*args, *waits)


def cost(flops=1):
    return pl.CostEstimate(flops=flops, bytes_accessed=1, transcendentals=0)


def whole():
    return pl.BlockSpec(memory_space=pltpu.VMEM)


def activate_kernel(features, cotangent, activation, flat, feat, cot, sems):
    loads = [
        pltpu.make_async_copy(source, target, sems.at[n])
        for n, (source, target) in enumerate(((features, feat), (cotangent, cot)))
    ]
    for load in loads:
        load.start()
    frames, pixels = feat.shape[2:]
    loads[0].wait()
    v = feat[:, 0].astype(F32)
    act = v / (1.0 + jnp.exp(-v))
    for t in range(frames):
        activation[:, t * pixels : (t + 1) * pixels] = act[:, t, :].astype(BF16)
    loads[1].wait()
    flatten(pixels, cot, flat, 0)


def flatten(pixels, source, flat, first):
    wide = source[:, 0].astype(F32)
    for t in range(wide.shape[1]):
        at = (first + t) * pixels
        at = at if isinstance(at, int) else pl.multiple_of(at, pixels)
        flat[:, pl.ds(at, pixels)] = wide[:, t, :]


def shard_at(count, k):
    z = lax.axis_index("chan")
    return (z, z + 1 - 2 * lax.rem(z, 2), lax.rem(z + 2, count), count - 1 - z)[k]


def in_slot(channels, rows, slot):
    lane = lax.broadcasted_iota(jnp.int32, (1, channels), 1)
    return (lane >= slot * rows) & (lane < (slot + 1) * rows)


def packed_rows(total):
    unit = total // 9
    return 7 * unit, 2 * unit


def fill_stack(pixels, flat, stack, which):
    rows = flat.shape[0]
    unit = rows // 2
    frames = flat.shape[1] // pixels
    for half in range(2):

        @pl.when(which == half)
        def _(half=half):
            for t in range(frames):
                at = slice(t * pixels, (t + 1) * pixels)
                for q in range(9):
                    tap, part = divmod(9 * half + q, 2)
                    i, j = divmod(tap, 3)
                    frame = flat[part * unit : (part + 1) * unit, at]
                    stack[q * unit : (q + 1) * unit, at] = shifted(frame, 1 - i, 1 - j).astype(BF16)


def block_terms(pixels, k, stack, here, there, out, rhs):
    channels = out.shape[1]
    rows, length = here.shape
    lanes, count = 2 * length, channels // rows
    shard = shard_at(count, k)
    for core in range(2):

        @pl.when(lax.axis_index("tm") == core)
        def _(first=(here, there)[core], second=(there, here)[core]):
            for a in range(3):
                skip = (2 - a) * pixels
                at = pl.ds(pl.multiple_of(lax.rem(shard + a, count) * rows, SUB), rows)
                if skip:
                    rhs[at, :skip] = jnp.zeros((rows, skip), BF16)
                rhs[at, skip : skip + length] = first[...]
                rhs[at, skip + length :] = second[:, : length - skip]

    last = lax.rem(shard + 3, count)
    rhs[pl.ds(pl.multiple_of(last * rows, SUB), rows), :] = jnp.zeros((rows, lanes), BF16)
    terms = lax.dot_general(
        stack[...], rhs[...], (((1,), (1,)), ((), ())), preferred_element_type=F32
    )
    main, tail = packed_rows(terms.shape[0])
    free = in_slot(channels, rows, last)
    for a in range(3):
        at = slice(a * tail, (a + 1) * tail)
        moved = pltpu.roll(terms[main:], (3 - a) * rows, 1)
        out[at, :] = jnp.where(free, moved, terms[at]).astype(BF16)
    out[3 * tail :, :] = terms[3 * tail : main].astype(BF16)


def own_terms_kernel(
    pixels, mine, other, flat_own, cot_other, weights, out, stack, flat, held, rhs, sems
):
    load = pltpu.make_async_copy(weights, held, sems.at[0])
    load.start()
    length = flat_own.shape[1]
    me = lax.axis_index("tm")
    flat[:, pl.ds(pl.multiple_of(me * length, pixels), length)] = flat_own[...]
    flatten(pixels, cot_other, flat, (1 - me) * (length // pixels))
    fill_stack(pixels, flat, stack, me)
    block_terms(pixels, 0, stack, mine, other, out, rhs)
    load.wait()


def terms_kernel(pixels, k, stack, here, there, out, rhs):
    block_terms(pixels, k, stack, here, there, out, rhs)


def share_kernel(pixels, weights, flat, own, kept, sent, stack, total):
    rows, length = own.shape
    frames = length // pixels
    count = weights.shape[1] // rows
    me = lax.axis_index("tm")
    for t in range(frames + 2):
        at = slice(t * pixels, (t + 1) * pixels)
        if t < frames:
            frame = flat[:, pl.ds(pl.multiple_of((me * frames + t) * pixels, pixels), pixels)]
        else:
            frame = jnp.where(me == 0, flat[:, at], 0.0)
        for i in range(3):
            for j in range(3):
                row = (3 * i + j) * rows
                stack[row : row + rows, at] = shifted(frame, 1 - i, 1 - j).astype(BF16)
    taps = 9 * rows
    acc = None
    for a in range(3):
        term = lax.dot_general(
            weights[a * taps : (a + 1) * taps, :],
            stack[:, (2 - a) * pixels : (2 - a) * pixels + length],
            (((0,), (0,)), ((), ())),
            preferred_element_type=F32,
        )
        acc = term if acc is None else acc + term
    total[...] = acc

    def part(k):
        return total[pl.ds(pl.multiple_of(shard_at(count, k) * rows, SUB), rows), :]

    own[...] = part(0)
    kept[...] = part(2)
    sent[0] = part(1).astype(BF16)
    sent[1] = part(3).astype(BF16)


def add_kernel(kept, came, out):
    out[...] = (kept[...] + came[1].astype(F32)).astype(out.dtype)


def conv_kernel(pixels, weights, *refs):
    blocks, (out, token, act) = refs[:-3], refs[-3:]
    token[...] = jnp.zeros(TOKEN, F32)
    rows, _, frames, _ = out.shape
    count = weights.shape[1] // rows
    length, front = frames * pixels, 2 * pixels
    me = lax.axis_index("tm")
    for k in range(count):
        here, there = blocks[2 * k], blocks[2 * k + 1]
        at = pl.ds(pl.multiple_of(shard_at(count, k) * rows, SUB), rows)
        earlier = there[:, length - front :]
        act[at, :front] = jnp.where(me == 0, jnp.zeros_like(earlier), earlier)
        act[at, front:] = here[...]

    taps = 9 * rows
    for t in range(frames):
        z_t = None
        for a in range(3):
            term = jnp.dot(
                weights[a * taps : (a + 1) * taps, :],
                act[:, (t + a) * pixels : (t + a + 1) * pixels],
                preferred_element_type=F32,
            )
            z_t = term if z_t is None else z_t + term
        acc = None
        for i in range(3):
            for j in range(3):
                at = (3 * i + j) * rows
                moved = shifted(z_t[at : at + rows, :], i - 1, j - 1)
                acc = moved if acc is None else acc + moved
        out[:, 0, t, :] = acc.astype(BF16)


def feature_kernel(pixels, features, own, first, second, out, token):
    token[...] = jnp.zeros(TOKEN, F32)
    frames = features.shape[2]
    total = own[...] + first[0].astype(F32) + second[...].astype(F32)
    v = features[:, 0].astype(F32)
    s = 1.0 / (1.0 + jnp.exp(-v))
    slope = s * (1.0 + v * (1.0 - s))
    for t in range(frames):
        piece = total[:, t * pixels : (t + 1) * pixels] * slope[:, t, :]
        out[:, 0, t, :] = piece.astype(BF16)


def sum_kernel(main, *refs):
    out, ins = refs[-1], refs[:-1]
    count = len(ins) // 2
    for k in range(count):
        total = ins[k][...].astype(F32) + ins[count + k][...].astype(F32)
        out[k * main : (k + 1) * main, :] = total.astype(BF16)


def finish_kernel(scale, main, whose, early, late, *refs):
    out, laid, sems = refs[-3:]
    channels = out.shape[2]
    first = early.shape[0] // main
    count = first + late.shape[0] // main
    rows, half = channels // count, out.shape[1] // 2
    unit = rows // 2
    which = lax.rem(lax.axis_index("tm") + whose, 2)
    at = pl.ds(pl.multiple_of(which * half, 8), half)
    shards = [shard_at(count, k) for k in range(count)]
    copies = []
    for a in range(3):
        for q in range(9):
            base = q * unit if q < 7 else a * 2 * unit + (q - 7) * unit
            step = a if q < 7 else 3
            total = None
            for k, shard in enumerate(shards):
                source, place = (early, k) if k < first else (late, k - first)
                piece = source[place * main + base : place * main + base + unit, :].astype(F32)
                mask = in_slot(channels, rows, lax.rem(shard + step, count))
                total = piece if total is None else jnp.where(mask, piece, total)
            total = total * scale
            if step:
                total = pltpu.roll(total, channels - step * rows, 1)
            laid[a, q * unit : (q + 1) * unit, :] = total
        copy = pltpu.make_async_copy(laid.at[a], out.at[a, at], sems.at[a])
        copy.start()
        copies.append(copy)
    for copy in copies:
        copy.wait()


def in_place(x):
    return pltpu.with_memory_space_constraint(x, pltpu.HBM)


def local_fast(features, kernel, cotangent):
    rows, _, frames, pixels = features.shape
    length = frames * pixels
    count = lax.axis_size("chan")
    channels = rows * count
    taps = kernel.shape[1]
    half = 9 * rows // 2
    main, _ = packed_rows(half)
    sds = jax.ShapeDtypeStruct
    block_shape = sds((rows, length), BF16)
    term_shape = sds((main, channels), BF16)
    stack_shape = sds((half, 2 * length), BF16)
    rhs = pltpu.VMEM((channels, 2 * length), BF16)

    def swap(x, far):
        return lax.ppermute(x, "chan", [(z, z ^ far) for z in range(count)])

    weights = jnp.transpose(kernel, (1, 0, 2)).reshape(taps * rows, channels)
    hbm = pl.BlockSpec(memory_space=pltpu.HBM)
    cot_other = rotate(cotangent, "tm", 1)
    activation, flat_own = run(
        activate_kernel,
        (in_place(features), in_place(cotangent)),
        in_specs=[hbm] * 2,
        out_shape=(block_shape, sds((rows, length), F32)),
        out_specs=(whole(),) * 2,
        scratch_shapes=[
            pltpu.VMEM(features.shape, BF16),
            pltpu.VMEM(features.shape, BF16),
            pltpu.SemaphoreType.DMA((2,)),
        ],
        name="activate",
    )
    other = rotate(activation, "tm", 1)
    near, far = swap(activation, 1), swap(activation, 2)
    own_term, stack, flat, weights = run(
        functools.partial(own_terms_kernel, pixels),
        (activation, other, flat_own, cot_other, in_place(weights)),
        in_specs=[whole()] * 4 + [hbm],
        out_shape=(
            term_shape,
            stack_shape,
            sds((rows, 2 * length), F32),
            sds(weights.shape, BF16),
        ),
        out_specs=(whole(),) * 4,
        scratch_shapes=[rhs, pltpu.SemaphoreType.DMA((1,))],
        name="own_terms",
    )
    terms, got = [own_term], [rotate(own_term, "dp", 1)]
    blocks = [activation, other]

    def terms_of(k, here, waits=()):
        blocks.extend((here, rotate(here, "tm", 1)))
        term = run(
            functools.partial(terms_kernel, pixels, k),
            (stack, *blocks[-2:]),
            waits=waits,
            out_shape=term_shape,
            out_specs=whole(),
            scratch_shapes=[rhs],
            name=f"terms_{k}",
        )
        terms.append(term)
        got.append(rotate(term, "dp", 1))
        return term

    near = after(near, own_term)
    own_share, kept, sent = run(
        functools.partial(share_kernel, pixels),
        (weights, flat),
        waits=(near,),
        out_shape=(
            sds((rows, length), F32),
            sds((rows, length), F32),
            sds((2, rows, length), BF16),
        ),
        out_specs=(whole(),) * 3,
        scratch_shapes=[
            pltpu.VMEM((9 * rows, (frames + 2) * pixels), BF16),
            pltpu.VMEM((channels, length), F32),
        ],
        name="shares",
    )
    first_share = swap(sent, 1)
    far = after(far, own_share, flops=FAR_COST)
    last = swap(far, 1)
    term = terms_of(1, near, (far, got[0]))
    term = terms_of(2, far, (term,))
    carry = run(
        add_kernel,
        (kept, first_share),
        waits=(term,),
        out_shape=block_shape,
        out_specs=whole(),
        name="carry_share",
    )
    second_share = swap(carry, 2)
    term = terms_of(3, after(last, carry, got[1]))

    def sums(first, stop, waits=()):
        return run(
            functools.partial(sum_kernel, main),
            (*terms[first:stop], *got[first:stop]),
            waits=waits,
            out_shape=sds(((stop - first) * main, channels), BF16),
            out_specs=whole(),
            name=f"sums_{first}",
        )

    conv_out, token = run(
        functools.partial(conv_kernel, pixels),
        (weights, *blocks),
        waits=(term, got[2]),
        out_shape=(sds(features.shape, BF16), sds(TOKEN, F32)),
        out_specs=(whole(),) * 2,
        scratch_shapes=[pltpu.VMEM((channels, (frames + 2) * pixels), BF16)],
        name="conv",
    )
    early = sums(0, 2)
    feature_grad, token = run(
        functools.partial(feature_kernel, pixels),
        (features, own_share, first_share, second_share),
        waits=(token, early),
        out_shape=(sds(features.shape, BF16), sds(TOKEN, F32)),
        out_specs=(whole(),) * 2,
        cost_estimate=cost(FEATURE_COST),
        name="feature_grad",
    )
    late = sums(2, count, (token,))
    scale = 1.0 / math.sqrt(lax.axis_size("dp") * lax.axis_size("tm") * length)

    def finish(whose, sums, base=()):
        anywhere = pl.BlockSpec(memory_space=pl.ANY)
        return run(
            functools.partial(finish_kernel, scale, main, whose),
            (*sums, *base),
            in_specs=[whole()] * 2 + [anywhere] * len(base),
            out_shape=sds((3, 9 * rows, channels), F32),
            out_specs=anywhere,
            input_output_aliases={2: 0} if base else {},
            scratch_shapes=[pltpu.VMEM((3, half, channels), F32), pltpu.SemaphoreType.DMA((3,))],
            name=f"kernel_grad_{whose}",
        )

    kernel_grad = finish(0, (early, late))
    kernel_grad = finish(1, (rotate(early, "tm", 1), rotate(late, "tm", 1)), (kernel_grad,))
    kernel_grad = jnp.transpose(kernel_grad.reshape(taps, rows, channels), (1, 0, 2))
    return (conv_out, feature_grad, kernel_grad)


def local(features, kernel, cotangent):
    rows, clips, _, pixels = features.shape
    fits = (
        clips == 1
        and lax.axis_size("tm") == 2
        and lax.axis_size("dp") == 2
        and rows % (2 * SUB) == 0
        and pixels % 128 == 0
        and kernel.shape[1] == 27
        and lax.axis_size("chan") == 4
    )
    return (local_fast if fits else local_generic)(features, kernel, cotangent)


def solution(mesh):
    return jax.shard_map(
        local,
        mesh=mesh,
        in_specs=(
            P("chan", ("groups", "dp"), "tm", None),
            P("chan", None, None),
            P("chan", ("groups", "dp"), "tm", None),
        ),
        out_specs=(
            P("chan", ("groups", "dp"), "tm", None),
            P("chan", ("groups", "dp"), "tm", None),
            P(("groups", "chan"), None, None),
        ),
        check_vma=False,
    )
```

```python
import functools
import math

import jax
import jax.numpy as jnp
from jax import lax
from jax.experimental import pallas as pl
from jax.experimental.pallas import tpu as pltpu
from jax.sharding import PartitionSpec as P

WID = 64
SUB = 16
F32 = jnp.float32
BF16 = jnp.bfloat16
VMEM_LIMIT = 24 * 1024 * 1024
TOKEN = (8, 128)
FEATURE_COST = 3 * 10**9
FAR_COST = 3 * 10**8
NEAR_COST = 10**9


def from_behind(x, axis, by):
    size = lax.axis_size(axis)
    pairs = [(i, i + by) for i in range(size) if 0 <= i + by < size]
    return lax.ppermute(x, axis, pairs)


def padded_copies(block):
    pixels = block.shape[-1]
    column = lax.broadcasted_iota(jnp.int32, (pixels,), 0) % WID
    nothing = jnp.zeros((), block.dtype)
    widths = [(0, 0), (0, 0), (0, 0), (WID + 1, WID + 1)]
    left_cut = jnp.pad(jnp.where(column == WID - 1, nothing, block), widths)
    untouched = jnp.pad(block, widths)
    right_cut = jnp.pad(jnp.where(column == 0, nothing, block), widths)
    return (left_cut, untouched, right_cut)


def tap_window(copies, first_frame, vertical, horizontal, frames, pixels):
    source = copies[horizontal]
    offset = vertical * WID + horizontal
    return source[:, :, first_frame : first_frame + frames, offset : offset + pixels]


def stacked_taps(copies, first_frame, flipped, frames, pixels):
    pieces = []
    for vertical in range(3):
        for horizontal in range(3):
            if flipped:
                pieces.append(
                    tap_window(copies, first_frame, 2 - vertical, 2 - horizontal, frames, pixels)
                )
            else:
                pieces.append(tap_window(copies, first_frame, vertical, horizontal, frames, pixels))
    concatenated = jnp.concatenate(pieces, axis=0)
    return concatenated.reshape(concatenated.shape[0], -1)


def local_generic(features, kernel, cotangent):
    channels, clip_count, frames, pixels = features.shape
    flat_length = clip_count * frames * pixels
    widened = features.astype(F32)
    logistic = jax.nn.sigmoid(widened)
    activation = (widened * logistic).astype(BF16)
    slope_factor = logistic * (1.0 + widened * (1.0 - logistic))
    earlier = from_behind(activation[:, :, frames - 2 :, :], "tm", 1)
    extended = jnp.concatenate([earlier, activation], axis=2)
    upcoming = from_behind(cotangent[:, :, :2, :], "tm", -1)
    later_padded = jnp.concatenate([cotangent, upcoming], axis=2)
    cotangent_rows = cotangent.reshape(channels, -1)
    portion = lax.all_gather(extended, "chan", axis=0, tiled=True)
    out_sum = jnp.zeros((channels, flat_length), F32)
    amount = portion.shape[0]
    copies = padded_copies(portion)
    grad_parts = []
    for temporal in range(3):
        stacked = stacked_taps(copies, temporal, False, frames, pixels)
        weights = kernel[:, 9 * temporal : 9 * temporal + 9, :].reshape(channels, 9 * amount)
        out_sum = out_sum + jnp.dot(weights, stacked, preferred_element_type=F32)
        grad_parts.append(
            lax.dot_general(
                cotangent_rows, stacked, (((1,), (1,)), ((), ())), preferred_element_type=F32
            ).reshape(channels, 9, amount)
        )
    grad_sum = jnp.concatenate(grad_parts, axis=1)
    conv_out = out_sum.reshape(features.shape).astype(BF16)
    position_count = lax.axis_size("dp") * lax.axis_size("tm") * flat_length
    kernel_grad = lax.psum(grad_sum, ("tm", "dp")) * (1.0 / math.sqrt(position_count))
    padded_later = padded_copies(later_padded)
    summed = jnp.zeros((amount, flat_length), F32)
    for temporal in range(3):
        weights = jnp.transpose(
            kernel[:, 9 * temporal : 9 * temporal + 9, :], (2, 1, 0)
        ).reshape(amount, 9 * channels)
        stacked = stacked_taps(padded_later, 2 - temporal, True, frames, pixels)
        summed = summed + jnp.dot(weights, stacked, preferred_element_type=F32)
    before_slope = lax.psum_scatter(
        summed.reshape(amount, clip_count, frames, pixels), "chan", scatter_dimension=0, tiled=True
    )
    feature_grad = (before_slope * slope_factor).astype(BF16)
    return (conv_out, feature_grad, kernel_grad)


def rotate(x, axis, by):
    size = lax.axis_size(axis)
    return lax.ppermute(x, axis, [(i, (i + by) % size) for i in range(size)])


def shifted(frame, down, right):
    pixels = frame.shape[-1]
    if down == 0 and right == 0:
        return frame
    cell = lax.broadcasted_iota(jnp.int32, (1, pixels), 1)
    row, column = cell // WID + down, cell % WID + right
    inside = (row >= 0) & (row < pixels // WID) & (column >= 0) & (column < WID)
    moved = pltpu.roll(frame, (-(down * WID + right)) % pixels, 1)
    return jnp.where(inside, moved, 0.0)


def after(x, *others, flops=1):
    anywhere = pl.BlockSpec(memory_space=pl.ANY)
    return pl.pallas_call(
        lambda *refs: None,
        out_shape=jax.ShapeDtypeStruct(x.shape, x.dtype),
        in_specs=[anywhere] * (1 + len(others)),
        out_specs=anywhere,
        input_output_aliases={0: 0},
        compiler_params=pltpu.CompilerParams(vmem_limit_bytes=1024 * 1024),
        cost_estimate=cost(flops),
        name="hand_on",
    )(x, *others)


def run(kernel, args, waits=(), **options):
    options.setdefault("in_specs", [whole()] * len(args))
    options.setdefault("cost_estimate", cost())
    options["in_specs"] = list(options["in_specs"]) + [
        pl.BlockSpec(memory_space=pl.ANY) for _ in waits
    ]
    count = len(args)

    def body(*refs):
        kernel(*refs[:count], *refs[count + len(waits) :])

    return pl.pallas_call(
        body, compiler_params=pltpu.CompilerParams(vmem_limit_bytes=VMEM_LIMIT), **options
    )(*args, *waits)


def cost(flops=1):
    return pl.CostEstimate(flops=flops, bytes_accessed=1, transcendentals=0)


def whole():
    return pl.BlockSpec(memory_space=pltpu.VMEM)


def activate_kernel(features, cotangent, activation, flat, feat, cot, sems):
    loads = [
        pltpu.make_async_copy(source, target, sems.at[n])
        for n, (source, target) in enumerate(((features, feat), (cotangent, cot)))
    ]
    for load in loads:
        load.start()
    frames, pixels = feat.shape[2:]
    loads[0].wait()
    v = feat[:, 0].astype(F32)
    act = v / (1.0 + jnp.exp(-v))
    for t in range(frames):
        activation[:, t * pixels : (t + 1) * pixels] = act[:, t, :].astype(BF16)
    loads[1].wait()
    flatten(pixels, cot, flat, 0)


def flatten(pixels, source, flat, first):
    wide = source[:, 0].astype(F32)
    for t in range(wide.shape[1]):
        at = (first + t) * pixels
        at = at if isinstance(at, int) else pl.multiple_of(at, pixels)
        flat[:, pl.ds(at, pixels)] = wide[:, t, :]


def shard_at(count, k):
    z = lax.axis_index("chan")
    return (z, z + 1 - 2 * lax.rem(z, 2), lax.rem(z + 2, count), count - 1 - z)[k]


def in_slot(channels, rows, slot):
    lane = lax.broadcasted_iota(jnp.int32, (1, channels), 1)
    return (lane >= slot * rows) & (lane < (slot + 1) * rows)


def packed_rows(total):
    unit = total // 9
    return 7 * unit, 2 * unit


def fill_stack(pixels, flat, stack, which):
    rows = flat.shape[0]
    unit = rows // 2
    frames = flat.shape[1] // pixels
    for half in range(2):

        @pl.when(which == half)
        def _(half=half):
            for t in range(frames):
                at = slice(t * pixels, (t + 1) * pixels)
                for q in range(9):
                    tap, part = divmod(9 * half + q, 2)
                    i, j = divmod(tap, 3)
                    frame = flat[part * unit : (part + 1) * unit, at]
                    stack[q * unit : (q + 1) * unit, at] = shifted(frame, 1 - i, 1 - j).astype(BF16)


def block_terms(pixels, k, stack, here, there, out, rhs):
    channels = out.shape[1]
    rows, length = here.shape
    lanes, count = 2 * length, channels // rows
    shard = shard_at(count, k)
    for core in range(2):

        @pl.when(lax.axis_index("tm") == core)
        def _(first=(here, there)[core], second=(there, here)[core]):
            for a in range(3):
                skip = (2 - a) * pixels
                at = pl.ds(pl.multiple_of(lax.rem(shard + a, count) * rows, SUB), rows)
                if skip:
                    rhs[at, :skip] = jnp.zeros((rows, skip), BF16)
                rhs[at, skip : skip + length] = first[...]
                rhs[at, skip + length :] = second[:, : length - skip]

    last = lax.rem(shard + 3, count)
    rhs[pl.ds(pl.multiple_of(last * rows, SUB), rows), :] = jnp.zeros((rows, lanes), BF16)
    terms = lax.dot_general(
        stack[...], rhs[...], (((1,), (1,)), ((), ())), preferred_element_type=F32
    )
    main, tail = packed_rows(terms.shape[0])
    free = in_slot(channels, rows, last)
    for a in range(3):
        at = slice(a * tail, (a + 1) * tail)
        moved = pltpu.roll(terms[main:], (3 - a) * rows, 1)
        out[at, :] = jnp.where(free, moved, terms[at]).astype(BF16)
    out[3 * tail :, :] = terms[3 * tail : main].astype(BF16)


def own_terms_kernel(
    pixels, mine, other, flat_own, cot_other, weights, out, stack, flat, held, rhs, sems
):
    load = pltpu.make_async_copy(weights, held, sems.at[0])
    load.start()
    length = flat_own.shape[1]
    me = lax.axis_index("tm")
    flat[:, pl.ds(pl.multiple_of(me * length, pixels), length)] = flat_own[...]
    flatten(pixels, cot_other, flat, (1 - me) * (length // pixels))
    fill_stack(pixels, flat, stack, me)
    block_terms(pixels, 0, stack, mine, other, out, rhs)
    load.wait()


def terms_kernel(pixels, k, stack, here, there, out, rhs):
    block_terms(pixels, k, stack, here, there, out, rhs)


def share_kernel(pixels, weights, flat, own, kept, sent, stack, total):
    rows, length = own.shape
    frames = length // pixels
    count = weights.shape[1] // rows
    me = lax.axis_index("tm")
    for t in range(frames + 2):
        at = slice(t * pixels, (t + 1) * pixels)
        if t < frames:
            frame = flat[:, pl.ds(pl.multiple_of((me * frames + t) * pixels, pixels), pixels)]
        else:
            frame = jnp.where(me == 0, flat[:, at], 0.0)
        for i in range(3):
            for j in range(3):
                row = (3 * i + j) * rows
                stack[row : row + rows, at] = shifted(frame, 1 - i, 1 - j).astype(BF16)
    taps = 9 * rows
    acc = None
    for a in range(3):
        term = lax.dot_general(
            weights[a * taps : (a + 1) * taps, :],
            stack[:, (2 - a) * pixels : (2 - a) * pixels + length],
            (((0,), (0,)), ((), ())),
            preferred_element_type=F32,
        )
        acc = term if acc is None else acc + term
    total[...] = acc

    def part(k):
        return total[pl.ds(pl.multiple_of(shard_at(count, k) * rows, SUB), rows), :]

    own[...] = part(0)
    kept[...] = part(2)
    sent[0] = part(1).astype(BF16)
    sent[1] = part(3).astype(BF16)


def split_kernel(block, out, first, second):
    out[...] = block[...]
    middle = block.shape[1] // 2
    first[...] = block[:, :middle]
    second[...] = block[:, middle:]


def join_kernel(first, second, out):
    middle = out.shape[1] // 2
    out[:, :middle] = first[...]
    out[:, middle:] = second[...]


def add_kernel(kept, came, out):
    out[...] = (kept[...] + came[1].astype(F32)).astype(out.dtype)


def conv_kernel(pixels, weights, *refs):
    blocks, (out, token, act) = refs[:-3], refs[-3:]
    token[...] = jnp.zeros(TOKEN, F32)
    rows, _, frames, _ = out.shape
    count = weights.shape[1] // rows
    length, front = frames * pixels, 2 * pixels
    me = lax.axis_index("tm")
    for k in range(count):
        here, there = blocks[2 * k], blocks[2 * k + 1]
        at = pl.ds(pl.multiple_of(shard_at(count, k) * rows, SUB), rows)
        earlier = there[:, length - front :]
        act[at, :front] = jnp.where(me == 0, jnp.zeros_like(earlier), earlier)
        act[at, front:] = here[...]

    taps = 9 * rows
    for t in range(frames):
        z_t = None
        for a in range(3):
            term = jnp.dot(
                weights[a * taps : (a + 1) * taps, :],
                act[:, (t + a) * pixels : (t + a + 1) * pixels],
                preferred_element_type=F32,
            )
            z_t = term if z_t is None else z_t + term
        acc = None
        for i in range(3):
            for j in range(3):
                at = (3 * i + j) * rows
                moved = shifted(z_t[at : at + rows, :], i - 1, j - 1)
                acc = moved if acc is None else acc + moved
        out[:, 0, t, :] = acc.astype(BF16)


def feature_kernel(pixels, features, own, first, second, out, token):
    token[...] = jnp.zeros(TOKEN, F32)
    frames = features.shape[2]
    total = own[...] + first[0].astype(F32) + second[...].astype(F32)
    v = features[:, 0].astype(F32)
    s = 1.0 / (1.0 + jnp.exp(-v))
    slope = s * (1.0 + v * (1.0 - s))
    for t in range(frames):
        piece = total[:, t * pixels : (t + 1) * pixels] * slope[:, t, :]
        out[:, 0, t, :] = piece.astype(BF16)


def sum_kernel(main, *refs):
    out, ins = refs[-1], refs[:-1]
    count = len(ins) // 2
    for k in range(count):
        total = ins[k][...].astype(F32) + ins[count + k][...].astype(F32)
        out[k * main : (k + 1) * main, :] = total.astype(BF16)


def finish_kernel(scale, main, whose, early, late, *refs):
    out, laid, sems = refs[-3:]
    channels = out.shape[2]
    first = early.shape[0] // main
    count = first + late.shape[0] // main
    rows, half = channels // count, out.shape[1] // 2
    unit = rows // 2
    which = lax.rem(lax.axis_index("tm") + whose, 2)
    at = pl.ds(pl.multiple_of(which * half, 8), half)
    shards = [shard_at(count, k) for k in range(count)]
    copies = []
    for a in range(3):
        for q in range(9):
            base = q * unit if q < 7 else a * 2 * unit + (q - 7) * unit
            step = a if q < 7 else 3
            total = None
            for k, shard in enumerate(shards):
                source, place = (early, k) if k < first else (late, k - first)
                piece = source[place * main + base : place * main + base + unit, :].astype(F32)
                mask = in_slot(channels, rows, lax.rem(shard + step, count))
                total = piece if total is None else jnp.where(mask, piece, total)
            total = total * scale
            if step:
                total = pltpu.roll(total, channels - step * rows, 1)
            laid[a, q * unit : (q + 1) * unit, :] = total
        copy = pltpu.make_async_copy(laid.at[a], out.at[a, at], sems.at[a])
        copy.start()
        copies.append(copy)
    for copy in copies:
        copy.wait()


def in_place(x):
    return pltpu.with_memory_space_constraint(x, pltpu.HBM)


def local_fast(features, kernel, cotangent):
    rows, _, frames, pixels = features.shape
    length = frames * pixels
    count = lax.axis_size("chan")
    channels = rows * count
    taps = kernel.shape[1]
    half = 9 * rows // 2
    main, _ = packed_rows(half)
    sds = jax.ShapeDtypeStruct
    block_shape = sds((rows, length), BF16)
    term_shape = sds((main, channels), BF16)
    stack_shape = sds((half, 2 * length), BF16)
    rhs = pltpu.VMEM((channels, 2 * length), BF16)

    def swap(x, far):
        return lax.ppermute(x, "chan", [(z, z ^ far) for z in range(count)])

    weights = jnp.transpose(kernel, (1, 0, 2)).reshape(taps * rows, channels)
    hbm = pl.BlockSpec(memory_space=pltpu.HBM)
    cot_other = rotate(cotangent, "tm", 1)
    activation, flat_own = run(
        activate_kernel,
        (in_place(features), in_place(cotangent)),
        in_specs=[hbm] * 2,
        out_shape=(block_shape, sds((rows, length), F32)),
        out_specs=(whole(),) * 2,
        scratch_shapes=[
            pltpu.VMEM(features.shape, BF16),
            pltpu.VMEM(features.shape, BF16),
            pltpu.SemaphoreType.DMA((2,)),
        ],
        name="activate",
    )
    other = rotate(activation, "tm", 1)
    near, far = swap(activation, 1), swap(activation, 2)
    own_term, stack, flat, weights = run(
        functools.partial(own_terms_kernel, pixels),
        (activation, other, flat_own, cot_other, in_place(weights)),
        in_specs=[whole()] * 4 + [hbm],
        out_shape=(
            term_shape,
            stack_shape,
            sds((rows, 2 * length), F32),
            sds(weights.shape, BF16),
        ),
        out_specs=(whole(),) * 4,
        scratch_shapes=[rhs, pltpu.SemaphoreType.DMA((1,))],
        name="own_terms",
    )
    terms, got = [own_term], [rotate(own_term, "dp", 1)]
    blocks = [activation, other]

    def terms_of(k, here, there, waits=()):
        blocks.extend((here, there))
        term = run(
            functools.partial(terms_kernel, pixels, k),
            (stack, *blocks[-2:]),
            waits=waits,
            out_shape=term_shape,
            out_specs=whole(),
            scratch_shapes=[rhs],
            name=f"terms_{k}",
        )
        terms.append(term)
        got.append(rotate(term, "dp", 1))
        return term

    own_share, kept, sent = run(
        functools.partial(share_kernel, pixels),
        (weights, flat),
        waits=(own_term,),
        out_shape=(
            sds((rows, length), F32),
            sds((rows, length), F32),
            sds((2, rows, length), BF16),
        ),
        out_specs=(whole(),) * 3,
        scratch_shapes=[
            pltpu.VMEM((9 * rows, (frames + 2) * pixels), BF16),
            pltpu.VMEM((channels, length), F32),
        ],
        name="shares",
    )
    first_share = swap(sent, 1)
    near = after(near, own_share, flops=NEAR_COST)
    far = after(far, own_share, flops=FAR_COST)
    last = swap(far, 1)
    term = terms_of(1, near, rotate(near, "tm", 1), (own_share, far, got[0]))
    term = terms_of(2, far, rotate(far, "tm", 1), (term,))
    carry = run(
        add_kernel,
        (kept, first_share),
        waits=(term,),
        out_shape=block_shape,
        out_specs=whole(),
        name="carry_share",
    )
    second_share = swap(carry, 2)
    last, *parts = run(
        split_kernel,
        (last,),
        waits=(carry, got[1]),
        out_shape=(block_shape,) + (sds((rows, length // 2), BF16),) * 2,
        out_specs=(whole(),) * 3,
        name="split",
    )
    last_other = run(
        join_kernel,
        [rotate(part, "tm", 1) for part in parts],
        out_shape=block_shape,
        out_specs=whole(),
        name="join",
    )
    term = terms_of(3, last, last_other)

    def sums(first, stop, waits=()):
        return run(
            functools.partial(sum_kernel, main),
            (*terms[first:stop], *got[first:stop]),
            waits=waits,
            out_shape=sds(((stop - first) * main, channels), BF16),
            out_specs=whole(),
            name=f"sums_{first}",
        )

    conv_out, token = run(
        functools.partial(conv_kernel, pixels),
        (weights, *blocks),
        waits=(term, got[2]),
        out_shape=(sds(features.shape, BF16), sds(TOKEN, F32)),
        out_specs=(whole(),) * 2,
        scratch_shapes=[pltpu.VMEM((channels, (frames + 2) * pixels), BF16)],
        name="conv",
    )
    early = sums(0, 2, (term,))
    feature_grad, token = run(
        functools.partial(feature_kernel, pixels),
        (features, own_share, first_share, second_share),
        waits=(token, early),
        out_shape=(sds(features.shape, BF16), sds(TOKEN, F32)),
        out_specs=(whole(),) * 2,
        cost_estimate=cost(FEATURE_COST),
        name="feature_grad",
    )
    late = sums(2, count, (token,))
    scale = 1.0 / math.sqrt(lax.axis_size("dp") * lax.axis_size("tm") * length)

    def finish(whose, sums, base=()):
        anywhere = pl.BlockSpec(memory_space=pl.ANY)
        return run(
            functools.partial(finish_kernel, scale, main, whose),
            (*sums, *base),
            in_specs=[whole()] * 2 + [anywhere] * len(base),
            out_shape=sds((3, 9 * rows, channels), F32),
            out_specs=anywhere,
            input_output_aliases={2: 0} if base else {},
            scratch_shapes=[pltpu.VMEM((3, half, channels), F32), pltpu.SemaphoreType.DMA((3,))],
            name=f"kernel_grad_{whose}",
        )

    kernel_grad = finish(0, (early, late))
    kernel_grad = finish(1, (rotate(early, "tm", 1), rotate(late, "tm", 1)), (kernel_grad,))
    kernel_grad = jnp.transpose(kernel_grad.reshape(taps, rows, channels), (1, 0, 2))
    return (conv_out, feature_grad, kernel_grad)


def local(features, kernel, cotangent):
    rows, clips, _, pixels = features.shape
    fits = (
        clips == 1
        and lax.axis_size("tm") == 2
        and lax.axis_size("dp") == 2
        and rows % (2 * SUB) == 0
        and pixels % 128 == 0
        and kernel.shape[1] == 27
        and lax.axis_size("chan") == 4
    )
    return (local_fast if fits else local_generic)(features, kernel, cotangent)


def solution(mesh):
    return jax.shard_map(
        local,
        mesh=mesh,
        in_specs=(
            P("chan", ("groups", "dp"), "tm", None),
            P("chan", None, None),
            P("chan", ("groups", "dp"), "tm", None),
        ),
        out_specs=(
            P("chan", ("groups", "dp"), "tm", None),
            P("chan", ("groups", "dp"), "tm", None),
            P(("groups", "chan"), None, None),
        ),
        check_vma=False,
    )
```

```python
import functools
import math

import jax
import jax.numpy as jnp
from jax import lax
from jax.experimental import pallas as pl
from jax.experimental.pallas import tpu as pltpu
from jax.sharding import PartitionSpec as P

WID = 64
SUB = 16
F32 = jnp.float32
BF16 = jnp.bfloat16
VMEM_LIMIT = 24 * 1024 * 1024
TOKEN = (8, 128)
FEATURE_COST = 3 * 10**9
FAR_COST = 6 * 10**8
NEAR_COST = 3 * 10**9


def from_behind(x, axis, by):
    size = lax.axis_size(axis)
    pairs = [(i, i + by) for i in range(size) if 0 <= i + by < size]
    return lax.ppermute(x, axis, pairs)


def padded_copies(block):
    pixels = block.shape[-1]
    column = lax.broadcasted_iota(jnp.int32, (pixels,), 0) % WID
    nothing = jnp.zeros((), block.dtype)
    widths = [(0, 0), (0, 0), (0, 0), (WID + 1, WID + 1)]
    left_cut = jnp.pad(jnp.where(column == WID - 1, nothing, block), widths)
    untouched = jnp.pad(block, widths)
    right_cut = jnp.pad(jnp.where(column == 0, nothing, block), widths)
    return (left_cut, untouched, right_cut)


def tap_window(copies, first_frame, vertical, horizontal, frames, pixels):
    source = copies[horizontal]
    offset = vertical * WID + horizontal
    return source[:, :, first_frame : first_frame + frames, offset : offset + pixels]


def stacked_taps(copies, first_frame, flipped, frames, pixels):
    pieces = []
    for vertical in range(3):
        for horizontal in range(3):
            if flipped:
                pieces.append(
                    tap_window(copies, first_frame, 2 - vertical, 2 - horizontal, frames, pixels)
                )
            else:
                pieces.append(tap_window(copies, first_frame, vertical, horizontal, frames, pixels))
    concatenated = jnp.concatenate(pieces, axis=0)
    return concatenated.reshape(concatenated.shape[0], -1)


def local_generic(features, kernel, cotangent):
    channels, clip_count, frames, pixels = features.shape
    flat_length = clip_count * frames * pixels
    widened = features.astype(F32)
    logistic = jax.nn.sigmoid(widened)
    activation = (widened * logistic).astype(BF16)
    slope_factor = logistic * (1.0 + widened * (1.0 - logistic))
    earlier = from_behind(activation[:, :, frames - 2 :, :], "tm", 1)
    extended = jnp.concatenate([earlier, activation], axis=2)
    upcoming = from_behind(cotangent[:, :, :2, :], "tm", -1)
    later_padded = jnp.concatenate([cotangent, upcoming], axis=2)
    cotangent_rows = cotangent.reshape(channels, -1)
    portion = lax.all_gather(extended, "chan", axis=0, tiled=True)
    out_sum = jnp.zeros((channels, flat_length), F32)
    amount = portion.shape[0]
    copies = padded_copies(portion)
    grad_parts = []
    for temporal in range(3):
        stacked = stacked_taps(copies, temporal, False, frames, pixels)
        weights = kernel[:, 9 * temporal : 9 * temporal + 9, :].reshape(channels, 9 * amount)
        out_sum = out_sum + jnp.dot(weights, stacked, preferred_element_type=F32)
        grad_parts.append(
            lax.dot_general(
                cotangent_rows, stacked, (((1,), (1,)), ((), ())), preferred_element_type=F32
            ).reshape(channels, 9, amount)
        )
    grad_sum = jnp.concatenate(grad_parts, axis=1)
    conv_out = out_sum.reshape(features.shape).astype(BF16)
    position_count = lax.axis_size("dp") * lax.axis_size("tm") * flat_length
    kernel_grad = lax.psum(grad_sum, ("tm", "dp")) * (1.0 / math.sqrt(position_count))
    padded_later = padded_copies(later_padded)
    summed = jnp.zeros((amount, flat_length), F32)
    for temporal in range(3):
        weights = jnp.transpose(
            kernel[:, 9 * temporal : 9 * temporal + 9, :], (2, 1, 0)
        ).reshape(amount, 9 * channels)
        stacked = stacked_taps(padded_later, 2 - temporal, True, frames, pixels)
        summed = summed + jnp.dot(weights, stacked, preferred_element_type=F32)
    before_slope = lax.psum_scatter(
        summed.reshape(amount, clip_count, frames, pixels), "chan", scatter_dimension=0, tiled=True
    )
    feature_grad = (before_slope * slope_factor).astype(BF16)
    return (conv_out, feature_grad, kernel_grad)


def rotate(x, axis, by):
    size = lax.axis_size(axis)
    return lax.ppermute(x, axis, [(i, (i + by) % size) for i in range(size)])


def shifted(frame, down, right):
    pixels = frame.shape[-1]
    if down == 0 and right == 0:
        return frame
    cell = lax.broadcasted_iota(jnp.int32, (1, pixels), 1)
    row, column = cell // WID + down, cell % WID + right
    inside = (row >= 0) & (row < pixels // WID) & (column >= 0) & (column < WID)
    moved = pltpu.roll(frame, (-(down * WID + right)) % pixels, 1)
    return jnp.where(inside, moved, 0.0)


def after(x, *others, flops=1):
    anywhere = pl.BlockSpec(memory_space=pl.ANY)
    return pl.pallas_call(
        lambda *refs: None,
        out_shape=jax.ShapeDtypeStruct(x.shape, x.dtype),
        in_specs=[anywhere] * (1 + len(others)),
        out_specs=anywhere,
        input_output_aliases={0: 0},
        compiler_params=pltpu.CompilerParams(vmem_limit_bytes=1024 * 1024),
        cost_estimate=cost(flops),
        name="hand_on",
    )(x, *others)


def run(kernel, args, waits=(), **options):
    options.setdefault("in_specs", [whole()] * len(args))
    options.setdefault("cost_estimate", cost())
    options["in_specs"] = list(options["in_specs"]) + [
        pl.BlockSpec(memory_space=pl.ANY) for _ in waits
    ]
    count = len(args)

    def body(*refs):
        kernel(*refs[:count], *refs[count + len(waits) :])

    return pl.pallas_call(
        body, compiler_params=pltpu.CompilerParams(vmem_limit_bytes=VMEM_LIMIT), **options
    )(*args, *waits)


def cost(flops=1):
    return pl.CostEstimate(flops=flops, bytes_accessed=1, transcendentals=0)


def whole():
    return pl.BlockSpec(memory_space=pltpu.VMEM)


def activate_kernel(features, cotangent, activation, flat, feat, cot, sems):
    parts = sems.shape[1]
    rows, _, frames, pixels = feat.shape
    size = rows // parts
    loads = []
    for n, (source, target) in enumerate(((features, feat), (cotangent, cot))):
        for part in range(parts):
            at = pl.ds(part * size, size)
            loads.append(pltpu.make_async_copy(source.at[at], target.at[at], sems.at[n, part]))
    for load in loads:
        load.start()
    for part in range(parts):
        loads[part].wait()
        at = slice(part * size, (part + 1) * size)
        v = feat[at, 0].astype(F32)
        act = v / (1.0 + jnp.exp(-v))
        for t in range(frames):
            activation[at, t * pixels : (t + 1) * pixels] = act[:, t, :].astype(BF16)
    for load in loads[parts:]:
        load.wait()
    flatten(pixels, cot, flat, 0)


def flatten(pixels, source, flat, first):
    wide = source[:, 0].astype(F32)
    for t in range(wide.shape[1]):
        at = (first + t) * pixels
        at = at if isinstance(at, int) else pl.multiple_of(at, pixels)
        flat[:, pl.ds(at, pixels)] = wide[:, t, :]


def shard_at(count, k):
    z = lax.axis_index("chan")
    return (z, z + 1 - 2 * lax.rem(z, 2), lax.rem(z + 2, count), count - 1 - z)[k]


def in_slot(channels, rows, slot):
    lane = lax.broadcasted_iota(jnp.int32, (1, channels), 1)
    return (lane >= slot * rows) & (lane < (slot + 1) * rows)


def packed_rows(total):
    unit = total // 9
    return 7 * unit, 2 * unit


def fill_stack(pixels, flat, stack, half, first, frames):
    unit = flat.shape[0] // 2
    for t in range(frames):
        at = slice(t * pixels, (t + 1) * pixels)
        source = slice((first + t) * pixels, (first + t + 1) * pixels)
        for q in range(9):
            tap, part = divmod(9 * half + q, 2)
            i, j = divmod(tap, 3)
            frame = flat[part * unit : (part + 1) * unit, source]
            stack[q * unit : (q + 1) * unit, at] = shifted(frame, 1 - i, 1 - j).astype(BF16)


def block_terms(pixels, k, stack, here, there, out, rhs):
    channels = out.shape[1]
    rows, length = here.shape
    lanes, count = 2 * length, channels // rows
    shard = shard_at(count, k)
    for core in range(2):

        @pl.when(lax.axis_index("tm") == core)
        def _(first=(here, there)[core], second=(there, here)[core]):
            for a in range(3):
                skip = (2 - a) * pixels
                at = pl.ds(pl.multiple_of(lax.rem(shard + a, count) * rows, SUB), rows)
                if skip:
                    rhs[at, :skip] = jnp.zeros((rows, skip), BF16)
                rhs[at, skip : skip + length] = first[...]
                rhs[at, skip + length :] = second[:, : length - skip]

    last = lax.rem(shard + 3, count)
    rhs[pl.ds(pl.multiple_of(last * rows, SUB), rows), :] = jnp.zeros((rows, lanes), BF16)
    terms = lax.dot_general(
        stack[...], rhs[...], (((1,), (1,)), ((), ())), preferred_element_type=F32
    )
    main, tail = packed_rows(terms.shape[0])
    free = in_slot(channels, rows, last)
    for a in range(3):
        at = slice(a * tail, (a + 1) * tail)
        moved = pltpu.roll(terms[main:], (3 - a) * rows, 1)
        out[at, :] = jnp.where(free, moved, terms[at]).astype(BF16)
    out[3 * tail :, :] = terms[3 * tail : main].astype(BF16)


def own_terms_kernel(
    pixels, mine, other, flat_own, cot_other, weights, out, stack, flat, held, rhs, sems
):
    load = pltpu.make_async_copy(weights, held, sems.at[0])
    load.start()
    length = flat_own.shape[1]
    me = lax.axis_index("tm")
    flat[:, pl.ds(pl.multiple_of(me * length, pixels), length)] = flat_own[...]
    flatten(pixels, cot_other, flat, (1 - me) * (length // pixels))
    for core in range(2):

        @pl.when(me == core)
        def _(core=core):
            fill_stack(pixels, flat, stack, core, 0, flat.shape[1] // pixels)

    block_terms(pixels, 0, stack, mine, other, out, rhs)
    load.wait()


def terms_kernel(pixels, k, stack, here, there, out, rhs):
    block_terms(pixels, k, stack, here, there, out, rhs)


def share_kernel(pixels, weights, flat, mine, own, kept, sent, window, other, total):
    rows, length = own.shape
    frames, half = length // pixels, mine.shape[0]
    count = weights.shape[1] // rows
    me = lax.axis_index("tm")
    front = 2 * pixels
    for core in range(2):

        @pl.when(me == core)
        def _(core=core):
            first = core * length
            held = min(length + front, mine.shape[1] - first)
            window[:, :held] = mine[:, first : first + held]
            if held < length + front:
                window[:, held:] = jnp.zeros((half, length + front - held), BF16)
                other[:, held:] = jnp.zeros((half, length + front - held), BF16)
            fill_stack(pixels, flat, other, 1 - core, core * frames, held // pixels)

    acc = None
    for a in range(3):
        lanes = slice((2 - a) * pixels, (2 - a) * pixels + length)
        for which, stack in ((me, window), (1 - me, other)):
            at = pl.multiple_of((2 * a + which) * half, SUB)
            term = lax.dot_general(
                weights[pl.ds(at, half), :],
                stack[:, lanes],
                (((0,), (0,)), ((), ())),
                preferred_element_type=F32,
            )
            acc = term if acc is None else acc + term
    total[...] = acc

    def part(k):
        return total[pl.ds(pl.multiple_of(shard_at(count, k) * rows, SUB), rows), :]

    own[...] = part(0)
    kept[...] = part(2)
    sent[0] = part(1).astype(BF16)
    sent[1] = part(3).astype(BF16)


def split_kernel(block, out, first, second):
    out[...] = block[...]
    middle = block.shape[1] // 2
    first[...] = block[:, :middle]
    second[...] = block[:, middle:]


def join_kernel(first, second, out):
    middle = out.shape[1] // 2
    out[:, :middle] = first[...]
    out[:, middle:] = second[...]


def add_kernel(kept, came, out):
    out[...] = (kept[...] + came[1].astype(F32)).astype(out.dtype)


def conv_kernel(pixels, weights, *refs):
    blocks, (out, token, act) = refs[:-3], refs[-3:]
    token[...] = jnp.zeros(TOKEN, F32)
    rows, _, frames, _ = out.shape
    count = weights.shape[1] // rows
    length, front = frames * pixels, 2 * pixels
    me = lax.axis_index("tm")
    for k in range(count):
        here, there = blocks[2 * k], blocks[2 * k + 1]
        at = pl.ds(pl.multiple_of(shard_at(count, k) * rows, SUB), rows)
        earlier = there[:, length - front :]
        act[at, :front] = jnp.where(me == 0, jnp.zeros_like(earlier), earlier)
        act[at, front:] = here[...]

    taps = 9 * rows
    for t in range(frames):
        z_t = None
        for a in range(3):
            term = jnp.dot(
                weights[a * taps : (a + 1) * taps, :],
                act[:, (t + a) * pixels : (t + a + 1) * pixels],
                preferred_element_type=F32,
            )
            z_t = term if z_t is None else z_t + term
        acc = None
        for i in range(3):
            for j in range(3):
                at = (3 * i + j) * rows
                moved = shifted(z_t[at : at + rows, :], i - 1, j - 1)
                acc = moved if acc is None else acc + moved
        out[:, 0, t, :] = acc.astype(BF16)


def feature_kernel(pixels, features, own, first, second, out, token):
    token[...] = jnp.zeros(TOKEN, F32)
    frames = features.shape[2]
    total = own[...] + first[0].astype(F32) + second[...].astype(F32)
    v = features[:, 0].astype(F32)
    s = 1.0 / (1.0 + jnp.exp(-v))
    slope = s * (1.0 + v * (1.0 - s))
    for t in range(frames):
        piece = total[:, t * pixels : (t + 1) * pixels] * slope[:, t, :]
        out[:, 0, t, :] = piece.astype(BF16)


def sum_kernel(main, *refs):
    out, ins = refs[-1], refs[:-1]
    count = len(ins) // 2
    for k in range(count):
        total = ins[k][...].astype(F32) + ins[count + k][...].astype(F32)
        out[k * main : (k + 1) * main, :] = total.astype(BF16)


def finish_kernel(scale, main, whose, early, late, *refs):
    out, laid, sems = refs[-3:]
    channels = out.shape[2]
    first = early.shape[0] // main
    count = first + late.shape[0] // main
    rows, half = channels // count, out.shape[1] // 2
    unit = rows // 2
    which = lax.rem(lax.axis_index("tm") + whose, 2)
    at = pl.ds(pl.multiple_of(which * half, 8), half)
    shards = [shard_at(count, k) for k in range(count)]
    copies = []
    for a in range(3):
        for q in range(9):
            base = q * unit if q < 7 else a * 2 * unit + (q - 7) * unit
            step = a if q < 7 else 3
            total = None
            for k, shard in enumerate(shards):
                source, place = (early, k) if k < first else (late, k - first)
                piece = source[place * main + base : place * main + base + unit, :].astype(F32)
                mask = in_slot(channels, rows, lax.rem(shard + step, count))
                total = piece if total is None else jnp.where(mask, piece, total)
            total = total * scale
            if step:
                total = pltpu.roll(total, channels - step * rows, 1)
            laid[a, q * unit : (q + 1) * unit, :] = total
        copy = pltpu.make_async_copy(laid.at[a], out.at[a, at], sems.at[a])
        copy.start()
        copies.append(copy)
    for copy in copies:
        copy.wait()


def in_place(x):
    return pltpu.with_memory_space_constraint(x, pltpu.HBM)


def local_fast(features, kernel, cotangent):
    rows, _, frames, pixels = features.shape
    length = frames * pixels
    count = lax.axis_size("chan")
    channels = rows * count
    taps = kernel.shape[1]
    half = 9 * rows // 2
    main, _ = packed_rows(half)
    sds = jax.ShapeDtypeStruct
    block_shape = sds((rows, length), BF16)
    term_shape = sds((main, channels), BF16)
    stack_shape = sds((half, 2 * length), BF16)
    rhs = pltpu.VMEM((channels, 2 * length), BF16)

    def swap(x, far):
        return lax.ppermute(x, "chan", [(z, z ^ far) for z in range(count)])

    weights = jnp.transpose(kernel, (1, 0, 2)).reshape(taps * rows, channels)
    hbm = pl.BlockSpec(memory_space=pltpu.HBM)
    cot_other = rotate(cotangent, "tm", 1)
    activation, flat_own = run(
        activate_kernel,
        (in_place(features), in_place(cotangent)),
        in_specs=[hbm] * 2,
        out_shape=(block_shape, sds((rows, length), F32)),
        out_specs=(whole(),) * 2,
        scratch_shapes=[
            pltpu.VMEM(features.shape, BF16),
            pltpu.VMEM(features.shape, BF16),
            pltpu.SemaphoreType.DMA((2, 3)),
        ],
        name="activate",
    )
    other = rotate(activation, "tm", 1)
    near, far = swap(activation, 1), swap(activation, 2)
    own_term, stack, flat, weights = run(
        functools.partial(own_terms_kernel, pixels),
        (activation, other, flat_own, cot_other, in_place(weights)),
        in_specs=[whole()] * 4 + [hbm],
        out_shape=(
            term_shape,
            stack_shape,
            sds((rows, 2 * length), F32),
            sds(weights.shape, BF16),
        ),
        out_specs=(whole(),) * 4,
        scratch_shapes=[rhs, pltpu.SemaphoreType.DMA((1,))],
        name="own_terms",
    )
    terms, got = [own_term], [rotate(own_term, "dp", 1)]
    blocks = [activation, other]

    def terms_of(k, here, there, waits=()):
        blocks.extend((here, there))
        term = run(
            functools.partial(terms_kernel, pixels, k),
            (stack, *blocks[-2:]),
            waits=waits,
            out_shape=term_shape,
            out_specs=whole(),
            scratch_shapes=[rhs],
            name=f"terms_{k}",
        )
        terms.append(term)
        got.append(rotate(term, "dp", 1))
        return term

    own_share, kept, sent = run(
        functools.partial(share_kernel, pixels),
        (weights, flat, stack),
        waits=(own_term,),
        out_shape=(
            sds((rows, length), F32),
            sds((rows, length), F32),
            sds((2, rows, length), BF16),
        ),
        out_specs=(whole(),) * 3,
        scratch_shapes=[
            pltpu.VMEM((half, (frames + 2) * pixels), BF16),
            pltpu.VMEM((half, (frames + 2) * pixels), BF16),
            pltpu.VMEM((channels, length), F32),
        ],
        name="shares",
    )
    first_share = swap(sent, 1)
    near = after(near, own_share, flops=NEAR_COST)
    far = after(far, own_share, flops=FAR_COST)
    last = swap(far, 1)
    term = terms_of(1, near, rotate(near, "tm", 1), (own_share, far, got[0]))
    term = terms_of(2, far, rotate(far, "tm", 1), (term,))
    carry = run(
        add_kernel,
        (kept, first_share),
        waits=(term,),
        out_shape=block_shape,
        out_specs=whole(),
        name="carry_share",
    )
    second_share = swap(carry, 2)
    last, *parts = run(
        split_kernel,
        (last,),
        waits=(carry,),
        out_shape=(block_shape,) + (sds((rows, length // 2), BF16),) * 2,
        out_specs=(whole(),) * 3,
        name="split",
    )
    last_other = run(
        join_kernel,
        [rotate(part, "tm", 1) for part in parts],
        out_shape=block_shape,
        out_specs=whole(),
        name="join",
    )
    term = terms_of(3, last, last_other, (got[1],))

    def sums(first, stop, waits=()):
        return run(
            functools.partial(sum_kernel, main),
            (*terms[first:stop], *got[first:stop]),
            waits=waits,
            out_shape=sds(((stop - first) * main, channels), BF16),
            out_specs=whole(),
            name=f"sums_{first}",
        )

    conv_out, token = run(
        functools.partial(conv_kernel, pixels),
        (weights, *blocks),
        waits=(term, got[2]),
        out_shape=(sds(features.shape, BF16), sds(TOKEN, F32)),
        out_specs=(whole(),) * 2,
        scratch_shapes=[pltpu.VMEM((channels, (frames + 2) * pixels), BF16)],
        name="conv",
    )
    early = sums(0, 2, (term,))
    feature_grad, token = run(
        functools.partial(feature_kernel, pixels),
        (features, own_share, first_share, second_share),
        waits=(token, early),
        out_shape=(sds(features.shape, BF16), sds(TOKEN, F32)),
        out_specs=(whole(),) * 2,
        cost_estimate=cost(FEATURE_COST),
        name="feature_grad",
    )
    late = sums(2, count, (token,))
    scale = 1.0 / math.sqrt(lax.axis_size("dp") * lax.axis_size("tm") * length)

    def finish(whose, sums, base=()):
        anywhere = pl.BlockSpec(memory_space=pl.ANY)
        return run(
            functools.partial(finish_kernel, scale, main, whose),
            (*sums, *base),
            in_specs=[whole()] * 2 + [anywhere] * len(base),
            out_shape=sds((3, 9 * rows, channels), F32),
            out_specs=anywhere,
            input_output_aliases={2: 0} if base else {},
            scratch_shapes=[pltpu.VMEM((3, half, channels), F32), pltpu.SemaphoreType.DMA((3,))],
            name=f"kernel_grad_{whose}",
        )

    kernel_grad = finish(0, (early, late))
    kernel_grad = finish(1, (rotate(early, "tm", 1), rotate(late, "tm", 1)), (kernel_grad,))
    kernel_grad = jnp.transpose(kernel_grad.reshape(taps, rows, channels), (1, 0, 2))
    return (conv_out, feature_grad, kernel_grad)


def local(features, kernel, cotangent):
    rows, clips, _, pixels = features.shape
    fits = (
        clips == 1
        and lax.axis_size("tm") == 2
        and lax.axis_size("dp") == 2
        and rows % (2 * SUB) == 0
        and pixels % 128 == 0
        and kernel.shape[1] == 27
        and lax.axis_size("chan") == 4
    )
    return (local_fast if fits else local_generic)(features, kernel, cotangent)


def solution(mesh):
    return jax.shard_map(
        local,
        mesh=mesh,
        in_specs=(
            P("chan", ("groups", "dp"), "tm", None),
            P("chan", None, None),
            P("chan", ("groups", "dp"), "tm", None),
        ),
        out_specs=(
            P("chan", ("groups", "dp"), "tm", None),
            P("chan", ("groups", "dp"), "tm", None),
            P(("groups", "chan"), None, None),
        ),
        check_vma=False,
    )
```

```python
import functools
import math

import jax
import jax.numpy as jnp
from jax import lax
from jax.experimental import pallas as pl
from jax.experimental.pallas import tpu as pltpu
from jax.sharding import PartitionSpec as P

WID = 64
SUB = 16
F32 = jnp.float32
BF16 = jnp.bfloat16
VMEM_LIMIT = 24 * 1024 * 1024
TOKEN = (8, 128)
FEATURE_COST = 3 * 10**9
FAR_COST = 10**9
NEAR_COST = 3 * 10**9


def from_behind(x, axis, by):
    size = lax.axis_size(axis)
    pairs = [(i, i + by) for i in range(size) if 0 <= i + by < size]
    return lax.ppermute(x, axis, pairs)


def padded_copies(block):
    pixels = block.shape[-1]
    column = lax.broadcasted_iota(jnp.int32, (pixels,), 0) % WID
    nothing = jnp.zeros((), block.dtype)
    widths = [(0, 0), (0, 0), (0, 0), (WID + 1, WID + 1)]
    left_cut = jnp.pad(jnp.where(column == WID - 1, nothing, block), widths)
    untouched = jnp.pad(block, widths)
    right_cut = jnp.pad(jnp.where(column == 0, nothing, block), widths)
    return (left_cut, untouched, right_cut)


def tap_window(copies, first_frame, vertical, horizontal, frames, pixels):
    source = copies[horizontal]
    offset = vertical * WID + horizontal
    return source[:, :, first_frame : first_frame + frames, offset : offset + pixels]


def stacked_taps(copies, first_frame, flipped, frames, pixels):
    pieces = []
    for vertical in range(3):
        for horizontal in range(3):
            if flipped:
                pieces.append(
                    tap_window(copies, first_frame, 2 - vertical, 2 - horizontal, frames, pixels)
                )
            else:
                pieces.append(tap_window(copies, first_frame, vertical, horizontal, frames, pixels))
    concatenated = jnp.concatenate(pieces, axis=0)
    return concatenated.reshape(concatenated.shape[0], -1)


def local_generic(features, kernel, cotangent):
    channels, clip_count, frames, pixels = features.shape
    flat_length = clip_count * frames * pixels
    widened = features.astype(F32)
    logistic = jax.nn.sigmoid(widened)
    activation = (widened * logistic).astype(BF16)
    slope_factor = logistic * (1.0 + widened * (1.0 - logistic))
    earlier = from_behind(activation[:, :, frames - 2 :, :], "tm", 1)
    extended = jnp.concatenate([earlier, activation], axis=2)
    upcoming = from_behind(cotangent[:, :, :2, :], "tm", -1)
    later_padded = jnp.concatenate([cotangent, upcoming], axis=2)
    cotangent_rows = cotangent.reshape(channels, -1)
    portion = lax.all_gather(extended, "chan", axis=0, tiled=True)
    out_sum = jnp.zeros((channels, flat_length), F32)
    amount = portion.shape[0]
    copies = padded_copies(portion)
    grad_parts = []
    for temporal in range(3):
        stacked = stacked_taps(copies, temporal, False, frames, pixels)
        weights = kernel[:, 9 * temporal : 9 * temporal + 9, :].reshape(channels, 9 * amount)
        out_sum = out_sum + jnp.dot(weights, stacked, preferred_element_type=F32)
        grad_parts.append(
            lax.dot_general(
                cotangent_rows, stacked, (((1,), (1,)), ((), ())), preferred_element_type=F32
            ).reshape(channels, 9, amount)
        )
    grad_sum = jnp.concatenate(grad_parts, axis=1)
    conv_out = out_sum.reshape(features.shape).astype(BF16)
    position_count = lax.axis_size("dp") * lax.axis_size("tm") * flat_length
    kernel_grad = lax.psum(grad_sum, ("tm", "dp")) * (1.0 / math.sqrt(position_count))
    padded_later = padded_copies(later_padded)
    summed = jnp.zeros((amount, flat_length), F32)
    for temporal in range(3):
        weights = jnp.transpose(
            kernel[:, 9 * temporal : 9 * temporal + 9, :], (2, 1, 0)
        ).reshape(amount, 9 * channels)
        stacked = stacked_taps(padded_later, 2 - temporal, True, frames, pixels)
        summed = summed + jnp.dot(weights, stacked, preferred_element_type=F32)
    before_slope = lax.psum_scatter(
        summed.reshape(amount, clip_count, frames, pixels), "chan", scatter_dimension=0, tiled=True
    )
    feature_grad = (before_slope * slope_factor).astype(BF16)
    return (conv_out, feature_grad, kernel_grad)


def rotate(x, axis, by):
    size = lax.axis_size(axis)
    return lax.ppermute(x, axis, [(i, (i + by) % size) for i in range(size)])


def shifted(frame, down, right):
    pixels = frame.shape[-1]
    if down == 0 and right == 0:
        return frame
    cell = lax.broadcasted_iota(jnp.int32, (1, pixels), 1)
    row, column = cell // WID + down, cell % WID + right
    inside = (row >= 0) & (row < pixels // WID) & (column >= 0) & (column < WID)
    moved = pltpu.roll(frame, (-(down * WID + right)) % pixels, 1)
    return jnp.where(inside, moved, 0.0)


def after(x, *others, flops=1):
    anywhere = pl.BlockSpec(memory_space=pl.ANY)
    return pl.pallas_call(
        lambda *refs: None,
        out_shape=jax.ShapeDtypeStruct(x.shape, x.dtype),
        in_specs=[anywhere] * (1 + len(others)),
        out_specs=anywhere,
        input_output_aliases={0: 0},
        compiler_params=pltpu.CompilerParams(vmem_limit_bytes=1024 * 1024),
        cost_estimate=cost(flops),
        name="hand_on",
    )(x, *others)


def run(kernel, args, waits=(), **options):
    options.setdefault("in_specs", [whole()] * len(args))
    options.setdefault("cost_estimate", cost())
    options["in_specs"] = list(options["in_specs"]) + [
        pl.BlockSpec(memory_space=pl.ANY) for _ in waits
    ]
    count = len(args)

    def body(*refs):
        kernel(*refs[:count], *refs[count + len(waits) :])

    return pl.pallas_call(
        body, compiler_params=pltpu.CompilerParams(vmem_limit_bytes=VMEM_LIMIT), **options
    )(*args, *waits)


def cost(flops=1):
    return pl.CostEstimate(flops=flops, bytes_accessed=1, transcendentals=0)


def whole():
    return pl.BlockSpec(memory_space=pltpu.VMEM)


def activate_kernel(features, cotangent, activation, flat, feat, cot, sems):
    parts = sems.shape[1]
    rows, _, frames, pixels = feat.shape
    size = rows // parts
    loads = []
    for n, (source, target) in enumerate(((features, feat), (cotangent, cot))):
        for part in range(parts):
            at = pl.ds(part * size, size)
            loads.append(pltpu.make_async_copy(source.at[at], target.at[at], sems.at[n, part]))
    for load in loads:
        load.start()
    for part in range(parts):
        loads[part].wait()
        at = slice(part * size, (part + 1) * size)
        v = feat[at, 0].astype(F32)
        act = v / (1.0 + jnp.exp(-v))
        for t in range(frames):
            activation[at, t * pixels : (t + 1) * pixels] = act[:, t, :].astype(BF16)
    for load in loads[parts:]:
        load.wait()
    flatten(pixels, cot, flat, 0)


def flatten(pixels, source, flat, first):
    wide = source[:, 0].astype(F32)
    for t in range(wide.shape[1]):
        at = (first + t) * pixels
        at = at if isinstance(at, int) else pl.multiple_of(at, pixels)
        flat[:, pl.ds(at, pixels)] = wide[:, t, :]


def shard_at(count, k):
    z = lax.axis_index("chan")
    return (z, z + 1 - 2 * lax.rem(z, 2), lax.rem(z + 2, count), count - 1 - z)[k]


def in_slot(channels, rows, slot):
    lane = lax.broadcasted_iota(jnp.int32, (1, channels), 1)
    return (lane >= slot * rows) & (lane < (slot + 1) * rows)


def packed_rows(total):
    unit = total // 9
    return 7 * unit, 2 * unit


def fill_stack(pixels, flat, stack, half, first, frames):
    unit = flat.shape[0] // 2
    for t in range(frames):
        at = slice(t * pixels, (t + 1) * pixels)
        source = slice((first + t) * pixels, (first + t + 1) * pixels)
        for q in range(9):
            tap, part = divmod(9 * half + q, 2)
            i, j = divmod(tap, 3)
            frame = flat[part * unit : (part + 1) * unit, source]
            stack[q * unit : (q + 1) * unit, at] = shifted(frame, 1 - i, 1 - j).astype(BF16)


def block_terms(pixels, k, stack, here, there, out, rhs):
    channels = out.shape[1]
    rows, length = here.shape
    lanes, count = 2 * length, channels // rows
    shard = shard_at(count, k)
    for core in range(2):

        @pl.when(lax.axis_index("tm") == core)
        def _(first=(here, there)[core], second=(there, here)[core]):
            for a in range(3):
                skip = (2 - a) * pixels
                at = pl.ds(pl.multiple_of(lax.rem(shard + a, count) * rows, SUB), rows)
                if skip:
                    rhs[at, :skip] = jnp.zeros((rows, skip), BF16)
                rhs[at, skip : skip + length] = first[...]
                rhs[at, skip + length :] = second[:, : length - skip]

    last = lax.rem(shard + 3, count)
    rhs[pl.ds(pl.multiple_of(last * rows, SUB), rows), :] = jnp.zeros((rows, lanes), BF16)
    terms = lax.dot_general(
        stack[...], rhs[...], (((1,), (1,)), ((), ())), preferred_element_type=F32
    )
    main, tail = packed_rows(terms.shape[0])
    free = in_slot(channels, rows, last)
    for a in range(3):
        at = slice(a * tail, (a + 1) * tail)
        moved = pltpu.roll(terms[main:], (3 - a) * rows, 1)
        out[at, :] = jnp.where(free, moved, terms[at]).astype(BF16)
    out[3 * tail :, :] = terms[3 * tail : main].astype(BF16)


def own_terms_kernel(
    pixels, mine, other, flat_own, cot_other, weights, out, stack, flat, held, rhs, sems
):
    load = pltpu.make_async_copy(weights, held, sems.at[0])
    load.start()
    length = flat_own.shape[1]
    me = lax.axis_index("tm")
    flat[:, pl.ds(pl.multiple_of(me * length, pixels), length)] = flat_own[...]
    flatten(pixels, cot_other, flat, (1 - me) * (length // pixels))
    for core in range(2):

        @pl.when(me == core)
        def _(core=core):
            fill_stack(pixels, flat, stack, core, 0, flat.shape[1] // pixels)

    block_terms(pixels, 0, stack, mine, other, out, rhs)
    load.wait()


def terms_kernel(pixels, k, stack, here, there, out, rhs):
    block_terms(pixels, k, stack, here, there, out, rhs)


def share_kernel(pixels, weights, flat, mine, own, kept, near, passed, window, other, total):
    rows, length = own.shape
    frames, half = length // pixels, mine.shape[0]
    count = weights.shape[1] // rows
    me = lax.axis_index("tm")
    front = 2 * pixels
    for core in range(2):

        @pl.when(me == core)
        def _(core=core):
            first = core * length
            held = min(length + front, mine.shape[1] - first)
            window[:, :held] = mine[:, first : first + held]
            if held < length + front:
                window[:, held:] = jnp.zeros((half, length + front - held), BF16)
                other[:, held:] = jnp.zeros((half, length + front - held), BF16)
            fill_stack(pixels, flat, other, 1 - core, core * frames, held // pixels)

    acc = None
    for a in range(3):
        lanes = slice((2 - a) * pixels, (2 - a) * pixels + length)
        for which, stack in ((me, window), (1 - me, other)):
            at = pl.multiple_of((2 * a + which) * half, SUB)
            term = lax.dot_general(
                weights[pl.ds(at, half), :],
                stack[:, lanes],
                (((0,), (0,)), ((), ())),
                preferred_element_type=F32,
            )
            acc = term if acc is None else acc + term
    total[...] = acc

    def part(k):
        return total[pl.ds(pl.multiple_of(shard_at(count, k) * rows, SUB), rows), :]

    own[...] = part(0)
    kept[...] = part(2)
    near[...] = part(1).astype(BF16)
    passed[...] = part(3).astype(BF16)


def pack_kernel(block, share, out, message):
    out[...] = block[...]
    message[0] = block[...]
    message[1] = share[...]


def unpack_kernel(message, block, share):
    block[...] = message[0]
    share[...] = message[1]


def add_kernel(kept, came, out):
    out[...] = (kept[...] + came[...].astype(F32)).astype(out.dtype)


def conv_kernel(pixels, weights, *refs):
    blocks, (out, token, act) = refs[:-3], refs[-3:]
    token[...] = jnp.zeros(TOKEN, F32)
    rows, _, frames, _ = out.shape
    count = weights.shape[1] // rows
    length, front = frames * pixels, 2 * pixels
    me = lax.axis_index("tm")
    for k in range(count):
        here, there = blocks[2 * k], blocks[2 * k + 1]
        at = pl.ds(pl.multiple_of(shard_at(count, k) * rows, SUB), rows)
        earlier = there[:, length - front :]
        act[at, :front] = jnp.where(me == 0, jnp.zeros_like(earlier), earlier)
        act[at, front:] = here[...]

    taps = 9 * rows
    for t in range(frames):
        z_t = None
        for a in range(3):
            term = jnp.dot(
                weights[a * taps : (a + 1) * taps, :],
                act[:, (t + a) * pixels : (t + a + 1) * pixels],
                preferred_element_type=F32,
            )
            z_t = term if z_t is None else z_t + term
        acc = None
        for i in range(3):
            for j in range(3):
                at = (3 * i + j) * rows
                moved = shifted(z_t[at : at + rows, :], i - 1, j - 1)
                acc = moved if acc is None else acc + moved
        out[:, 0, t, :] = acc.astype(BF16)


def feature_kernel(pixels, features, own, first, second, out, token):
    token[...] = jnp.zeros(TOKEN, F32)
    frames = features.shape[2]
    total = own[...] + first[...].astype(F32) + second[...].astype(F32)
    v = features[:, 0].astype(F32)
    s = 1.0 / (1.0 + jnp.exp(-v))
    slope = s * (1.0 + v * (1.0 - s))
    for t in range(frames):
        piece = total[:, t * pixels : (t + 1) * pixels] * slope[:, t, :]
        out[:, 0, t, :] = piece.astype(BF16)


def sum_kernel(main, *refs):
    out, ins = refs[-1], refs[:-1]
    count = len(ins) // 2
    for k in range(count):
        total = ins[k][...].astype(F32) + ins[count + k][...].astype(F32)
        out[k * main : (k + 1) * main, :] = total.astype(BF16)


def finish_kernel(scale, main, whose, early, late, *refs):
    out, laid, sems = refs[-3:]
    channels = out.shape[2]
    first = early.shape[0] // main
    count = first + late.shape[0] // main
    rows, half = channels // count, out.shape[1] // 2
    unit = rows // 2
    which = lax.rem(lax.axis_index("tm") + whose, 2)
    at = pl.ds(pl.multiple_of(which * half, 8), half)
    shards = [shard_at(count, k) for k in range(count)]
    copies = []
    for a in range(3):
        for q in range(9):
            base = q * unit if q < 7 else a * 2 * unit + (q - 7) * unit
            step = a if q < 7 else 3
            total = None
            for k, shard in enumerate(shards):
                source, place = (early, k) if k < first else (late, k - first)
                piece = source[place * main + base : place * main + base + unit, :].astype(F32)
                mask = in_slot(channels, rows, lax.rem(shard + step, count))
                total = piece if total is None else jnp.where(mask, piece, total)
            total = total * scale
            if step:
                total = pltpu.roll(total, channels - step * rows, 1)
            laid[a, q * unit : (q + 1) * unit, :] = total
        copy = pltpu.make_async_copy(laid.at[a], out.at[a, at], sems.at[a])
        copy.start()
        copies.append(copy)
    for copy in copies:
        copy.wait()


def in_place(x):
    return pltpu.with_memory_space_constraint(x, pltpu.HBM)


def local_fast(features, kernel, cotangent):
    rows, _, frames, pixels = features.shape
    length = frames * pixels
    count = lax.axis_size("chan")
    channels = rows * count
    taps = kernel.shape[1]
    half = 9 * rows // 2
    main, _ = packed_rows(half)
    sds = jax.ShapeDtypeStruct
    block_shape = sds((rows, length), BF16)
    term_shape = sds((main, channels), BF16)
    stack_shape = sds((half, 2 * length), BF16)
    rhs = pltpu.VMEM((channels, 2 * length), BF16)

    def swap(x, far):
        return lax.ppermute(x, "chan", [(z, z ^ far) for z in range(count)])

    weights = jnp.transpose(kernel, (1, 0, 2)).reshape(taps * rows, channels)
    hbm = pl.BlockSpec(memory_space=pltpu.HBM)
    cot_other = rotate(cotangent, "tm", 1)
    activation, flat_own = run(
        activate_kernel,
        (in_place(features), in_place(cotangent)),
        in_specs=[hbm] * 2,
        out_shape=(block_shape, sds((rows, length), F32)),
        out_specs=(whole(),) * 2,
        scratch_shapes=[
            pltpu.VMEM(features.shape, BF16),
            pltpu.VMEM(features.shape, BF16),
            pltpu.SemaphoreType.DMA((2, 3)),
        ],
        name="activate",
    )
    other = rotate(activation, "tm", 1)
    near, far = swap(activation, 1), swap(activation, 2)
    own_term, stack, flat, weights = run(
        functools.partial(own_terms_kernel, pixels),
        (activation, other, flat_own, cot_other, in_place(weights)),
        in_specs=[whole()] * 4 + [hbm],
        out_shape=(
            term_shape,
            stack_shape,
            sds((rows, 2 * length), F32),
            sds(weights.shape, BF16),
        ),
        out_specs=(whole(),) * 4,
        scratch_shapes=[rhs, pltpu.SemaphoreType.DMA((1,))],
        name="own_terms",
    )
    terms, got = [own_term], [rotate(own_term, "dp", 1)]
    blocks = [activation, other]

    def terms_of(k, here, there, waits=()):
        blocks.extend((here, there))
        term = run(
            functools.partial(terms_kernel, pixels, k),
            (stack, *blocks[-2:]),
            waits=waits,
            out_shape=term_shape,
            out_specs=whole(),
            scratch_shapes=[rhs],
            name=f"terms_{k}",
        )
        terms.append(term)
        got.append(rotate(term, "dp", 1))
        return term

    own_share, kept, near_share, passed_share = run(
        functools.partial(share_kernel, pixels),
        (weights, flat, stack),
        waits=(own_term,),
        out_shape=(
            sds((rows, length), F32),
            sds((rows, length), F32),
            block_shape,
            block_shape,
        ),
        out_specs=(whole(),) * 4,
        scratch_shapes=[
            pltpu.VMEM((half, (frames + 2) * pixels), BF16),
            pltpu.VMEM((half, (frames + 2) * pixels), BF16),
            pltpu.VMEM((channels, length), F32),
        ],
        name="shares",
    )
    first_share = swap(near_share, 1)
    near = after(near, own_share, flops=NEAR_COST)
    far, message = run(
        pack_kernel,
        (far, passed_share),
        out_shape=(block_shape, sds((2, rows, length), BF16)),
        out_specs=(whole(),) * 2,
        cost_estimate=cost(FAR_COST),
        name="pack",
    )
    message = swap(message, 1)
    term = terms_of(1, near, rotate(near, "tm", 1), (own_share, far, got[0]))
    term = terms_of(2, far, rotate(far, "tm", 1), (term,))
    last, passed_share = run(
        unpack_kernel,
        (message,),
        waits=(term, got[1]),
        out_shape=(block_shape, block_shape),
        out_specs=(whole(),) * 2,
        name="unpack",
    )
    carry = run(
        add_kernel,
        (kept, passed_share),
        out_shape=block_shape,
        out_specs=whole(),
        name="carry_share",
    )
    second_share = swap(carry, 2)
    term = terms_of(3, last, rotate(last, "tm", 1), (carry,))

    def sums(first, stop, waits=()):
        return run(
            functools.partial(sum_kernel, main),
            (*terms[first:stop], *got[first:stop]),
            waits=waits,
            out_shape=sds(((stop - first) * main, channels), BF16),
            out_specs=whole(),
            name=f"sums_{first}",
        )

    conv_out, token = run(
        functools.partial(conv_kernel, pixels),
        (weights, *blocks),
        waits=(term, got[2]),
        out_shape=(sds(features.shape, BF16), sds(TOKEN, F32)),
        out_specs=(whole(),) * 2,
        scratch_shapes=[pltpu.VMEM((channels, (frames + 2) * pixels), BF16)],
        name="conv",
    )
    early = sums(0, 2, (term,))
    feature_grad, token = run(
        functools.partial(feature_kernel, pixels),
        (features, own_share, first_share, second_share),
        waits=(token, early),
        out_shape=(sds(features.shape, BF16), sds(TOKEN, F32)),
        out_specs=(whole(),) * 2,
        cost_estimate=cost(FEATURE_COST),
        name="feature_grad",
    )
    late = sums(2, count, (token,))
    scale = 1.0 / math.sqrt(lax.axis_size("dp") * lax.axis_size("tm") * length)

    def finish(whose, sums, base=()):
        anywhere = pl.BlockSpec(memory_space=pl.ANY)
        return run(
            functools.partial(finish_kernel, scale, main, whose),
            (*sums, *base),
            in_specs=[whole()] * 2 + [anywhere] * len(base),
            out_shape=sds((3, 9 * rows, channels), F32),
            out_specs=anywhere,
            input_output_aliases={2: 0} if base else {},
            scratch_shapes=[pltpu.VMEM((3, half, channels), F32), pltpu.SemaphoreType.DMA((3,))],
            name=f"kernel_grad_{whose}",
        )

    kernel_grad = finish(0, (early, late))
    kernel_grad = finish(1, (rotate(early, "tm", 1), rotate(late, "tm", 1)), (kernel_grad,))
    kernel_grad = jnp.transpose(kernel_grad.reshape(taps, rows, channels), (1, 0, 2))
    return (conv_out, feature_grad, kernel_grad)


def local(features, kernel, cotangent):
    rows, clips, _, pixels = features.shape
    fits = (
        clips == 1
        and lax.axis_size("tm") == 2
        and lax.axis_size("dp") == 2
        and rows % (2 * SUB) == 0
        and pixels % 128 == 0
        and kernel.shape[1] == 27
        and lax.axis_size("chan") == 4
    )
    return (local_fast if fits else local_generic)(features, kernel, cotangent)


def solution(mesh):
    return jax.shard_map(
        local,
        mesh=mesh,
        in_specs=(
            P("chan", ("groups", "dp"), "tm", None),
            P("chan", None, None),
            P("chan", ("groups", "dp"), "tm", None),
        ),
        out_specs=(
            P("chan", ("groups", "dp"), "tm", None),
            P("chan", ("groups", "dp"), "tm", None),
            P(("groups", "chan"), None, None),
        ),
        check_vma=False,
    )
```

```python
import functools
import math

import jax
import jax.numpy as jnp
from jax import lax
from jax.experimental import pallas as pl
from jax.experimental.pallas import tpu as pltpu
from jax.sharding import PartitionSpec as P

WID = 64
SUB = 16
F32 = jnp.float32
BF16 = jnp.bfloat16
VMEM_LIMIT = 24 * 1024 * 1024
TOKEN = (8, 128)
FEATURE_COST = 3 * 10**9
FAR_COST = 10**9
NEAR_COST = 3 * 10**9


def from_behind(x, axis, by):
    size = lax.axis_size(axis)
    pairs = [(i, i + by) for i in range(size) if 0 <= i + by < size]
    return lax.ppermute(x, axis, pairs)


def padded_copies(block):
    pixels = block.shape[-1]
    column = lax.broadcasted_iota(jnp.int32, (pixels,), 0) % WID
    nothing = jnp.zeros((), block.dtype)
    widths = [(0, 0), (0, 0), (0, 0), (WID + 1, WID + 1)]
    left_cut = jnp.pad(jnp.where(column == WID - 1, nothing, block), widths)
    untouched = jnp.pad(block, widths)
    right_cut = jnp.pad(jnp.where(column == 0, nothing, block), widths)
    return (left_cut, untouched, right_cut)


def tap_window(copies, first_frame, vertical, horizontal, frames, pixels):
    source = copies[horizontal]
    offset = vertical * WID + horizontal
    return source[:, :, first_frame : first_frame + frames, offset : offset + pixels]


def stacked_taps(copies, first_frame, flipped, frames, pixels):
    pieces = []
    for vertical in range(3):
        for horizontal in range(3):
            if flipped:
                pieces.append(
                    tap_window(copies, first_frame, 2 - vertical, 2 - horizontal, frames, pixels)
                )
            else:
                pieces.append(tap_window(copies, first_frame, vertical, horizontal, frames, pixels))
    concatenated = jnp.concatenate(pieces, axis=0)
    return concatenated.reshape(concatenated.shape[0], -1)


def local_generic(features, kernel, cotangent):
    channels, clip_count, frames, pixels = features.shape
    flat_length = clip_count * frames * pixels
    widened = features.astype(F32)
    logistic = jax.nn.sigmoid(widened)
    activation = (widened * logistic).astype(BF16)
    slope_factor = logistic * (1.0 + widened * (1.0 - logistic))
    earlier = from_behind(activation[:, :, frames - 2 :, :], "tm", 1)
    extended = jnp.concatenate([earlier, activation], axis=2)
    upcoming = from_behind(cotangent[:, :, :2, :], "tm", -1)
    later_padded = jnp.concatenate([cotangent, upcoming], axis=2)
    cotangent_rows = cotangent.reshape(channels, -1)
    portion = lax.all_gather(extended, "chan", axis=0, tiled=True)
    out_sum = jnp.zeros((channels, flat_length), F32)
    amount = portion.shape[0]
    copies = padded_copies(portion)
    grad_parts = []
    for temporal in range(3):
        stacked = stacked_taps(copies, temporal, False, frames, pixels)
        weights = kernel[:, 9 * temporal : 9 * temporal + 9, :].reshape(channels, 9 * amount)
        out_sum = out_sum + jnp.dot(weights, stacked, preferred_element_type=F32)
        grad_parts.append(
            lax.dot_general(
                cotangent_rows, stacked, (((1,), (1,)), ((), ())), preferred_element_type=F32
            ).reshape(channels, 9, amount)
        )
    grad_sum = jnp.concatenate(grad_parts, axis=1)
    conv_out = out_sum.reshape(features.shape).astype(BF16)
    position_count = lax.axis_size("dp") * lax.axis_size("tm") * flat_length
    kernel_grad = lax.psum(grad_sum, ("tm", "dp")) * (1.0 / math.sqrt(position_count))
    padded_later = padded_copies(later_padded)
    summed = jnp.zeros((amount, flat_length), F32)
    for temporal in range(3):
        weights = jnp.transpose(
            kernel[:, 9 * temporal : 9 * temporal + 9, :], (2, 1, 0)
        ).reshape(amount, 9 * channels)
        stacked = stacked_taps(padded_later, 2 - temporal, True, frames, pixels)
        summed = summed + jnp.dot(weights, stacked, preferred_element_type=F32)
    before_slope = lax.psum_scatter(
        summed.reshape(amount, clip_count, frames, pixels), "chan", scatter_dimension=0, tiled=True
    )
    feature_grad = (before_slope * slope_factor).astype(BF16)
    return (conv_out, feature_grad, kernel_grad)


def rotate(x, axis, by):
    size = lax.axis_size(axis)
    return lax.ppermute(x, axis, [(i, (i + by) % size) for i in range(size)])


def shifted(frame, down, right):
    pixels = frame.shape[-1]
    if down == 0 and right == 0:
        return frame
    cell = lax.broadcasted_iota(jnp.int32, (1, pixels), 1)
    row, column = cell // WID + down, cell % WID + right
    inside = (row >= 0) & (row < pixels // WID) & (column >= 0) & (column < WID)
    moved = pltpu.roll(frame, (-(down * WID + right)) % pixels, 1)
    return jnp.where(inside, moved, 0.0)


def after(x, *others, flops=1):
    anywhere = pl.BlockSpec(memory_space=pl.ANY)
    return pl.pallas_call(
        lambda *refs: None,
        out_shape=jax.ShapeDtypeStruct(x.shape, x.dtype),
        in_specs=[anywhere] * (1 + len(others)),
        out_specs=anywhere,
        input_output_aliases={0: 0},
        compiler_params=pltpu.CompilerParams(vmem_limit_bytes=1024 * 1024),
        cost_estimate=cost(flops),
        name="hand_on",
    )(x, *others)


def run(kernel, args, waits=(), **options):
    options.setdefault("in_specs", [whole()] * len(args))
    options.setdefault("cost_estimate", cost())
    options["in_specs"] = list(options["in_specs"]) + [
        pl.BlockSpec(memory_space=pl.ANY) for _ in waits
    ]
    count = len(args)

    def body(*refs):
        kernel(*refs[:count], *refs[count + len(waits) :])

    return pl.pallas_call(
        body, compiler_params=pltpu.CompilerParams(vmem_limit_bytes=VMEM_LIMIT), **options
    )(*args, *waits)


def cost(flops=1):
    return pl.CostEstimate(flops=flops, bytes_accessed=1, transcendentals=0)


def whole():
    return pl.BlockSpec(memory_space=pltpu.VMEM)


def activate_kernel(features, cotangent, activation, flat, feat, cot, sems):
    parts = sems.shape[1]
    rows, _, frames, pixels = feat.shape
    size = rows // parts
    loads = []
    for n, (source, target) in enumerate(((features, feat), (cotangent, cot))):
        for part in range(parts):
            at = pl.ds(part * size, size)
            loads.append(pltpu.make_async_copy(source.at[at], target.at[at], sems.at[n, part]))
    for load in loads:
        load.start()
    for part in range(parts):
        loads[part].wait()
        at = slice(part * size, (part + 1) * size)
        v = feat[at, 0].astype(F32)
        act = v / (1.0 + jnp.exp(-v))
        for t in range(frames):
            activation[at, t * pixels : (t + 1) * pixels] = act[:, t, :].astype(BF16)
    for load in loads[parts:]:
        load.wait()
    flatten(pixels, cot, flat, 0)


def flatten(pixels, source, flat, first):
    wide = source[:, 0].astype(F32)
    for t in range(wide.shape[1]):
        at = (first + t) * pixels
        at = at if isinstance(at, int) else pl.multiple_of(at, pixels)
        flat[:, pl.ds(at, pixels)] = wide[:, t, :]


def shard_at(count, k):
    z = lax.axis_index("chan")
    return (z, z + 1 - 2 * lax.rem(z, 2), lax.rem(z + 2, count), count - 1 - z)[k]


def in_slot(channels, rows, slot):
    lane = lax.broadcasted_iota(jnp.int32, (1, channels), 1)
    return (lane >= slot * rows) & (lane < (slot + 1) * rows)


def packed_rows(total):
    unit = total // 9
    return 7 * unit, 2 * unit


def fill_stack(pixels, flat, stack, half, first, frames):
    unit = flat.shape[0] // 2
    for t in range(frames):
        at = slice(t * pixels, (t + 1) * pixels)
        source = slice((first + t) * pixels, (first + t + 1) * pixels)
        for q in range(9):
            tap, part = divmod(9 * half + q, 2)
            i, j = divmod(tap, 3)
            frame = flat[part * unit : (part + 1) * unit, source]
            stack[q * unit : (q + 1) * unit, at] = shifted(frame, 1 - i, 1 - j).astype(BF16)


def block_terms(pixels, k, stack, here, there, out, rhs):
    channels = out.shape[1]
    rows, length = here.shape
    lanes, count = 2 * length, channels // rows
    shard = shard_at(count, k)
    for core in range(2):

        @pl.when(lax.axis_index("tm") == core)
        def _(first=(here, there)[core], second=(there, here)[core]):
            for a in range(3):
                skip = (2 - a) * pixels
                at = pl.ds(pl.multiple_of(lax.rem(shard + a, count) * rows, SUB), rows)
                if skip:
                    rhs[at, :skip] = jnp.zeros((rows, skip), BF16)
                rhs[at, skip : skip + length] = first[...]
                rhs[at, skip + length :] = second[:, : length - skip]

    last = lax.rem(shard + 3, count)
    rhs[pl.ds(pl.multiple_of(last * rows, SUB), rows), :] = jnp.zeros((rows, lanes), BF16)
    terms = lax.dot_general(
        stack[...], rhs[...], (((1,), (1,)), ((), ())), preferred_element_type=F32
    )
    main, tail = packed_rows(terms.shape[0])
    free = in_slot(channels, rows, last)
    for a in range(3):
        at = slice(a * tail, (a + 1) * tail)
        moved = pltpu.roll(terms[main:], (3 - a) * rows, 1)
        out[at, :] = jnp.where(free, moved, terms[at]).astype(BF16)
    out[3 * tail :, :] = terms[3 * tail : main].astype(BF16)


def own_terms_kernel(
    pixels, mine, other, flat_own, cot_other, weights, out, stack, flat, held, rhs, sems
):
    load = pltpu.make_async_copy(weights, held, sems.at[0])
    load.start()
    length = flat_own.shape[1]
    me = lax.axis_index("tm")
    flat[:, pl.ds(pl.multiple_of(me * length, pixels), length)] = flat_own[...]
    flatten(pixels, cot_other, flat, (1 - me) * (length // pixels))
    for core in range(2):

        @pl.when(me == core)
        def _(core=core):
            fill_stack(pixels, flat, stack, core, 0, flat.shape[1] // pixels)

    block_terms(pixels, 0, stack, mine, other, out, rhs)
    load.wait()


def terms_kernel(pixels, k, stack, here, there, out, rhs):
    block_terms(pixels, k, stack, here, there, out, rhs)


def share_kernel(pixels, weights, flat, mine, own, kept, near, passed, window, other, total):
    rows, length = own.shape
    frames, half = length // pixels, mine.shape[0]
    count = weights.shape[1] // rows
    me = lax.axis_index("tm")
    front = 2 * pixels
    for core in range(2):

        @pl.when(me == core)
        def _(core=core):
            first = core * length
            held = min(length + front, mine.shape[1] - first)
            window[:, :held] = mine[:, first : first + held]
            if held < length + front:
                window[:, held:] = jnp.zeros((half, length + front - held), BF16)
                other[:, held:] = jnp.zeros((half, length + front - held), BF16)
            fill_stack(pixels, flat, other, 1 - core, core * frames, held // pixels)

    acc = None
    for a in range(3):
        lanes = slice((2 - a) * pixels, (2 - a) * pixels + length)
        for which, stack in ((me, window), (1 - me, other)):
            at = pl.multiple_of((2 * a + which) * half, SUB)
            term = lax.dot_general(
                weights[pl.ds(at, half), :],
                stack[:, lanes],
                (((0,), (0,)), ((), ())),
                preferred_element_type=F32,
            )
            acc = term if acc is None else acc + term
    total[...] = acc

    def part(k):
        return total[pl.ds(pl.multiple_of(shard_at(count, k) * rows, SUB), rows), :]

    own[...] = part(0)
    kept[...] = part(2)
    near[...] = part(1).astype(BF16)
    passed[...] = part(3).astype(BF16)


def pack_kernel(block, share, out, message):
    out[...] = block[...]
    message[0] = block[...]
    message[1] = share[...]


def unpack_kernel(message, block, share):
    block[...] = message[0]
    share[...] = message[1]


def add_kernel(kept, came, out):
    out[...] = (kept[...] + came[...].astype(F32)).astype(out.dtype)


def conv_kernel(pixels, weights, *refs):
    blocks, (out, token, act) = refs[:-3], refs[-3:]
    token[...] = jnp.zeros(TOKEN, F32)
    rows, _, frames, _ = out.shape
    count = weights.shape[1] // rows
    length, front = frames * pixels, 2 * pixels
    me = lax.axis_index("tm")
    for k in range(count):
        here, there = blocks[2 * k], blocks[2 * k + 1]
        at = pl.ds(pl.multiple_of(shard_at(count, k) * rows, SUB), rows)
        earlier = there[:, length - front :]
        act[at, :front] = jnp.where(me == 0, jnp.zeros_like(earlier), earlier)
        act[at, front:] = here[...]

    taps = 9 * rows
    for t in range(frames):
        z_t = None
        for a in range(3):
            term = jnp.dot(
                weights[a * taps : (a + 1) * taps, :],
                act[:, (t + a) * pixels : (t + a + 1) * pixels],
                preferred_element_type=F32,
            )
            z_t = term if z_t is None else z_t + term
        acc = None
        for i in range(3):
            for j in range(3):
                at = (3 * i + j) * rows
                moved = shifted(z_t[at : at + rows, :], i - 1, j - 1)
                acc = moved if acc is None else acc + moved
        out[:, 0, t, :] = acc.astype(BF16)


def slope_kernel(pixels, features, slope):
    v = features[:, 0].astype(F32)
    s = 1.0 / (1.0 + jnp.exp(-v))
    factor = s * (1.0 + v * (1.0 - s))
    for t in range(factor.shape[1]):
        slope[:, t * pixels : (t + 1) * pixels] = factor[:, t, :]


def feature_kernel(pixels, slope, own, first, second, out, token):
    token[...] = jnp.zeros(TOKEN, F32)
    total = (own[...] + first[...].astype(F32) + second[...].astype(F32)) * slope[...]
    for t in range(out.shape[2]):
        out[:, 0, t, :] = total[:, t * pixels : (t + 1) * pixels].astype(BF16)


def sum_kernel(main, *refs):
    out, ins = refs[-1], refs[:-1]
    count = len(ins) // 2
    for k in range(count):
        total = ins[k][...].astype(F32) + ins[count + k][...].astype(F32)
        out[k * main : (k + 1) * main, :] = total.astype(BF16)


def finish_kernel(scale, main, whose, early, late, *refs):
    out, laid, sems = refs[-3:]
    channels = out.shape[2]
    first = early.shape[0] // main
    count = first + late.shape[0] // main
    rows, half = channels // count, out.shape[1] // 2
    unit = rows // 2
    which = lax.rem(lax.axis_index("tm") + whose, 2)
    at = pl.ds(pl.multiple_of(which * half, 8), half)
    shards = [shard_at(count, k) for k in range(count)]
    copies = []
    for a in range(3):
        for q in range(9):
            base = q * unit if q < 7 else a * 2 * unit + (q - 7) * unit
            step = a if q < 7 else 3
            total = None
            for k, shard in enumerate(shards):
                source, place = (early, k) if k < first else (late, k - first)
                piece = source[place * main + base : place * main + base + unit, :]
                mask = in_slot(channels, rows, lax.rem(shard + step, count))
                total = piece if total is None else jnp.where(mask, piece, total)
            total = total.astype(F32) * scale
            if step:
                total = pltpu.roll(total, channels - step * rows, 1)
            laid[a, q * unit : (q + 1) * unit, :] = total
        copy = pltpu.make_async_copy(laid.at[a], out.at[a, at], sems.at[a])
        copy.start()
        copies.append(copy)
    for copy in copies:
        copy.wait()


def in_place(x):
    return pltpu.with_memory_space_constraint(x, pltpu.HBM)


def local_fast(features, kernel, cotangent):
    rows, _, frames, pixels = features.shape
    length = frames * pixels
    count = lax.axis_size("chan")
    channels = rows * count
    taps = kernel.shape[1]
    half = 9 * rows // 2
    main, _ = packed_rows(half)
    sds = jax.ShapeDtypeStruct
    block_shape = sds((rows, length), BF16)
    term_shape = sds((main, channels), BF16)
    stack_shape = sds((half, 2 * length), BF16)
    rhs = pltpu.VMEM((channels, 2 * length), BF16)

    def swap(x, far):
        return lax.ppermute(x, "chan", [(z, z ^ far) for z in range(count)])

    weights = jnp.transpose(kernel, (1, 0, 2)).reshape(taps * rows, channels)
    hbm = pl.BlockSpec(memory_space=pltpu.HBM)
    cot_other = rotate(cotangent, "tm", 1)
    activation, flat_own = run(
        activate_kernel,
        (in_place(features), in_place(cotangent)),
        in_specs=[hbm] * 2,
        out_shape=(block_shape, sds((rows, length), F32)),
        out_specs=(whole(),) * 2,
        scratch_shapes=[
            pltpu.VMEM(features.shape, BF16),
            pltpu.VMEM(features.shape, BF16),
            pltpu.SemaphoreType.DMA((2, 3)),
        ],
        name="activate",
    )
    other = rotate(activation, "tm", 1)
    near, far = swap(activation, 1), swap(activation, 2)
    own_term, stack, flat, weights = run(
        functools.partial(own_terms_kernel, pixels),
        (activation, other, flat_own, cot_other, in_place(weights)),
        in_specs=[whole()] * 4 + [hbm],
        out_shape=(
            term_shape,
            stack_shape,
            sds((rows, 2 * length), F32),
            sds(weights.shape, BF16),
        ),
        out_specs=(whole(),) * 4,
        scratch_shapes=[rhs, pltpu.SemaphoreType.DMA((1,))],
        name="own_terms",
    )
    terms, got = [own_term], [rotate(own_term, "dp", 1)]
    blocks = [activation, other]

    def terms_of(k, here, there, waits=()):
        blocks.extend((here, there))
        term = run(
            functools.partial(terms_kernel, pixels, k),
            (stack, *blocks[-2:]),
            waits=waits,
            out_shape=term_shape,
            out_specs=whole(),
            scratch_shapes=[rhs],
            name=f"terms_{k}",
        )
        terms.append(term)
        got.append(rotate(term, "dp", 1))
        return term

    own_share, kept, near_share, passed_share = run(
        functools.partial(share_kernel, pixels),
        (weights, flat, stack),
        waits=(own_term,),
        out_shape=(
            sds((rows, length), F32),
            sds((rows, length), F32),
            block_shape,
            block_shape,
        ),
        out_specs=(whole(),) * 4,
        scratch_shapes=[
            pltpu.VMEM((half, (frames + 2) * pixels), BF16),
            pltpu.VMEM((half, (frames + 2) * pixels), BF16),
            pltpu.VMEM((channels, length), F32),
        ],
        name="shares",
    )
    first_share = swap(near_share, 1)
    near = after(near, own_share, flops=NEAR_COST)
    far, message = run(
        pack_kernel,
        (far, passed_share),
        out_shape=(block_shape, sds((2, rows, length), BF16)),
        out_specs=(whole(),) * 2,
        cost_estimate=cost(FAR_COST),
        name="pack",
    )
    message = swap(message, 1)
    term = terms_of(1, near, rotate(near, "tm", 1), (own_share, far, got[0]))
    term = terms_of(2, far, rotate(far, "tm", 1), (term,))
    slope = run(
        functools.partial(slope_kernel, pixels),
        (features,),
        waits=(term,),
        out_shape=sds((rows, length), F32),
        out_specs=whole(),
        name="slope",
    )
    last, passed_share = run(
        unpack_kernel,
        (message,),
        waits=(slope, got[1]),
        out_shape=(block_shape, block_shape),
        out_specs=(whole(),) * 2,
        name="unpack",
    )
    carry = run(
        add_kernel,
        (kept, passed_share),
        out_shape=block_shape,
        out_specs=whole(),
        name="carry_share",
    )
    second_share = swap(carry, 2)
    term = terms_of(3, last, rotate(last, "tm", 1), (carry,))

    def sums(first, stop, waits=()):
        return run(
            functools.partial(sum_kernel, main),
            (*terms[first:stop], *got[first:stop]),
            waits=waits,
            out_shape=sds(((stop - first) * main, channels), BF16),
            out_specs=whole(),
            name=f"sums_{first}",
        )

    conv_out, token = run(
        functools.partial(conv_kernel, pixels),
        (weights, *blocks),
        waits=(term, got[2]),
        out_shape=(sds(features.shape, BF16), sds(TOKEN, F32)),
        out_specs=(whole(),) * 2,
        scratch_shapes=[pltpu.VMEM((channels, (frames + 2) * pixels), BF16)],
        name="conv",
    )
    early = sums(0, 2, (term,))
    feature_grad, token = run(
        functools.partial(feature_kernel, pixels),
        (slope, own_share, first_share, second_share),
        waits=(token, early),
        out_shape=(sds(features.shape, BF16), sds(TOKEN, F32)),
        out_specs=(whole(),) * 2,
        cost_estimate=cost(FEATURE_COST),
        name="feature_grad",
    )
    late = sums(2, count, (token,))
    scale = 1.0 / math.sqrt(lax.axis_size("dp") * lax.axis_size("tm") * length)

    def finish(whose, sums, base=()):
        anywhere = pl.BlockSpec(memory_space=pl.ANY)
        return run(
            functools.partial(finish_kernel, scale, main, whose),
            (*sums, *base),
            in_specs=[whole()] * 2 + [anywhere] * len(base),
            out_shape=sds((3, 9 * rows, channels), F32),
            out_specs=anywhere,
            input_output_aliases={2: 0} if base else {},
            scratch_shapes=[pltpu.VMEM((3, half, channels), F32), pltpu.SemaphoreType.DMA((3,))],
            name=f"kernel_grad_{whose}",
        )

    kernel_grad = finish(0, (early, late))
    kernel_grad = finish(1, (rotate(early, "tm", 1), rotate(late, "tm", 1)), (kernel_grad,))
    kernel_grad = jnp.transpose(kernel_grad.reshape(taps, rows, channels), (1, 0, 2))
    return (conv_out, feature_grad, kernel_grad)


def local(features, kernel, cotangent):
    rows, clips, _, pixels = features.shape
    fits = (
        clips == 1
        and lax.axis_size("tm") == 2
        and lax.axis_size("dp") == 2
        and rows % (2 * SUB) == 0
        and pixels % 128 == 0
        and kernel.shape[1] == 27
        and lax.axis_size("chan") == 4
    )
    return (local_fast if fits else local_generic)(features, kernel, cotangent)


def solution(mesh):
    return jax.shard_map(
        local,
        mesh=mesh,
        in_specs=(
            P("chan", ("groups", "dp"), "tm", None),
            P("chan", None, None),
            P("chan", ("groups", "dp"), "tm", None),
        ),
        out_specs=(
            P("chan", ("groups", "dp"), "tm", None),
            P("chan", ("groups", "dp"), "tm", None),
            P(("groups", "chan"), None, None),
        ),
        check_vma=False,
    )
```

```python
import functools
import math

import jax
import jax.numpy as jnp
from jax import lax
from jax.experimental import pallas as pl
from jax.experimental.pallas import tpu as pltpu
from jax.sharding import PartitionSpec as P

WID = 64
SUB = 16
F32 = jnp.float32
BF16 = jnp.bfloat16
VMEM_LIMIT = 24 * 1024 * 1024
TOKEN = (8, 128)
FEATURE_COST = 3 * 10**9
GATHER_COST = 10**8
FAR_COST = 10**9
NEAR_COST = 3 * 10**9


def from_behind(x, axis, by):
    size = lax.axis_size(axis)
    pairs = [(i, i + by) for i in range(size) if 0 <= i + by < size]
    return lax.ppermute(x, axis, pairs)


def padded_copies(block):
    pixels = block.shape[-1]
    column = lax.broadcasted_iota(jnp.int32, (pixels,), 0) % WID
    nothing = jnp.zeros((), block.dtype)
    widths = [(0, 0), (0, 0), (0, 0), (WID + 1, WID + 1)]
    left_cut = jnp.pad(jnp.where(column == WID - 1, nothing, block), widths)
    untouched = jnp.pad(block, widths)
    right_cut = jnp.pad(jnp.where(column == 0, nothing, block), widths)
    return (left_cut, untouched, right_cut)


def tap_window(copies, first_frame, vertical, horizontal, frames, pixels):
    source = copies[horizontal]
    offset = vertical * WID + horizontal
    return source[:, :, first_frame : first_frame + frames, offset : offset + pixels]


def stacked_taps(copies, first_frame, flipped, frames, pixels):
    pieces = []
    for vertical in range(3):
        for horizontal in range(3):
            if flipped:
                pieces.append(
                    tap_window(copies, first_frame, 2 - vertical, 2 - horizontal, frames, pixels)
                )
            else:
                pieces.append(tap_window(copies, first_frame, vertical, horizontal, frames, pixels))
    concatenated = jnp.concatenate(pieces, axis=0)
    return concatenated.reshape(concatenated.shape[0], -1)


def local_generic(features, kernel, cotangent):
    channels, clip_count, frames, pixels = features.shape
    flat_length = clip_count * frames * pixels
    widened = features.astype(F32)
    logistic = jax.nn.sigmoid(widened)
    activation = (widened * logistic).astype(BF16)
    slope_factor = logistic * (1.0 + widened * (1.0 - logistic))
    earlier = from_behind(activation[:, :, frames - 2 :, :], "tm", 1)
    extended = jnp.concatenate([earlier, activation], axis=2)
    upcoming = from_behind(cotangent[:, :, :2, :], "tm", -1)
    later_padded = jnp.concatenate([cotangent, upcoming], axis=2)
    cotangent_rows = cotangent.reshape(channels, -1)
    portion = lax.all_gather(extended, "chan", axis=0, tiled=True)
    out_sum = jnp.zeros((channels, flat_length), F32)
    amount = portion.shape[0]
    copies = padded_copies(portion)
    grad_parts = []
    for temporal in range(3):
        stacked = stacked_taps(copies, temporal, False, frames, pixels)
        weights = kernel[:, 9 * temporal : 9 * temporal + 9, :].reshape(channels, 9 * amount)
        out_sum = out_sum + jnp.dot(weights, stacked, preferred_element_type=F32)
        grad_parts.append(
            lax.dot_general(
                cotangent_rows, stacked, (((1,), (1,)), ((), ())), preferred_element_type=F32
            ).reshape(channels, 9, amount)
        )
    grad_sum = jnp.concatenate(grad_parts, axis=1)
    conv_out = out_sum.reshape(features.shape).astype(BF16)
    position_count = lax.axis_size("dp") * lax.axis_size("tm") * flat_length
    kernel_grad = lax.psum(grad_sum, ("tm", "dp")) * (1.0 / math.sqrt(position_count))
    padded_later = padded_copies(later_padded)
    summed = jnp.zeros((amount, flat_length), F32)
    for temporal in range(3):
        weights = jnp.transpose(
            kernel[:, 9 * temporal : 9 * temporal + 9, :], (2, 1, 0)
        ).reshape(amount, 9 * channels)
        stacked = stacked_taps(padded_later, 2 - temporal, True, frames, pixels)
        summed = summed + jnp.dot(weights, stacked, preferred_element_type=F32)
    before_slope = lax.psum_scatter(
        summed.reshape(amount, clip_count, frames, pixels), "chan", scatter_dimension=0, tiled=True
    )
    feature_grad = (before_slope * slope_factor).astype(BF16)
    return (conv_out, feature_grad, kernel_grad)


def rotate(x, axis, by):
    size = lax.axis_size(axis)
    return lax.ppermute(x, axis, [(i, (i + by) % size) for i in range(size)])


def shifted(frame, down, right):
    pixels = frame.shape[-1]
    if down == 0 and right == 0:
        return frame
    cell = lax.broadcasted_iota(jnp.int32, (1, pixels), 1)
    row, column = cell // WID + down, cell % WID + right
    inside = (row >= 0) & (row < pixels // WID) & (column >= 0) & (column < WID)
    moved = pltpu.roll(frame, (-(down * WID + right)) % pixels, 1)
    return jnp.where(inside, moved, 0.0)


def after(x, *others, flops=1):
    anywhere = pl.BlockSpec(memory_space=pl.ANY)
    return pl.pallas_call(
        lambda *refs: None,
        out_shape=jax.ShapeDtypeStruct(x.shape, x.dtype),
        in_specs=[anywhere] * (1 + len(others)),
        out_specs=anywhere,
        input_output_aliases={0: 0},
        compiler_params=pltpu.CompilerParams(vmem_limit_bytes=1024 * 1024),
        cost_estimate=cost(flops),
        name="hand_on",
    )(x, *others)


def run(kernel, args, waits=(), **options):
    options.setdefault("in_specs", [whole()] * len(args))
    options.setdefault("cost_estimate", cost())
    options["in_specs"] = list(options["in_specs"]) + [
        pl.BlockSpec(memory_space=pl.ANY) for _ in waits
    ]
    count = len(args)

    def body(*refs):
        kernel(*refs[:count], *refs[count + len(waits) :])

    return pl.pallas_call(
        body, compiler_params=pltpu.CompilerParams(vmem_limit_bytes=VMEM_LIMIT), **options
    )(*args, *waits)


def cost(flops=1):
    return pl.CostEstimate(flops=flops, bytes_accessed=1, transcendentals=0)


def whole():
    return pl.BlockSpec(memory_space=pltpu.VMEM)


def activate_kernel(features, cotangent, activation, flat, feat, cot, sems):
    parts = sems.shape[1]
    rows, _, frames, pixels = feat.shape
    size = rows // parts
    loads = []
    for n, (source, target) in enumerate(((features, feat), (cotangent, cot))):
        for part in range(parts):
            at = pl.ds(part * size, size)
            loads.append(pltpu.make_async_copy(source.at[at], target.at[at], sems.at[n, part]))
    for load in loads:
        load.start()
    for part in range(parts):
        loads[part].wait()
        at = slice(part * size, (part + 1) * size)
        v = feat[at, 0].astype(F32)
        act = v / (1.0 + jnp.exp(-v))
        for t in range(frames):
            activation[at, t * pixels : (t + 1) * pixels] = act[:, t, :].astype(BF16)
    for load in loads[parts:]:
        load.wait()
    flatten(pixels, cot, flat, 0)


def flatten(pixels, source, flat, first):
    wide = source[:, 0].astype(F32)
    for t in range(wide.shape[1]):
        at = (first + t) * pixels
        at = at if isinstance(at, int) else pl.multiple_of(at, pixels)
        flat[:, pl.ds(at, pixels)] = wide[:, t, :]


def shard_at(count, k):
    z = lax.axis_index("chan")
    return (z, z + 1 - 2 * lax.rem(z, 2), lax.rem(z + 2, count), count - 1 - z)[k]


def in_slot(channels, rows, slot):
    lane = lax.broadcasted_iota(jnp.int32, (1, channels), 1)
    return (lane >= slot * rows) & (lane < (slot + 1) * rows)


def packed_rows(total):
    unit = total // 9
    return 7 * unit, 2 * unit


def fill_stack(pixels, flat, stack, half, first, frames):
    unit = flat.shape[0] // 2
    for t in range(frames):
        at = slice(t * pixels, (t + 1) * pixels)
        source = slice((first + t) * pixels, (first + t + 1) * pixels)
        for q in range(9):
            tap, part = divmod(9 * half + q, 2)
            i, j = divmod(tap, 3)
            frame = flat[part * unit : (part + 1) * unit, source]
            stack[q * unit : (q + 1) * unit, at] = shifted(frame, 1 - i, 1 - j).astype(BF16)


def block_terms(pixels, k, stack, here, there, out, rhs):
    channels = out.shape[1]
    rows, length = here.shape
    lanes, count = 2 * length, channels // rows
    shard = shard_at(count, k)
    for core in range(2):

        @pl.when(lax.axis_index("tm") == core)
        def _(first=(here, there)[core], second=(there, here)[core]):
            for a in range(3):
                skip = (2 - a) * pixels
                at = pl.ds(pl.multiple_of(lax.rem(shard + a, count) * rows, SUB), rows)
                if skip:
                    rhs[at, :skip] = jnp.zeros((rows, skip), BF16)
                rhs[at, skip : skip + length] = first[...]
                rhs[at, skip + length :] = second[:, : length - skip]

    last = lax.rem(shard + 3, count)
    rhs[pl.ds(pl.multiple_of(last * rows, SUB), rows), :] = jnp.zeros((rows, lanes), BF16)
    terms = lax.dot_general(
        stack[...], rhs[...], (((1,), (1,)), ((), ())), preferred_element_type=F32
    )
    main, tail = packed_rows(terms.shape[0])
    free = in_slot(channels, rows, last)
    for a in range(3):
        at = slice(a * tail, (a + 1) * tail)
        moved = pltpu.roll(terms[main:], (3 - a) * rows, 1)
        out[at, :] = jnp.where(free, moved, terms[at]).astype(BF16)
    out[3 * tail :, :] = terms[3 * tail : main].astype(BF16)


def own_terms_kernel(
    pixels, mine, other, flat_own, cot_other, weights, out, stack, flat, held, rhs, sems
):
    load = pltpu.make_async_copy(weights, held, sems.at[0])
    load.start()
    length = flat_own.shape[1]
    me = lax.axis_index("tm")
    flat[:, pl.ds(pl.multiple_of(me * length, pixels), length)] = flat_own[...]
    flatten(pixels, cot_other, flat, (1 - me) * (length // pixels))
    for core in range(2):

        @pl.when(me == core)
        def _(core=core):
            fill_stack(pixels, flat, stack, core, 0, flat.shape[1] // pixels)

    block_terms(pixels, 0, stack, mine, other, out, rhs)
    load.wait()


def terms_kernel(pixels, k, stack, here, there, out, rhs):
    block_terms(pixels, k, stack, here, there, out, rhs)


def share_kernel(pixels, weights, flat, mine, own, kept, near, passed, window, other, total):
    rows, length = own.shape
    frames, half = length // pixels, mine.shape[0]
    count = weights.shape[1] // rows
    me = lax.axis_index("tm")
    front = 2 * pixels
    for core in range(2):

        @pl.when(me == core)
        def _(core=core):
            first = core * length
            held = min(length + front, mine.shape[1] - first)
            window[:, :held] = mine[:, first : first + held]
            if held < length + front:
                window[:, held:] = jnp.zeros((half, length + front - held), BF16)
                other[:, held:] = jnp.zeros((half, length + front - held), BF16)
            fill_stack(pixels, flat, other, 1 - core, core * frames, held // pixels)

    acc = None
    for a in range(3):
        lanes = slice((2 - a) * pixels, (2 - a) * pixels + length)
        for which, stack in ((me, window), (1 - me, other)):
            at = pl.multiple_of((2 * a + which) * half, SUB)
            term = lax.dot_general(
                weights[pl.ds(at, half), :],
                stack[:, lanes],
                (((0,), (0,)), ((), ())),
                preferred_element_type=F32,
            )
            acc = term if acc is None else acc + term
    total[...] = acc

    def part(k):
        return total[pl.ds(pl.multiple_of(shard_at(count, k) * rows, SUB), rows), :]

    own[...] = part(0)
    kept[...] = part(2)
    near[...] = part(1).astype(BF16)
    passed[...] = part(3).astype(BF16)


def pack_kernel(block, share, out, message):
    out[...] = block[...]
    message[0] = block[...]
    message[1] = share[...]


def unpack_kernel(message, block, share):
    block[...] = message[0]
    share[...] = message[1]


def add_kernel(kept, came, out):
    out[...] = (kept[...] + came[...].astype(F32)).astype(out.dtype)


def conv_kernel(pixels, weights, *refs):
    blocks, (out, token, act) = refs[:-3], refs[-3:]
    token[...] = jnp.zeros(TOKEN, F32)
    rows, _, frames, _ = out.shape
    count = weights.shape[1] // rows
    length, front = frames * pixels, 2 * pixels
    me = lax.axis_index("tm")
    for k in range(count):
        here, there = blocks[2 * k], blocks[2 * k + 1]
        at = pl.ds(pl.multiple_of(shard_at(count, k) * rows, SUB), rows)
        earlier = there[:, length - front :]
        act[at, :front] = jnp.where(me == 0, jnp.zeros_like(earlier), earlier)
        act[at, front:] = here[...]

    taps = 9 * rows
    for t in range(frames):
        z_t = None
        for a in range(3):
            term = jnp.dot(
                weights[a * taps : (a + 1) * taps, :],
                act[:, (t + a) * pixels : (t + a + 1) * pixels],
                preferred_element_type=F32,
            )
            z_t = term if z_t is None else z_t + term
        acc = None
        for i in range(3):
            for j in range(3):
                at = (3 * i + j) * rows
                moved = shifted(z_t[at : at + rows, :], i - 1, j - 1)
                acc = moved if acc is None else acc + moved
        out[:, 0, t, :] = acc.astype(BF16)


def slope_kernel(pixels, features, slope):
    v = features[:, 0].astype(F32)
    s = 1.0 / (1.0 + jnp.exp(-v))
    factor = s * (1.0 + v * (1.0 - s))
    for t in range(factor.shape[1]):
        slope[:, t * pixels : (t + 1) * pixels] = factor[:, t, :]


def gather_share_kernel(own, second, out):
    out[...] = own[...] + second[...].astype(F32)


def feature_kernel(pixels, slope, gathered, first, out, token):
    token[...] = jnp.zeros(TOKEN, F32)
    total = (gathered[...] + first[...].astype(F32)) * slope[...]
    frames = [total[:, t * pixels : (t + 1) * pixels] for t in range(out.shape[2])]
    out[:, 0] = jnp.stack(frames, axis=1).astype(BF16)


def sum_kernel(main, *refs):
    out, ins = refs[-1], refs[:-1]
    count = len(ins) // 2
    for k in range(count):
        total = ins[k][...].astype(F32) + ins[count + k][...].astype(F32)
        out[k * main : (k + 1) * main, :] = total.astype(BF16)


def finish_kernel(scale, main, whose, early, late, *refs):
    out, laid, sems = refs[-3:]
    channels = out.shape[2]
    first = early.shape[0] // main
    count = first + late.shape[0] // main
    rows, half = channels // count, out.shape[1] // 2
    unit = rows // 2
    which = lax.rem(lax.axis_index("tm") + whose, 2)
    at = pl.ds(pl.multiple_of(which * half, 8), half)
    shards = [shard_at(count, k) for k in range(count)]
    copies = []
    for a in range(3):
        for q in range(9):
            base = q * unit if q < 7 else a * 2 * unit + (q - 7) * unit
            step = a if q < 7 else 3
            total = None
            for k, shard in enumerate(shards):
                source, place = (early, k) if k < first else (late, k - first)
                piece = source[place * main + base : place * main + base + unit, :]
                mask = in_slot(channels, rows, lax.rem(shard + step, count))
                total = piece if total is None else jnp.where(mask, piece, total)
            total = total.astype(F32) * scale
            if step:
                total = pltpu.roll(total, channels - step * rows, 1)
            laid[a, q * unit : (q + 1) * unit, :] = total
        copy = pltpu.make_async_copy(laid.at[a], out.at[a, at], sems.at[a])
        copy.start()
        copies.append(copy)
    for copy in copies:
        copy.wait()


def in_place(x):
    return pltpu.with_memory_space_constraint(x, pltpu.HBM)


def local_fast(features, kernel, cotangent):
    rows, _, frames, pixels = features.shape
    length = frames * pixels
    count = lax.axis_size("chan")
    channels = rows * count
    taps = kernel.shape[1]
    half = 9 * rows // 2
    main, _ = packed_rows(half)
    sds = jax.ShapeDtypeStruct
    block_shape = sds((rows, length), BF16)
    term_shape = sds((main, channels), BF16)
    stack_shape = sds((half, 2 * length), BF16)
    rhs = pltpu.VMEM((channels, 2 * length), BF16)

    def swap(x, far):
        return lax.ppermute(x, "chan", [(z, z ^ far) for z in range(count)])

    weights = jnp.transpose(kernel, (1, 0, 2)).reshape(taps * rows, channels)
    hbm = pl.BlockSpec(memory_space=pltpu.HBM)
    cot_other = rotate(cotangent, "tm", 1)
    activation, flat_own = run(
        activate_kernel,
        (in_place(features), in_place(cotangent)),
        in_specs=[hbm] * 2,
        out_shape=(block_shape, sds((rows, length), F32)),
        out_specs=(whole(),) * 2,
        scratch_shapes=[
            pltpu.VMEM(features.shape, BF16),
            pltpu.VMEM(features.shape, BF16),
            pltpu.SemaphoreType.DMA((2, 3)),
        ],
        name="activate",
    )
    other = rotate(activation, "tm", 1)
    near, far = swap(activation, 1), swap(activation, 2)
    own_term, stack, flat, weights = run(
        functools.partial(own_terms_kernel, pixels),
        (activation, other, flat_own, cot_other, in_place(weights)),
        in_specs=[whole()] * 4 + [hbm],
        out_shape=(
            term_shape,
            stack_shape,
            sds((rows, 2 * length), F32),
            sds(weights.shape, BF16),
        ),
        out_specs=(whole(),) * 4,
        scratch_shapes=[rhs, pltpu.SemaphoreType.DMA((1,))],
        name="own_terms",
    )
    terms, got = [own_term], [rotate(own_term, "dp", 1)]
    blocks = [activation, other]

    def terms_of(k, here, there, waits=()):
        blocks.extend((here, there))
        term = run(
            functools.partial(terms_kernel, pixels, k),
            (stack, *blocks[-2:]),
            waits=waits,
            out_shape=term_shape,
            out_specs=whole(),
            scratch_shapes=[rhs],
            name=f"terms_{k}",
        )
        terms.append(term)
        got.append(rotate(term, "dp", 1))
        return term

    own_share, kept, near_share, passed_share = run(
        functools.partial(share_kernel, pixels),
        (weights, flat, stack),
        waits=(own_term,),
        out_shape=(
            sds((rows, length), F32),
            sds((rows, length), F32),
            block_shape,
            block_shape,
        ),
        out_specs=(whole(),) * 4,
        scratch_shapes=[
            pltpu.VMEM((half, (frames + 2) * pixels), BF16),
            pltpu.VMEM((half, (frames + 2) * pixels), BF16),
            pltpu.VMEM((channels, length), F32),
        ],
        name="shares",
    )
    first_share = swap(near_share, 1)
    near = after(near, own_share, flops=NEAR_COST)
    far, message = run(
        pack_kernel,
        (far, passed_share),
        out_shape=(block_shape, sds((2, rows, length), BF16)),
        out_specs=(whole(),) * 2,
        cost_estimate=cost(FAR_COST),
        name="pack",
    )
    message = swap(message, 1)
    term = terms_of(1, near, rotate(near, "tm", 1), (own_share, far, got[0]))
    term = terms_of(2, far, rotate(far, "tm", 1), (term,))
    slope = run(
        functools.partial(slope_kernel, pixels),
        (features,),
        waits=(term,),
        out_shape=sds((rows, length), F32),
        out_specs=whole(),
        name="slope",
    )
    last, passed_share = run(
        unpack_kernel,
        (message,),
        waits=(slope, got[1]),
        out_shape=(block_shape, block_shape),
        out_specs=(whole(),) * 2,
        name="unpack",
    )
    carry = run(
        add_kernel,
        (kept, passed_share),
        out_shape=block_shape,
        out_specs=whole(),
        name="carry_share",
    )
    second_share = swap(carry, 2)
    term = terms_of(3, last, rotate(last, "tm", 1), (carry,))

    def sums(first, stop, waits=()):
        return run(
            functools.partial(sum_kernel, main),
            (*terms[first:stop], *got[first:stop]),
            waits=waits,
            out_shape=sds(((stop - first) * main, channels), BF16),
            out_specs=whole(),
            name=f"sums_{first}",
        )

    conv_out, token = run(
        functools.partial(conv_kernel, pixels),
        (weights, *blocks),
        waits=(term, got[2]),
        out_shape=(sds(features.shape, BF16), sds(TOKEN, F32)),
        out_specs=(whole(),) * 2,
        scratch_shapes=[pltpu.VMEM((channels, (frames + 2) * pixels), BF16)],
        name="conv",
    )
    early = sums(0, 2, (term,))
    gathered = run(
        gather_share_kernel,
        (own_share, second_share),
        waits=(token, early),
        out_shape=sds((rows, length), F32),
        out_specs=whole(),
        cost_estimate=cost(GATHER_COST),
        name="gather_share",
    )
    feature_grad, token = run(
        functools.partial(feature_kernel, pixels),
        (slope, gathered, first_share),
        out_shape=(sds(features.shape, BF16), sds(TOKEN, F32)),
        out_specs=(whole(),) * 2,
        cost_estimate=cost(FEATURE_COST),
        name="feature_grad",
    )
    late = sums(2, count, (token,))
    scale = 1.0 / math.sqrt(lax.axis_size("dp") * lax.axis_size("tm") * length)

    def finish(whose, sums, base=()):
        anywhere = pl.BlockSpec(memory_space=pl.ANY)
        return run(
            functools.partial(finish_kernel, scale, main, whose),
            (*sums, *base),
            in_specs=[whole()] * 2 + [anywhere] * len(base),
            out_shape=sds((3, 9 * rows, channels), F32),
            out_specs=anywhere,
            input_output_aliases={2: 0} if base else {},
            scratch_shapes=[pltpu.VMEM((3, half, channels), F32), pltpu.SemaphoreType.DMA((3,))],
            name=f"kernel_grad_{whose}",
        )

    kernel_grad = finish(0, (early, late))
    kernel_grad = finish(1, (rotate(early, "tm", 1), rotate(late, "tm", 1)), (kernel_grad,))
    kernel_grad = jnp.transpose(kernel_grad.reshape(taps, rows, channels), (1, 0, 2))
    return (conv_out, feature_grad, kernel_grad)


def local(features, kernel, cotangent):
    rows, clips, _, pixels = features.shape
    fits = (
        clips == 1
        and lax.axis_size("tm") == 2
        and lax.axis_size("dp") == 2
        and rows % (2 * SUB) == 0
        and pixels % 128 == 0
        and kernel.shape[1] == 27
        and lax.axis_size("chan") == 4
    )
    return (local_fast if fits else local_generic)(features, kernel, cotangent)


def solution(mesh):
    return jax.shard_map(
        local,
        mesh=mesh,
        in_specs=(
            P("chan", ("groups", "dp"), "tm", None),
            P("chan", None, None),
            P("chan", ("groups", "dp"), "tm", None),
        ),
        out_specs=(
            P("chan", ("groups", "dp"), "tm", None),
            P("chan", ("groups", "dp"), "tm", None),
            P(("groups", "chan"), None, None),
        ),
        check_vma=False,
    )
```

```python
import functools
import math

import jax
import jax.numpy as jnp
from jax import lax
from jax.experimental import pallas as pl
from jax.experimental.pallas import tpu as pltpu
from jax.sharding import PartitionSpec as P

WID = 64
SUB = 16
F32 = jnp.float32
BF16 = jnp.bfloat16
VMEM_LIMIT = 24 * 1024 * 1024
TOKEN = (8, 128)
FEATURE_COST = 3 * 10**9
GATHER_COST = 10**8
FAR_COST = 10**9
NEAR_COST = 3 * 10**9


def from_behind(x, axis, by):
    size = lax.axis_size(axis)
    pairs = [(i, i + by) for i in range(size) if 0 <= i + by < size]
    return lax.ppermute(x, axis, pairs)


def padded_copies(block):
    pixels = block.shape[-1]
    column = lax.broadcasted_iota(jnp.int32, (pixels,), 0) % WID
    nothing = jnp.zeros((), block.dtype)
    widths = [(0, 0), (0, 0), (0, 0), (WID + 1, WID + 1)]
    left_cut = jnp.pad(jnp.where(column == WID - 1, nothing, block), widths)
    untouched = jnp.pad(block, widths)
    right_cut = jnp.pad(jnp.where(column == 0, nothing, block), widths)
    return (left_cut, untouched, right_cut)


def tap_window(copies, first_frame, vertical, horizontal, frames, pixels):
    source = copies[horizontal]
    offset = vertical * WID + horizontal
    return source[:, :, first_frame : first_frame + frames, offset : offset + pixels]


def stacked_taps(copies, first_frame, flipped, frames, pixels):
    pieces = []
    for vertical in range(3):
        for horizontal in range(3):
            if flipped:
                pieces.append(
                    tap_window(copies, first_frame, 2 - vertical, 2 - horizontal, frames, pixels)
                )
            else:
                pieces.append(tap_window(copies, first_frame, vertical, horizontal, frames, pixels))
    concatenated = jnp.concatenate(pieces, axis=0)
    return concatenated.reshape(concatenated.shape[0], -1)


def local_generic(features, kernel, cotangent):
    channels, clip_count, frames, pixels = features.shape
    flat_length = clip_count * frames * pixels
    widened = features.astype(F32)
    logistic = jax.nn.sigmoid(widened)
    activation = (widened * logistic).astype(BF16)
    slope_factor = logistic * (1.0 + widened * (1.0 - logistic))
    earlier = from_behind(activation[:, :, frames - 2 :, :], "tm", 1)
    extended = jnp.concatenate([earlier, activation], axis=2)
    upcoming = from_behind(cotangent[:, :, :2, :], "tm", -1)
    later_padded = jnp.concatenate([cotangent, upcoming], axis=2)
    cotangent_rows = cotangent.reshape(channels, -1)
    portion = lax.all_gather(extended, "chan", axis=0, tiled=True)
    out_sum = jnp.zeros((channels, flat_length), F32)
    amount = portion.shape[0]
    copies = padded_copies(portion)
    grad_parts = []
    for temporal in range(3):
        stacked = stacked_taps(copies, temporal, False, frames, pixels)
        weights = kernel[:, 9 * temporal : 9 * temporal + 9, :].reshape(channels, 9 * amount)
        out_sum = out_sum + jnp.dot(weights, stacked, preferred_element_type=F32)
        grad_parts.append(
            lax.dot_general(
                cotangent_rows, stacked, (((1,), (1,)), ((), ())), preferred_element_type=F32
            ).reshape(channels, 9, amount)
        )
    grad_sum = jnp.concatenate(grad_parts, axis=1)
    conv_out = out_sum.reshape(features.shape).astype(BF16)
    position_count = lax.axis_size("dp") * lax.axis_size("tm") * flat_length
    kernel_grad = lax.psum(grad_sum, ("tm", "dp")) * (1.0 / math.sqrt(position_count))
    padded_later = padded_copies(later_padded)
    summed = jnp.zeros((amount, flat_length), F32)
    for temporal in range(3):
        weights = jnp.transpose(
            kernel[:, 9 * temporal : 9 * temporal + 9, :], (2, 1, 0)
        ).reshape(amount, 9 * channels)
        stacked = stacked_taps(padded_later, 2 - temporal, True, frames, pixels)
        summed = summed + jnp.dot(weights, stacked, preferred_element_type=F32)
    before_slope = lax.psum_scatter(
        summed.reshape(amount, clip_count, frames, pixels), "chan", scatter_dimension=0, tiled=True
    )
    feature_grad = (before_slope * slope_factor).astype(BF16)
    return (conv_out, feature_grad, kernel_grad)


def rotate(x, axis, by):
    size = lax.axis_size(axis)
    return lax.ppermute(x, axis, [(i, (i + by) % size) for i in range(size)])


def shifted(frame, down, right):
    pixels = frame.shape[-1]
    if down == 0 and right == 0:
        return frame
    cell = lax.broadcasted_iota(jnp.int32, (1, pixels), 1)
    row, column = cell // WID + down, cell % WID + right
    inside = (row >= 0) & (row < pixels // WID) & (column >= 0) & (column < WID)
    moved = pltpu.roll(frame, (-(down * WID + right)) % pixels, 1)
    return jnp.where(inside, moved, 0.0)


def after(x, *others, flops=1):
    anywhere = pl.BlockSpec(memory_space=pl.ANY)
    return pl.pallas_call(
        lambda *refs: None,
        out_shape=jax.ShapeDtypeStruct(x.shape, x.dtype),
        in_specs=[anywhere] * (1 + len(others)),
        out_specs=anywhere,
        input_output_aliases={0: 0},
        compiler_params=pltpu.CompilerParams(vmem_limit_bytes=1024 * 1024),
        cost_estimate=cost(flops),
        name="hand_on",
    )(x, *others)


def run(kernel, args, waits=(), **options):
    options.setdefault("in_specs", [whole()] * len(args))
    options.setdefault("cost_estimate", cost())
    options["in_specs"] = list(options["in_specs"]) + [
        pl.BlockSpec(memory_space=pl.ANY) for _ in waits
    ]
    count = len(args)

    def body(*refs):
        kernel(*refs[:count], *refs[count + len(waits) :])

    return pl.pallas_call(
        body, compiler_params=pltpu.CompilerParams(vmem_limit_bytes=VMEM_LIMIT), **options
    )(*args, *waits)


def cost(flops=1):
    return pl.CostEstimate(flops=flops, bytes_accessed=1, transcendentals=0)


def whole():
    return pl.BlockSpec(memory_space=pltpu.VMEM)


def activate_kernel(features, cotangent, activation, flat, feat, cot, sems):
    parts = sems.shape[1]
    rows, _, frames, pixels = feat.shape
    size = rows // parts
    loads = []
    for n, (source, target) in enumerate(((features, feat), (cotangent, cot))):
        for part in range(parts):
            at = pl.ds(part * size, size)
            loads.append(pltpu.make_async_copy(source.at[at], target.at[at], sems.at[n, part]))
    for load in loads:
        load.start()
    for part in range(parts):
        loads[part].wait()
        at = slice(part * size, (part + 1) * size)
        v = feat[at, 0].astype(F32)
        act = v / (1.0 + jnp.exp(-v))
        for t in range(frames):
            activation[at, t * pixels : (t + 1) * pixels] = act[:, t, :].astype(BF16)
    for load in loads[parts:]:
        load.wait()
    flatten(pixels, cot, flat, 0)


def flatten(pixels, source, flat, first):
    wide = source[:, 0].astype(F32)
    for t in range(wide.shape[1]):
        at = (first + t) * pixels
        at = at if isinstance(at, int) else pl.multiple_of(at, pixels)
        flat[:, pl.ds(at, pixels)] = wide[:, t, :]


def shard_at(count, k):
    z = lax.axis_index("chan")
    return (z, z + 1 - 2 * lax.rem(z, 2), lax.rem(z + 2, count), count - 1 - z)[k]


def in_slot(channels, rows, slot):
    lane = lax.broadcasted_iota(jnp.int32, (1, channels), 1)
    return (lane >= slot * rows) & (lane < (slot + 1) * rows)


def packed_rows(total):
    unit = total // 9
    return 7 * unit, 2 * unit


def fill_stack(pixels, flat, stack, half, first, frames):
    unit = flat.shape[0] // 2
    for t in range(frames):
        at = slice(t * pixels, (t + 1) * pixels)
        source = slice((first + t) * pixels, (first + t + 1) * pixels)
        for q in range(9):
            tap, part = divmod(9 * half + q, 2)
            i, j = divmod(tap, 3)
            frame = flat[part * unit : (part + 1) * unit, source]
            stack[q * unit : (q + 1) * unit, at] = shifted(frame, 1 - i, 1 - j).astype(BF16)


def block_terms(pixels, k, stack, here, there, out, rhs):
    channels = out.shape[1]
    rows, length = here.shape
    lanes, count = 2 * length, channels // rows
    shard = shard_at(count, k)
    for core in range(2):

        @pl.when(lax.axis_index("tm") == core)
        def _(first=(here, there)[core], second=(there, here)[core]):
            for a in range(3):
                skip = (2 - a) * pixels
                at = pl.ds(pl.multiple_of(lax.rem(shard + a, count) * rows, SUB), rows)
                if skip:
                    rhs[at, :skip] = jnp.zeros((rows, skip), BF16)
                rhs[at, skip : skip + length] = first[...]
                rhs[at, skip + length :] = second[:, : length - skip]

    last = lax.rem(shard + 3, count)
    rhs[pl.ds(pl.multiple_of(last * rows, SUB), rows), :] = jnp.zeros((rows, lanes), BF16)
    terms = lax.dot_general(
        stack[...], rhs[...], (((1,), (1,)), ((), ())), preferred_element_type=F32
    )
    main, tail = packed_rows(terms.shape[0])
    free = in_slot(channels, rows, last)
    for a in range(3):
        at = slice(a * tail, (a + 1) * tail)
        moved = pltpu.roll(terms[main:], (3 - a) * rows, 1)
        out[at, :] = jnp.where(free, moved, terms[at]).astype(BF16)
    out[3 * tail :, :] = terms[3 * tail : main].astype(BF16)


def own_terms_kernel(
    pixels, mine, other, flat_own, cot_other, weights, out, stack, flat, held, rhs, sems
):
    load = pltpu.make_async_copy(weights, held, sems.at[0])
    load.start()
    length = flat_own.shape[1]
    me = lax.axis_index("tm")
    flat[:, pl.ds(pl.multiple_of(me * length, pixels), length)] = flat_own[...]
    flatten(pixels, cot_other, flat, (1 - me) * (length // pixels))
    for core in range(2):

        @pl.when(me == core)
        def _(core=core):
            fill_stack(pixels, flat, stack, core, 0, flat.shape[1] // pixels)

    block_terms(pixels, 0, stack, mine, other, out, rhs)
    load.wait()


def terms_kernel(pixels, k, stack, here, there, out, rhs):
    block_terms(pixels, k, stack, here, there, out, rhs)


def share_kernel(pixels, weights, flat, mine, own, kept, near, passed, window, other, total):
    rows, length = own.shape
    frames, half = length // pixels, mine.shape[0]
    count = weights.shape[1] // rows
    me = lax.axis_index("tm")
    front = 2 * pixels
    for core in range(2):

        @pl.when(me == core)
        def _(core=core):
            first = core * length
            held = min(length + front, mine.shape[1] - first)
            window[:, :held] = mine[:, first : first + held]
            if held < length + front:
                window[:, held:] = jnp.zeros((half, length + front - held), BF16)
                other[:, held:] = jnp.zeros((half, length + front - held), BF16)
            fill_stack(pixels, flat, other, 1 - core, core * frames, held // pixels)

    acc = None
    for a in range(3):
        lanes = slice((2 - a) * pixels, (2 - a) * pixels + length)
        for which, stack in ((me, window), (1 - me, other)):
            at = pl.multiple_of((2 * a + which) * half, SUB)
            term = lax.dot_general(
                weights[pl.ds(at, half), :],
                stack[:, lanes],
                (((0,), (0,)), ((), ())),
                preferred_element_type=F32,
            )
            acc = term if acc is None else acc + term
    total[...] = acc

    def part(k):
        return total[pl.ds(pl.multiple_of(shard_at(count, k) * rows, SUB), rows), :]

    own[...] = part(0)
    kept[...] = part(2)
    near[...] = part(1).astype(BF16)
    passed[...] = part(3).astype(BF16)


def pack_kernel(block, share, out, message):
    out[...] = block[...]
    message[0] = block[...]
    message[1] = share[...]


def unpack_kernel(message, block, share):
    block[...] = message[0]
    share[...] = message[1]


def add_kernel(kept, came, out):
    out[...] = (kept[...] + came[...].astype(F32)).astype(out.dtype)


def conv_kernel(pixels, weights, *refs):
    blocks, (out, token, act) = refs[:-3], refs[-3:]
    token[...] = jnp.zeros(TOKEN, F32)
    rows, _, frames, _ = out.shape
    count = weights.shape[1] // rows
    length, front = frames * pixels, 2 * pixels
    me = lax.axis_index("tm")
    for k in range(count):
        here, there = blocks[2 * k], blocks[2 * k + 1]
        at = pl.ds(pl.multiple_of(shard_at(count, k) * rows, SUB), rows)
        earlier = there[:, length - front :]
        act[at, :front] = jnp.where(me == 0, jnp.zeros_like(earlier), earlier)
        act[at, front:] = here[...]

    taps = 9 * rows
    for t in range(frames):
        z_t = None
        for a in range(3):
            term = jnp.dot(
                weights[a * taps : (a + 1) * taps, :],
                act[:, (t + a) * pixels : (t + a + 1) * pixels],
                preferred_element_type=F32,
            )
            z_t = term if z_t is None else z_t + term
        acc = None
        for i in range(3):
            for j in range(3):
                at = (3 * i + j) * rows
                moved = shifted(z_t[at : at + rows, :], i - 1, j - 1)
                acc = moved if acc is None else acc + moved
        out[:, 0, t, :] = acc.astype(BF16)


def slope_kernel(pixels, features, slope):
    v = features[:, 0].astype(F32)
    s = 1.0 / (1.0 + jnp.exp(-v))
    factor = s * (1.0 + v * (1.0 - s))
    for t in range(factor.shape[1]):
        slope[:, t * pixels : (t + 1) * pixels] = factor[:, t, :]


def gather_share_kernel(own, second, out):
    out[...] = own[...] + second[...].astype(F32)


def feature_kernel(pixels, slope, gathered, first, out, token):
    token[...] = jnp.zeros(TOKEN, F32)
    total = (gathered[...] + first[...].astype(F32)) * slope[...]
    frames = [total[:, t * pixels : (t + 1) * pixels] for t in range(out.shape[2])]
    out[:, 0] = jnp.stack(frames, axis=1).astype(BF16)


def sum_kernel(main, *refs):
    out, ins = refs[-1], refs[:-1]
    count = len(ins) // 2
    for k in range(count):
        total = ins[k][...].astype(F32) + ins[count + k][...].astype(F32)
        out[k * main : (k + 1) * main, :] = total.astype(BF16)


def finish_kernel(scale, main, whose, early, late, *refs):
    out, laid, sems = refs[-3:]
    channels = out.shape[2]
    first = early.shape[0] // main
    count = first + late.shape[0] // main
    rows, half = channels // count, out.shape[1] // 2
    unit = rows // 2
    which = lax.rem(lax.axis_index("tm") + whose, 2)
    shards = [shard_at(count, k) for k in range(count)]
    copies = []
    for a in range(3):
        for q in range(9):
            base = q * unit if q < 7 else a * 2 * unit + (q - 7) * unit
            step = a if q < 7 else 3
            total = None
            for k, shard in enumerate(shards):
                source, place = (early, k) if k < first else (late, k - first)
                piece = source[place * main + base : place * main + base + unit, :]
                mask = in_slot(channels, rows, lax.rem(shard + step, count))
                total = piece if total is None else jnp.where(mask, piece, total)
            if step:
                total = pltpu.roll(total, channels - step * rows, 1)
            total = total.astype(F32) * scale
            laid[a, q * unit : (q + 1) * unit, :] = total
            if q % 3 == 2:
                part = pl.ds((q - 2) * unit, 3 * unit)
                there = pl.ds(pl.multiple_of(which * half + (q - 2) * unit, 8), 3 * unit)
                copy = pltpu.make_async_copy(
                    laid.at[a, part], out.at[a, there], sems.at[len(copies)]
                )
                copy.start()
                copies.append(copy)
    for copy in copies:
        copy.wait()


def in_place(x):
    return pltpu.with_memory_space_constraint(x, pltpu.HBM)


def local_fast(features, kernel, cotangent):
    rows, _, frames, pixels = features.shape
    length = frames * pixels
    count = lax.axis_size("chan")
    channels = rows * count
    taps = kernel.shape[1]
    half = 9 * rows // 2
    main, _ = packed_rows(half)
    sds = jax.ShapeDtypeStruct
    block_shape = sds((rows, length), BF16)
    term_shape = sds((main, channels), BF16)
    stack_shape = sds((half, 2 * length), BF16)
    rhs = pltpu.VMEM((channels, 2 * length), BF16)

    def swap(x, far):
        return lax.ppermute(x, "chan", [(z, z ^ far) for z in range(count)])

    weights = jnp.transpose(kernel, (1, 0, 2)).reshape(taps * rows, channels)
    hbm = pl.BlockSpec(memory_space=pltpu.HBM)
    cot_other = rotate(cotangent, "tm", 1)
    activation, flat_own = run(
        activate_kernel,
        (in_place(features), in_place(cotangent)),
        in_specs=[hbm] * 2,
        out_shape=(block_shape, sds((rows, length), F32)),
        out_specs=(whole(),) * 2,
        scratch_shapes=[
            pltpu.VMEM(features.shape, BF16),
            pltpu.VMEM(features.shape, BF16),
            pltpu.SemaphoreType.DMA((2, 3)),
        ],
        name="activate",
    )
    other = rotate(activation, "tm", 1)
    near, far = swap(activation, 1), swap(activation, 2)
    own_term, stack, flat, weights = run(
        functools.partial(own_terms_kernel, pixels),
        (activation, other, flat_own, cot_other, in_place(weights)),
        in_specs=[whole()] * 4 + [hbm],
        out_shape=(
            term_shape,
            stack_shape,
            sds((rows, 2 * length), F32),
            sds(weights.shape, BF16),
        ),
        out_specs=(whole(),) * 4,
        scratch_shapes=[rhs, pltpu.SemaphoreType.DMA((1,))],
        name="own_terms",
    )
    terms, got = [own_term], [rotate(own_term, "dp", 1)]
    blocks = [activation, other]

    def terms_of(k, here, there, waits=()):
        blocks.extend((here, there))
        term = run(
            functools.partial(terms_kernel, pixels, k),
            (stack, *blocks[-2:]),
            waits=waits,
            out_shape=term_shape,
            out_specs=whole(),
            scratch_shapes=[rhs],
            name=f"terms_{k}",
        )
        terms.append(term)
        got.append(rotate(term, "dp", 1))
        return term

    own_share, kept, near_share, passed_share = run(
        functools.partial(share_kernel, pixels),
        (weights, flat, stack),
        waits=(own_term,),
        out_shape=(
            sds((rows, length), F32),
            sds((rows, length), F32),
            block_shape,
            block_shape,
        ),
        out_specs=(whole(),) * 4,
        scratch_shapes=[
            pltpu.VMEM((half, (frames + 2) * pixels), BF16),
            pltpu.VMEM((half, (frames + 2) * pixels), BF16),
            pltpu.VMEM((channels, length), F32),
        ],
        name="shares",
    )
    first_share = swap(near_share, 1)
    near = after(near, own_share, flops=NEAR_COST)
    far, message = run(
        pack_kernel,
        (far, passed_share),
        out_shape=(block_shape, sds((2, rows, length), BF16)),
        out_specs=(whole(),) * 2,
        cost_estimate=cost(FAR_COST),
        name="pack",
    )
    message = swap(message, 1)
    term = terms_of(1, near, rotate(near, "tm", 1), (own_share, far, got[0]))
    term = terms_of(2, far, rotate(far, "tm", 1), (term,))
    slope = run(
        functools.partial(slope_kernel, pixels),
        (features,),
        waits=(term,),
        out_shape=sds((rows, length), F32),
        out_specs=whole(),
        name="slope",
    )
    last, passed_share = run(
        unpack_kernel,
        (message,),
        waits=(slope, got[1]),
        out_shape=(block_shape, block_shape),
        out_specs=(whole(),) * 2,
        name="unpack",
    )
    carry = run(
        add_kernel,
        (kept, passed_share),
        out_shape=block_shape,
        out_specs=whole(),
        name="carry_share",
    )
    second_share = swap(carry, 2)
    term = terms_of(3, last, rotate(last, "tm", 1), (carry,))

    def sums(first, stop, waits=()):
        return run(
            functools.partial(sum_kernel, main),
            (*terms[first:stop], *got[first:stop]),
            waits=waits,
            out_shape=sds(((stop - first) * main, channels), BF16),
            out_specs=whole(),
            name=f"sums_{first}",
        )

    conv_out, token = run(
        functools.partial(conv_kernel, pixels),
        (weights, *blocks),
        waits=(term, got[2]),
        out_shape=(sds(features.shape, BF16), sds(TOKEN, F32)),
        out_specs=(whole(),) * 2,
        scratch_shapes=[pltpu.VMEM((channels, (frames + 2) * pixels), BF16)],
        name="conv",
    )
    early = sums(0, 2, (term,))
    gathered = run(
        gather_share_kernel,
        (own_share, second_share),
        waits=(token, early),
        out_shape=sds((rows, length), F32),
        out_specs=whole(),
        cost_estimate=cost(GATHER_COST),
        name="gather_share",
    )
    feature_grad, token = run(
        functools.partial(feature_kernel, pixels),
        (slope, gathered, first_share),
        out_shape=(sds(features.shape, BF16), sds(TOKEN, F32)),
        out_specs=(whole(),) * 2,
        cost_estimate=cost(FEATURE_COST),
        name="feature_grad",
    )
    late = sums(2, count, (token,))
    scale = 1.0 / math.sqrt(lax.axis_size("dp") * lax.axis_size("tm") * length)

    def finish(whose, sums, base=()):
        anywhere = pl.BlockSpec(memory_space=pl.ANY)
        return run(
            functools.partial(finish_kernel, scale, main, whose),
            (*sums, *base),
            in_specs=[whole()] * 2 + [anywhere] * len(base),
            out_shape=sds((3, 9 * rows, channels), F32),
            out_specs=anywhere,
            input_output_aliases={2: 0} if base else {},
            scratch_shapes=[pltpu.VMEM((3, half, channels), F32), pltpu.SemaphoreType.DMA((9,))],
            name=f"kernel_grad_{whose}",
        )

    kernel_grad = finish(0, (early, late))
    kernel_grad = finish(1, (rotate(early, "tm", 1), rotate(late, "tm", 1)), (kernel_grad,))
    kernel_grad = jnp.transpose(kernel_grad.reshape(taps, rows, channels), (1, 0, 2))
    return (conv_out, feature_grad, kernel_grad)


def local(features, kernel, cotangent):
    rows, clips, _, pixels = features.shape
    fits = (
        clips == 1
        and lax.axis_size("tm") == 2
        and lax.axis_size("dp") == 2
        and rows % (2 * SUB) == 0
        and pixels % 128 == 0
        and kernel.shape[1] == 27
        and lax.axis_size("chan") == 4
    )
    return (local_fast if fits else local_generic)(features, kernel, cotangent)


def solution(mesh):
    return jax.shard_map(
        local,
        mesh=mesh,
        in_specs=(
            P("chan", ("groups", "dp"), "tm", None),
            P("chan", None, None),
            P("chan", ("groups", "dp"), "tm", None),
        ),
        out_specs=(
            P("chan", ("groups", "dp"), "tm", None),
            P("chan", ("groups", "dp"), "tm", None),
            P(("groups", "chan"), None, None),
        ),
        check_vma=False,
    )
```

```python
import functools
import math

import jax
import jax.numpy as jnp
from jax import lax
from jax.experimental import pallas as pl
from jax.experimental.pallas import tpu as pltpu
from jax.sharding import PartitionSpec as P

WID = 64
SUB = 16
F32 = jnp.float32
BF16 = jnp.bfloat16
VMEM_LIMIT = 24 * 1024 * 1024
TOKEN = (8, 128)
FEATURE_COST = 2 * 10**10
GATHER_COST = 3 * 10**9
FAR_COST = 10**9
NEAR_COST = 3 * 10**9


def from_behind(x, axis, by):
    size = lax.axis_size(axis)
    pairs = [(i, i + by) for i in range(size) if 0 <= i + by < size]
    return lax.ppermute(x, axis, pairs)


def padded_copies(block):
    pixels = block.shape[-1]
    column = lax.broadcasted_iota(jnp.int32, (pixels,), 0) % WID
    nothing = jnp.zeros((), block.dtype)
    widths = [(0, 0), (0, 0), (0, 0), (WID + 1, WID + 1)]
    left_cut = jnp.pad(jnp.where(column == WID - 1, nothing, block), widths)
    untouched = jnp.pad(block, widths)
    right_cut = jnp.pad(jnp.where(column == 0, nothing, block), widths)
    return (left_cut, untouched, right_cut)


def tap_window(copies, first_frame, vertical, horizontal, frames, pixels):
    source = copies[horizontal]
    offset = vertical * WID + horizontal
    return source[:, :, first_frame : first_frame + frames, offset : offset + pixels]


def stacked_taps(copies, first_frame, flipped, frames, pixels):
    pieces = []
    for vertical in range(3):
        for horizontal in range(3):
            if flipped:
                pieces.append(
                    tap_window(copies, first_frame, 2 - vertical, 2 - horizontal, frames, pixels)
                )
            else:
                pieces.append(tap_window(copies, first_frame, vertical, horizontal, frames, pixels))
    concatenated = jnp.concatenate(pieces, axis=0)
    return concatenated.reshape(concatenated.shape[0], -1)


def local_generic(features, kernel, cotangent):
    channels, clip_count, frames, pixels = features.shape
    flat_length = clip_count * frames * pixels
    widened = features.astype(F32)
    logistic = jax.nn.sigmoid(widened)
    activation = (widened * logistic).astype(BF16)
    slope_factor = logistic * (1.0 + widened * (1.0 - logistic))
    earlier = from_behind(activation[:, :, frames - 2 :, :], "tm", 1)
    extended = jnp.concatenate([earlier, activation], axis=2)
    upcoming = from_behind(cotangent[:, :, :2, :], "tm", -1)
    later_padded = jnp.concatenate([cotangent, upcoming], axis=2)
    cotangent_rows = cotangent.reshape(channels, -1)
    portion = lax.all_gather(extended, "chan", axis=0, tiled=True)
    out_sum = jnp.zeros((channels, flat_length), F32)
    amount = portion.shape[0]
    copies = padded_copies(portion)
    grad_parts = []
    for temporal in range(3):
        stacked = stacked_taps(copies, temporal, False, frames, pixels)
        weights = kernel[:, 9 * temporal : 9 * temporal + 9, :].reshape(channels, 9 * amount)
        out_sum = out_sum + jnp.dot(weights, stacked, preferred_element_type=F32)
        grad_parts.append(
            lax.dot_general(
                cotangent_rows, stacked, (((1,), (1,)), ((), ())), preferred_element_type=F32
            ).reshape(channels, 9, amount)
        )
    grad_sum = jnp.concatenate(grad_parts, axis=1)
    conv_out = out_sum.reshape(features.shape).astype(BF16)
    position_count = lax.axis_size("dp") * lax.axis_size("tm") * flat_length
    kernel_grad = lax.psum(grad_sum, ("tm", "dp")) * (1.0 / math.sqrt(position_count))
    padded_later = padded_copies(later_padded)
    summed = jnp.zeros((amount, flat_length), F32)
    for temporal in range(3):
        weights = jnp.transpose(
            kernel[:, 9 * temporal : 9 * temporal + 9, :], (2, 1, 0)
        ).reshape(amount, 9 * channels)
        stacked = stacked_taps(padded_later, 2 - temporal, True, frames, pixels)
        summed = summed + jnp.dot(weights, stacked, preferred_element_type=F32)
    before_slope = lax.psum_scatter(
        summed.reshape(amount, clip_count, frames, pixels), "chan", scatter_dimension=0, tiled=True
    )
    feature_grad = (before_slope * slope_factor).astype(BF16)
    return (conv_out, feature_grad, kernel_grad)


def rotate(x, axis, by):
    size = lax.axis_size(axis)
    return lax.ppermute(x, axis, [(i, (i + by) % size) for i in range(size)])


def shifted(frame, down, right):
    pixels = frame.shape[-1]
    if down == 0 and right == 0:
        return frame
    cell = lax.broadcasted_iota(jnp.int32, (1, pixels), 1)
    row, column = cell // WID + down, cell % WID + right
    inside = (row >= 0) & (row < pixels // WID) & (column >= 0) & (column < WID)
    moved = pltpu.roll(frame, (-(down * WID + right)) % pixels, 1)
    return jnp.where(inside, moved, 0.0)


def after(x, *others, flops=1):
    anywhere = pl.BlockSpec(memory_space=pl.ANY)
    return pl.pallas_call(
        lambda *refs: None,
        out_shape=jax.ShapeDtypeStruct(x.shape, x.dtype),
        in_specs=[anywhere] * (1 + len(others)),
        out_specs=anywhere,
        input_output_aliases={0: 0},
        compiler_params=pltpu.CompilerParams(vmem_limit_bytes=1024 * 1024),
        cost_estimate=cost(flops),
        name="hand_on",
    )(x, *others)


def run(kernel, args, waits=(), **options):
    options.setdefault("in_specs", [whole()] * len(args))
    options.setdefault("cost_estimate", cost())
    options["in_specs"] = list(options["in_specs"]) + [
        pl.BlockSpec(memory_space=pl.ANY) for _ in waits
    ]
    count = len(args)

    def body(*refs):
        kernel(*refs[:count], *refs[count + len(waits) :])

    return pl.pallas_call(
        body, compiler_params=pltpu.CompilerParams(vmem_limit_bytes=VMEM_LIMIT), **options
    )(*args, *waits)


def cost(flops=1):
    return pl.CostEstimate(flops=flops, bytes_accessed=1, transcendentals=0)


def whole():
    return pl.BlockSpec(memory_space=pltpu.VMEM)


def activate_kernel(features, cotangent, activation, flat, feat, cot, sems):
    parts = sems.shape[1]
    rows, _, frames, pixels = feat.shape
    size = rows // parts
    loads = []
    for n, (source, target) in enumerate(((features, feat), (cotangent, cot))):
        for part in range(parts):
            at = pl.ds(part * size, size)
            loads.append(pltpu.make_async_copy(source.at[at], target.at[at], sems.at[n, part]))
    for load in loads:
        load.start()
    for part in range(parts):
        loads[part].wait()
        at = slice(part * size, (part + 1) * size)
        v = feat[at, 0].astype(F32)
        act = v / (1.0 + jnp.exp(-v))
        for t in range(frames):
            activation[at, t * pixels : (t + 1) * pixels] = act[:, t, :].astype(BF16)
    for load in loads[parts:]:
        load.wait()
    flatten(pixels, cot, flat, 0)


def flatten(pixels, source, flat, first):
    wide = source[:, 0].astype(F32)
    for t in range(wide.shape[1]):
        at = (first + t) * pixels
        at = at if isinstance(at, int) else pl.multiple_of(at, pixels)
        flat[:, pl.ds(at, pixels)] = wide[:, t, :]


def shard_at(count, k):
    z = lax.axis_index("chan")
    return (z, z + 1 - 2 * lax.rem(z, 2), lax.rem(z + 2, count), count - 1 - z)[k]


def in_slot(channels, rows, slot):
    lane = lax.broadcasted_iota(jnp.int32, (1, channels), 1)
    return (lane >= slot * rows) & (lane < (slot + 1) * rows)


def packed_rows(total):
    unit = total // 9
    return 7 * unit, 2 * unit


def fill_stack(pixels, flat, stack, half, first, frames):
    unit = flat.shape[0] // 2
    for t in range(frames):
        at = slice(t * pixels, (t + 1) * pixels)
        source = slice((first + t) * pixels, (first + t + 1) * pixels)
        for q in range(9):
            tap, part = divmod(9 * half + q, 2)
            i, j = divmod(tap, 3)
            frame = flat[part * unit : (part + 1) * unit, source]
            stack[q * unit : (q + 1) * unit, at] = shifted(frame, 1 - i, 1 - j).astype(BF16)


def block_terms(pixels, k, stack, here, there, out, rhs):
    channels = out.shape[1]
    rows, length = here.shape
    lanes, count = 2 * length, channels // rows
    shard = shard_at(count, k)
    for core in range(2):

        @pl.when(lax.axis_index("tm") == core)
        def _(first=(here, there)[core], second=(there, here)[core]):
            for a in range(3):
                skip = (2 - a) * pixels
                at = pl.ds(pl.multiple_of(lax.rem(shard + a, count) * rows, SUB), rows)
                if skip:
                    rhs[at, :skip] = jnp.zeros((rows, skip), BF16)
                rhs[at, skip : skip + length] = first[...]
                rhs[at, skip + length :] = second[:, : length - skip]

    last = lax.rem(shard + 3, count)
    rhs[pl.ds(pl.multiple_of(last * rows, SUB), rows), :] = jnp.zeros((rows, lanes), BF16)
    terms = lax.dot_general(
        stack[...], rhs[...], (((1,), (1,)), ((), ())), preferred_element_type=F32
    )
    main, tail = packed_rows(terms.shape[0])
    free = in_slot(channels, rows, last)
    for a in range(3):
        at = slice(a * tail, (a + 1) * tail)
        moved = pltpu.roll(terms[main:], (3 - a) * rows, 1)
        out[at, :] = jnp.where(free, moved, terms[at]).astype(BF16)
    out[3 * tail :, :] = terms[3 * tail : main].astype(BF16)


def own_terms_kernel(
    pixels, mine, other, flat_own, cot_other, weights, out, stack, flat, held, rhs, sems
):
    load = pltpu.make_async_copy(weights, held, sems.at[0])
    load.start()
    length = flat_own.shape[1]
    me = lax.axis_index("tm")
    flat[:, pl.ds(pl.multiple_of(me * length, pixels), length)] = flat_own[...]
    flatten(pixels, cot_other, flat, (1 - me) * (length // pixels))
    for core in range(2):

        @pl.when(me == core)
        def _(core=core):
            fill_stack(pixels, flat, stack, core, 0, flat.shape[1] // pixels)

    block_terms(pixels, 0, stack, mine, other, out, rhs)
    load.wait()


def terms_kernel(pixels, k, stack, here, there, out, rhs):
    block_terms(pixels, k, stack, here, there, out, rhs)


def share_kernel(pixels, weights, flat, mine, own, kept, near, passed, window, other, total):
    rows, length = own.shape
    frames, half = length // pixels, mine.shape[0]
    count = weights.shape[1] // rows
    me = lax.axis_index("tm")
    front = 2 * pixels
    for core in range(2):

        @pl.when(me == core)
        def _(core=core):
            first = core * length
            held = min(length + front, mine.shape[1] - first)
            window[:, :held] = mine[:, first : first + held]
            if held < length + front:
                window[:, held:] = jnp.zeros((half, length + front - held), BF16)
                other[:, held:] = jnp.zeros((half, length + front - held), BF16)
            fill_stack(pixels, flat, other, 1 - core, core * frames, held // pixels)

    acc = None
    for a in range(3):
        lanes = slice((2 - a) * pixels, (2 - a) * pixels + length)
        for which, stack in ((me, window), (1 - me, other)):
            at = pl.multiple_of((2 * a + which) * half, SUB)
            term = lax.dot_general(
                weights[pl.ds(at, half), :],
                stack[:, lanes],
                (((0,), (0,)), ((), ())),
                preferred_element_type=F32,
            )
            acc = term if acc is None else acc + term
    total[...] = acc

    def part(k):
        return total[pl.ds(pl.multiple_of(shard_at(count, k) * rows, SUB), rows), :]

    own[...] = part(0)
    kept[...] = part(2)
    near[...] = part(1).astype(BF16)
    passed[...] = part(3).astype(BF16)


def pack_kernel(block, share, out, message):
    out[...] = block[...]
    message[0] = block[...]
    message[1] = share[...]


def unpack_kernel(message, block, share):
    block[...] = message[0]
    share[...] = message[1]


def add_kernel(kept, came, out):
    out[...] = (kept[...] + came[...].astype(F32)).astype(out.dtype)


def conv_kernel(pixels, weights, *refs):
    blocks, (out, token, act) = refs[:-3], refs[-3:]
    token[...] = jnp.zeros(TOKEN, F32)
    rows, _, frames, _ = out.shape
    count = weights.shape[1] // rows
    length, front = frames * pixels, 2 * pixels
    me = lax.axis_index("tm")
    for k in range(count):
        here, there = blocks[2 * k], blocks[2 * k + 1]
        at = pl.ds(pl.multiple_of(shard_at(count, k) * rows, SUB), rows)
        earlier = there[:, length - front :]
        act[at, :front] = jnp.where(me == 0, jnp.zeros_like(earlier), earlier)
        act[at, front:] = here[...]

    taps = 9 * rows
    for t in range(frames):
        z_t = None
        for a in range(3):
            term = jnp.dot(
                weights[a * taps : (a + 1) * taps, :],
                act[:, (t + a) * pixels : (t + a + 1) * pixels],
                preferred_element_type=F32,
            )
            z_t = term if z_t is None else z_t + term
        acc = None
        for i in range(3):
            for j in range(3):
                at = (3 * i + j) * rows
                moved = shifted(z_t[at : at + rows, :], i - 1, j - 1)
                acc = moved if acc is None else acc + moved
        out[:, 0, t, :] = acc.astype(BF16)


def slope_kernel(pixels, features, slope):
    v = features[:, 0].astype(F32)
    s = 1.0 / (1.0 + jnp.exp(-v))
    factor = s * (1.0 + v * (1.0 - s))
    for t in range(factor.shape[1]):
        slope[:, t * pixels : (t + 1) * pixels] = factor[:, t, :]


def gather_share_kernel(own, second, out):
    out[...] = own[...] + second[...].astype(F32)


def feature_kernel(pixels, slope, gathered, first, out, token):
    token[...] = jnp.zeros(TOKEN, F32)
    total = (gathered[...] + first[...].astype(F32)) * slope[...]
    frames = [total[:, t * pixels : (t + 1) * pixels] for t in range(out.shape[2])]
    out[:, 0] = jnp.stack(frames, axis=1).astype(BF16)


def sum_kernel(main, *refs):
    out, ins = refs[-1], refs[:-1]
    count = len(ins) // 2
    for k in range(count):
        total = ins[k][...].astype(F32) + ins[count + k][...].astype(F32)
        out[k * main : (k + 1) * main, :] = total.astype(BF16)


def finish_kernel(scale, main, whose, early, late, *refs):
    out, laid, sems = refs[-3:]
    channels = out.shape[2]
    first = early.shape[0] // main
    count = first + late.shape[0] // main
    rows, half = channels // count, out.shape[1] // 2
    unit = rows // 2
    which = lax.rem(lax.axis_index("tm") + whose, 2)
    shards = [shard_at(count, k) for k in range(count)]
    copies = []
    for a in range(3):
        for q in range(9):
            base = q * unit if q < 7 else a * 2 * unit + (q - 7) * unit
            step = a if q < 7 else 3
            total = None
            for k, shard in enumerate(shards):
                source, place = (early, k) if k < first else (late, k - first)
                piece = source[place * main + base : place * main + base + unit, :]
                mask = in_slot(channels, rows, lax.rem(shard + step, count))
                total = piece if total is None else jnp.where(mask, piece, total)
            if step:
                total = pltpu.roll(total, channels - step * rows, 1)
            total = total.astype(F32) * scale
            laid[a, q * unit : (q + 1) * unit, :] = total
            if q % 3 == 2:
                part = pl.ds((q - 2) * unit, 3 * unit)
                there = pl.ds(pl.multiple_of(which * half + (q - 2) * unit, 8), 3 * unit)
                copy = pltpu.make_async_copy(
                    laid.at[a, part], out.at[a, there], sems.at[len(copies)]
                )
                copy.start()
                copies.append(copy)
    for copy in copies:
        copy.wait()


def in_place(x):
    return pltpu.with_memory_space_constraint(x, pltpu.HBM)


def local_fast(features, kernel, cotangent):
    rows, _, frames, pixels = features.shape
    length = frames * pixels
    count = lax.axis_size("chan")
    channels = rows * count
    taps = kernel.shape[1]
    half = 9 * rows // 2
    main, _ = packed_rows(half)
    sds = jax.ShapeDtypeStruct
    block_shape = sds((rows, length), BF16)
    term_shape = sds((main, channels), BF16)
    stack_shape = sds((half, 2 * length), BF16)
    rhs = pltpu.VMEM((channels, 2 * length), BF16)

    def swap(x, far):
        return lax.ppermute(x, "chan", [(z, z ^ far) for z in range(count)])

    weights = jnp.transpose(kernel, (1, 0, 2)).reshape(taps * rows, channels)
    hbm = pl.BlockSpec(memory_space=pltpu.HBM)
    cot_other = rotate(cotangent, "tm", 1)
    activation, flat_own = run(
        activate_kernel,
        (in_place(features), in_place(cotangent)),
        in_specs=[hbm] * 2,
        out_shape=(block_shape, sds((rows, length), F32)),
        out_specs=(whole(),) * 2,
        scratch_shapes=[
            pltpu.VMEM(features.shape, BF16),
            pltpu.VMEM(features.shape, BF16),
            pltpu.SemaphoreType.DMA((2, 3)),
        ],
        name="activate",
    )
    other = rotate(activation, "tm", 1)
    near, far = swap(activation, 1), swap(activation, 2)
    own_term, stack, flat, weights = run(
        functools.partial(own_terms_kernel, pixels),
        (activation, other, flat_own, cot_other, in_place(weights)),
        in_specs=[whole()] * 4 + [hbm],
        out_shape=(
            term_shape,
            stack_shape,
            sds((rows, 2 * length), F32),
            sds(weights.shape, BF16),
        ),
        out_specs=(whole(),) * 4,
        scratch_shapes=[rhs, pltpu.SemaphoreType.DMA((1,))],
        name="own_terms",
    )
    terms, got = [own_term], [rotate(own_term, "dp", 1)]
    blocks = [activation, other]

    def terms_of(k, here, there, waits=()):
        blocks.extend((here, there))
        term = run(
            functools.partial(terms_kernel, pixels, k),
            (stack, *blocks[-2:]),
            waits=waits,
            out_shape=term_shape,
            out_specs=whole(),
            scratch_shapes=[rhs],
            name=f"terms_{k}",
        )
        terms.append(term)
        got.append(rotate(term, "dp", 1))
        return term

    own_share, kept, near_share, passed_share = run(
        functools.partial(share_kernel, pixels),
        (weights, flat, stack),
        waits=(own_term,),
        out_shape=(
            sds((rows, length), F32),
            sds((rows, length), F32),
            block_shape,
            block_shape,
        ),
        out_specs=(whole(),) * 4,
        scratch_shapes=[
            pltpu.VMEM((half, (frames + 2) * pixels), BF16),
            pltpu.VMEM((half, (frames + 2) * pixels), BF16),
            pltpu.VMEM((channels, length), F32),
        ],
        name="shares",
    )
    first_share = swap(near_share, 1)
    near = after(near, own_share, flops=NEAR_COST)
    far, message = run(
        pack_kernel,
        (far, passed_share),
        out_shape=(block_shape, sds((2, rows, length), BF16)),
        out_specs=(whole(),) * 2,
        cost_estimate=cost(FAR_COST),
        name="pack",
    )
    message = swap(message, 1)
    term = terms_of(1, near, rotate(near, "tm", 1), (own_share, far, got[0]))
    term = terms_of(2, far, rotate(far, "tm", 1), (term,))
    slope = run(
        functools.partial(slope_kernel, pixels),
        (features,),
        waits=(term,),
        out_shape=sds((rows, length), F32),
        out_specs=whole(),
        name="slope",
    )
    last, passed_share = run(
        unpack_kernel,
        (message,),
        waits=(slope, got[1]),
        out_shape=(block_shape, block_shape),
        out_specs=(whole(),) * 2,
        name="unpack",
    )
    carry = run(
        add_kernel,
        (kept, passed_share),
        out_shape=block_shape,
        out_specs=whole(),
        name="carry_share",
    )
    second_share = swap(carry, 2)
    term = terms_of(3, last, rotate(last, "tm", 1), (carry,))

    def sums(first, stop, waits=()):
        return run(
            functools.partial(sum_kernel, main),
            (*terms[first:stop], *got[first:stop]),
            waits=waits,
            out_shape=sds(((stop - first) * main, channels), BF16),
            out_specs=whole(),
            name=f"sums_{first}",
        )

    conv_out, token = run(
        functools.partial(conv_kernel, pixels),
        (weights, *blocks),
        waits=(term, got[2]),
        out_shape=(sds(features.shape, BF16), sds(TOKEN, F32)),
        out_specs=(whole(),) * 2,
        scratch_shapes=[pltpu.VMEM((channels, (frames + 2) * pixels), BF16)],
        name="conv",
    )
    early = sums(0, 2, (term,))
    gathered = run(
        gather_share_kernel,
        (own_share, second_share),
        waits=(token, early),
        out_shape=sds((rows, length), F32),
        out_specs=whole(),
        cost_estimate=cost(GATHER_COST),
        name="gather_share",
    )
    late = sums(2, count, (gathered,))
    scale = 1.0 / math.sqrt(lax.axis_size("dp") * lax.axis_size("tm") * length)

    def finish(whose, sums, base=(), waits=()):
        anywhere = pl.BlockSpec(memory_space=pl.ANY)
        return run(
            functools.partial(finish_kernel, scale, main, whose),
            (*sums, *base),
            waits=waits,
            in_specs=[whole()] * 2 + [anywhere] * len(base),
            out_shape=sds((3, 9 * rows, channels), F32),
            out_specs=anywhere,
            input_output_aliases={2: 0} if base else {},
            scratch_shapes=[pltpu.VMEM((3, half, channels), F32), pltpu.SemaphoreType.DMA((9,))],
            name=f"kernel_grad_{whose}",
        )

    feature_grad, token = run(
        functools.partial(feature_kernel, pixels),
        (slope, gathered, first_share),
        out_shape=(sds(features.shape, BF16), sds(TOKEN, F32)),
        out_specs=(whole(),) * 2,
        cost_estimate=cost(FEATURE_COST),
        name="feature_grad",
    )
    kernel_grad = finish(0, (early, late), (), (token,))
    kernel_grad = finish(1, (rotate(early, "tm", 1), rotate(late, "tm", 1)), (kernel_grad,))
    kernel_grad = jnp.transpose(kernel_grad.reshape(taps, rows, channels), (1, 0, 2))
    return (conv_out, feature_grad, kernel_grad)


def local(features, kernel, cotangent):
    rows, clips, _, pixels = features.shape
    fits = (
        clips == 1
        and lax.axis_size("tm") == 2
        and lax.axis_size("dp") == 2
        and rows % (2 * SUB) == 0
        and pixels % 128 == 0
        and kernel.shape[1] == 27
        and lax.axis_size("chan") == 4
    )
    return (local_fast if fits else local_generic)(features, kernel, cotangent)


def solution(mesh):
    return jax.shard_map(
        local,
        mesh=mesh,
        in_specs=(
            P("chan", ("groups", "dp"), "tm", None),
            P("chan", None, None),
            P("chan", ("groups", "dp"), "tm", None),
        ),
        out_specs=(
            P("chan", ("groups", "dp"), "tm", None),
            P("chan", ("groups", "dp"), "tm", None),
            P(("groups", "chan"), None, None),
        ),
        check_vma=False,
    )
```

```python
import functools
import math

import jax
import jax.numpy as jnp
from jax import lax
from jax.experimental import pallas as pl
from jax.experimental.pallas import tpu as pltpu
from jax.sharding import PartitionSpec as P

WID = 64
SUB = 16
F32 = jnp.float32
BF16 = jnp.bfloat16
VMEM_LIMIT = 24 * 1024 * 1024
TOKEN = (8, 128)
FEATURE_COST = 3 * 10**9
GATHER_COST = 3 * 10**9
FAR_COST = 10**9
NEAR_COST = 3 * 10**9


def from_behind(x, axis, by):
    size = lax.axis_size(axis)
    pairs = [(i, i + by) for i in range(size) if 0 <= i + by < size]
    return lax.ppermute(x, axis, pairs)


def padded_copies(block):
    pixels = block.shape[-1]
    column = lax.broadcasted_iota(jnp.int32, (pixels,), 0) % WID
    nothing = jnp.zeros((), block.dtype)
    widths = [(0, 0), (0, 0), (0, 0), (WID + 1, WID + 1)]
    left_cut = jnp.pad(jnp.where(column == WID - 1, nothing, block), widths)
    untouched = jnp.pad(block, widths)
    right_cut = jnp.pad(jnp.where(column == 0, nothing, block), widths)
    return (left_cut, untouched, right_cut)


def tap_window(copies, first_frame, vertical, horizontal, frames, pixels):
    source = copies[horizontal]
    offset = vertical * WID + horizontal
    return source[:, :, first_frame : first_frame + frames, offset : offset + pixels]


def stacked_taps(copies, first_frame, flipped, frames, pixels):
    pieces = []
    for vertical in range(3):
        for horizontal in range(3):
            if flipped:
                pieces.append(
                    tap_window(copies, first_frame, 2 - vertical, 2 - horizontal, frames, pixels)
                )
            else:
                pieces.append(tap_window(copies, first_frame, vertical, horizontal, frames, pixels))
    concatenated = jnp.concatenate(pieces, axis=0)
    return concatenated.reshape(concatenated.shape[0], -1)


def local_generic(features, kernel, cotangent):
    channels, clip_count, frames, pixels = features.shape
    flat_length = clip_count * frames * pixels
    widened = features.astype(F32)
    logistic = jax.nn.sigmoid(widened)
    activation = (widened * logistic).astype(BF16)
    slope_factor = logistic * (1.0 + widened * (1.0 - logistic))
    earlier = from_behind(activation[:, :, frames - 2 :, :], "tm", 1)
    extended = jnp.concatenate([earlier, activation], axis=2)
    upcoming = from_behind(cotangent[:, :, :2, :], "tm", -1)
    later_padded = jnp.concatenate([cotangent, upcoming], axis=2)
    cotangent_rows = cotangent.reshape(channels, -1)
    portion = lax.all_gather(extended, "chan", axis=0, tiled=True)
    out_sum = jnp.zeros((channels, flat_length), F32)
    amount = portion.shape[0]
    copies = padded_copies(portion)
    grad_parts = []
    for temporal in range(3):
        stacked = stacked_taps(copies, temporal, False, frames, pixels)
        weights = kernel[:, 9 * temporal : 9 * temporal + 9, :].reshape(channels, 9 * amount)
        out_sum = out_sum + jnp.dot(weights, stacked, preferred_element_type=F32)
        grad_parts.append(
            lax.dot_general(
                cotangent_rows, stacked, (((1,), (1,)), ((), ())), preferred_element_type=F32
            ).reshape(channels, 9, amount)
        )
    grad_sum = jnp.concatenate(grad_parts, axis=1)
    conv_out = out_sum.reshape(features.shape).astype(BF16)
    position_count = lax.axis_size("dp") * lax.axis_size("tm") * flat_length
    kernel_grad = lax.psum(grad_sum, ("tm", "dp")) * (1.0 / math.sqrt(position_count))
    padded_later = padded_copies(later_padded)
    summed = jnp.zeros((amount, flat_length), F32)
    for temporal in range(3):
        weights = jnp.transpose(
            kernel[:, 9 * temporal : 9 * temporal + 9, :], (2, 1, 0)
        ).reshape(amount, 9 * channels)
        stacked = stacked_taps(padded_later, 2 - temporal, True, frames, pixels)
        summed = summed + jnp.dot(weights, stacked, preferred_element_type=F32)
    before_slope = lax.psum_scatter(
        summed.reshape(amount, clip_count, frames, pixels), "chan", scatter_dimension=0, tiled=True
    )
    feature_grad = (before_slope * slope_factor).astype(BF16)
    return (conv_out, feature_grad, kernel_grad)


def rotate(x, axis, by):
    size = lax.axis_size(axis)
    return lax.ppermute(x, axis, [(i, (i + by) % size) for i in range(size)])


def shifted(frame, down, right):
    pixels = frame.shape[-1]
    if down == 0 and right == 0:
        return frame
    cell = lax.broadcasted_iota(jnp.int32, (1, pixels), 1)
    row, column = cell // WID + down, cell % WID + right
    inside = (row >= 0) & (row < pixels // WID) & (column >= 0) & (column < WID)
    moved = pltpu.roll(frame, (-(down * WID + right)) % pixels, 1)
    return jnp.where(inside, moved, 0.0)


def after(x, *others, flops=1):
    anywhere = pl.BlockSpec(memory_space=pl.ANY)
    return pl.pallas_call(
        lambda *refs: None,
        out_shape=jax.ShapeDtypeStruct(x.shape, x.dtype),
        in_specs=[anywhere] * (1 + len(others)),
        out_specs=anywhere,
        input_output_aliases={0: 0},
        compiler_params=pltpu.CompilerParams(vmem_limit_bytes=1024 * 1024),
        cost_estimate=cost(flops),
        name="hand_on",
    )(x, *others)


def run(kernel, args, waits=(), **options):
    options.setdefault("in_specs", [whole()] * len(args))
    options.setdefault("cost_estimate", cost())
    options["in_specs"] = list(options["in_specs"]) + [
        pl.BlockSpec(memory_space=pl.ANY) for _ in waits
    ]
    count = len(args)

    def body(*refs):
        kernel(*refs[:count], *refs[count + len(waits) :])

    return pl.pallas_call(
        body, compiler_params=pltpu.CompilerParams(vmem_limit_bytes=VMEM_LIMIT), **options
    )(*args, *waits)


def cost(flops=1):
    return pl.CostEstimate(flops=flops, bytes_accessed=1, transcendentals=0)


def whole():
    return pl.BlockSpec(memory_space=pltpu.VMEM)


def activate_kernel(features, cotangent, activation, flat, feat, cot, sems):
    parts = sems.shape[1]
    rows, _, frames, pixels = feat.shape
    size = rows // parts
    loads = []
    for n, (source, target) in enumerate(((features, feat), (cotangent, cot))):
        for part in range(parts):
            at = pl.ds(part * size, size)
            loads.append(pltpu.make_async_copy(source.at[at], target.at[at], sems.at[n, part]))
    for load in loads:
        load.start()
    for part in range(parts):
        loads[part].wait()
        at = slice(part * size, (part + 1) * size)
        v = feat[at, 0].astype(F32)
        act = v / (1.0 + jnp.exp(-v))
        for t in range(frames):
            activation[at, t * pixels : (t + 1) * pixels] = act[:, t, :].astype(BF16)
    for load in loads[parts:]:
        load.wait()
    flatten(pixels, cot, flat, 0)


def flatten(pixels, source, flat, first):
    wide = source[:, 0].astype(F32)
    for t in range(wide.shape[1]):
        at = (first + t) * pixels
        at = at if isinstance(at, int) else pl.multiple_of(at, pixels)
        flat[:, pl.ds(at, pixels)] = wide[:, t, :]


def shard_at(count, k):
    z = lax.axis_index("chan")
    return (z, z + 1 - 2 * lax.rem(z, 2), lax.rem(z + 2, count), count - 1 - z)[k]


def in_slot(channels, rows, slot):
    lane = lax.broadcasted_iota(jnp.int32, (1, channels), 1)
    return (lane >= slot * rows) & (lane < (slot + 1) * rows)


def packed_rows(total):
    unit = total // 9
    return 7 * unit, 2 * unit


def fill_stack(pixels, flat, stack, half, first, frames):
    unit = flat.shape[0] // 2
    for t in range(frames):
        at = slice(t * pixels, (t + 1) * pixels)
        source = slice((first + t) * pixels, (first + t + 1) * pixels)
        for q in range(9):
            tap, part = divmod(9 * half + q, 2)
            i, j = divmod(tap, 3)
            frame = flat[part * unit : (part + 1) * unit, source]
            stack[q * unit : (q + 1) * unit, at] = shifted(frame, 1 - i, 1 - j).astype(BF16)


def block_terms(pixels, k, stack, here, there, out, rhs):
    channels = out.shape[1]
    rows, length = here.shape
    lanes, count = 2 * length, channels // rows
    shard = shard_at(count, k)
    for core in range(2):

        @pl.when(lax.axis_index("tm") == core)
        def _(first=(here, there)[core], second=(there, here)[core]):
            for a in range(3):
                skip = (2 - a) * pixels
                at = pl.ds(pl.multiple_of(lax.rem(shard + a, count) * rows, SUB), rows)
                if skip:
                    rhs[at, :skip] = jnp.zeros((rows, skip), BF16)
                rhs[at, skip : skip + length] = first[...]
                rhs[at, skip + length :] = second[:, : length - skip]

    last = lax.rem(shard + 3, count)
    rhs[pl.ds(pl.multiple_of(last * rows, SUB), rows), :] = jnp.zeros((rows, lanes), BF16)
    terms = lax.dot_general(
        stack[...], rhs[...], (((1,), (1,)), ((), ())), preferred_element_type=F32
    )
    main, tail = packed_rows(terms.shape[0])
    free = in_slot(channels, rows, last)
    for a in range(3):
        at = slice(a * tail, (a + 1) * tail)
        moved = pltpu.roll(terms[main:], (3 - a) * rows, 1)
        out[at, :] = jnp.where(free, moved, terms[at]).astype(BF16)
    out[3 * tail :, :] = terms[3 * tail : main].astype(BF16)


def own_terms_kernel(
    pixels, mine, other, flat_own, cot_other, weights, out, stack, flat, held, rhs, sems
):
    load = pltpu.make_async_copy(weights, held, sems.at[0])
    load.start()
    length = flat_own.shape[1]
    me = lax.axis_index("tm")
    flat[:, pl.ds(pl.multiple_of(me * length, pixels), length)] = flat_own[...]
    flatten(pixels, cot_other, flat, (1 - me) * (length // pixels))
    for core in range(2):

        @pl.when(me == core)
        def _(core=core):
            fill_stack(pixels, flat, stack, core, 0, flat.shape[1] // pixels)

    block_terms(pixels, 0, stack, mine, other, out, rhs)
    load.wait()


def terms_kernel(pixels, k, stack, here, there, out, rhs):
    block_terms(pixels, k, stack, here, there, out, rhs)


def share_kernel(pixels, weights, flat, mine, own, kept, near, passed, window, other, total):
    rows, length = own.shape
    frames, half = length // pixels, mine.shape[0]
    count = weights.shape[1] // rows
    me = lax.axis_index("tm")
    front = 2 * pixels
    for core in range(2):

        @pl.when(me == core)
        def _(core=core):
            first = core * length
            held = min(length + front, mine.shape[1] - first)
            window[:, :held] = mine[:, first : first + held]
            if held < length + front:
                window[:, held:] = jnp.zeros((half, length + front - held), BF16)
                other[:, held:] = jnp.zeros((half, length + front - held), BF16)
            fill_stack(pixels, flat, other, 1 - core, core * frames, held // pixels)

    acc = None
    for a in range(3):
        lanes = slice((2 - a) * pixels, (2 - a) * pixels + length)
        for which, stack in ((me, window), (1 - me, other)):
            at = pl.multiple_of((2 * a + which) * half, SUB)
            term = lax.dot_general(
                weights[pl.ds(at, half), :],
                stack[:, lanes],
                (((0,), (0,)), ((), ())),
                preferred_element_type=F32,
            )
            acc = term if acc is None else acc + term
    total[...] = acc

    def part(k):
        return total[pl.ds(pl.multiple_of(shard_at(count, k) * rows, SUB), rows), :]

    own[...] = part(0)
    kept[...] = part(2)
    near[...] = part(1).astype(BF16)
    passed[...] = part(3).astype(BF16)


def pack_kernel(block, share, out, message):
    out[...] = block[...]
    message[0] = block[...]
    message[1] = share[...]


def unpack_kernel(message, block, share):
    block[...] = message[0]
    share[...] = message[1]


def add_kernel(kept, came, out):
    out[...] = (kept[...] + came[...].astype(F32)).astype(out.dtype)


def conv_kernel(pixels, weights, *refs):
    blocks, (out, token, act) = refs[:-3], refs[-3:]
    token[...] = jnp.zeros(TOKEN, F32)
    rows, _, frames, _ = out.shape
    count = weights.shape[1] // rows
    length, front = frames * pixels, 2 * pixels
    me = lax.axis_index("tm")
    for k in range(count):
        here, there = blocks[2 * k], blocks[2 * k + 1]
        at = pl.ds(pl.multiple_of(shard_at(count, k) * rows, SUB), rows)
        earlier = there[:, length - front :]
        act[at, :front] = jnp.where(me == 0, jnp.zeros_like(earlier), earlier)
        act[at, front:] = here[...]

    taps = 9 * rows
    for t in range(frames):
        z_t = None
        for a in range(3):
            term = jnp.dot(
                weights[a * taps : (a + 1) * taps, :],
                act[:, (t + a) * pixels : (t + a + 1) * pixels],
                preferred_element_type=F32,
            )
            z_t = term if z_t is None else z_t + term
        acc = None
        for i in range(3):
            for j in range(3):
                at = (3 * i + j) * rows
                moved = shifted(z_t[at : at + rows, :], i - 1, j - 1)
                acc = moved if acc is None else acc + moved
        out[:, 0, t, :] = acc.astype(BF16)


def slope_kernel(pixels, features, slope):
    v = features[:, 0].astype(F32)
    s = 1.0 / (1.0 + jnp.exp(-v))
    factor = s * (1.0 + v * (1.0 - s))
    for t in range(factor.shape[1]):
        slope[:, t * pixels : (t + 1) * pixels] = factor[:, t, :]


def gather_share_kernel(own, second, out):
    out[...] = own[...] + second[...].astype(F32)


def feature_kernel(pixels, slope, gathered, first, out, token):
    token[...] = jnp.zeros(TOKEN, F32)
    total = (gathered[...] + first[...].astype(F32)) * slope[...]
    frames = [total[:, t * pixels : (t + 1) * pixels] for t in range(out.shape[2])]
    out[:, 0] = jnp.stack(frames, axis=1).astype(BF16)


def sum_kernel(main, *refs):
    out, ins = refs[-1], refs[:-1]
    count = len(ins) // 2
    for k in range(count):
        total = ins[k][...].astype(F32) + ins[count + k][...].astype(F32)
        out[k * main : (k + 1) * main, :] = total.astype(BF16)


def finish_kernel(scale, main, whose, early, late, *refs):
    out, laid, sems = refs[-3:]
    channels = out.shape[2]
    first = early.shape[0] // main
    count = first + late.shape[0] // main
    rows, half = channels // count, out.shape[1] // 2
    unit = rows // 2
    which = lax.rem(lax.axis_index("tm") + whose, 2)
    shards = [shard_at(count, k) for k in range(count)]
    copies = []
    for a in range(3):
        for q in range(9):
            base = q * unit if q < 7 else a * 2 * unit + (q - 7) * unit
            step = a if q < 7 else 3
            total = None
            for k, shard in enumerate(shards):
                source, place = (early, k) if k < first else (late, k - first)
                piece = source[place * main + base : place * main + base + unit, :]
                mask = in_slot(channels, rows, lax.rem(shard + step, count))
                total = piece if total is None else jnp.where(mask, piece, total)
            if step:
                total = pltpu.roll(total, channels - step * rows, 1)
            total = total.astype(F32) * scale
            laid[a, q * unit : (q + 1) * unit, :] = total
            if q % 3 == 2:
                part = pl.ds((q - 2) * unit, 3 * unit)
                there = pl.ds(pl.multiple_of(which * half + (q - 2) * unit, 8), 3 * unit)
                copy = pltpu.make_async_copy(
                    laid.at[a, part], out.at[a, there], sems.at[len(copies)]
                )
                copy.start()
                copies.append(copy)
    for copy in copies:
        copy.wait()


def in_place(x):
    return pltpu.with_memory_space_constraint(x, pltpu.HBM)


def local_fast(features, kernel, cotangent):
    rows, _, frames, pixels = features.shape
    length = frames * pixels
    count = lax.axis_size("chan")
    channels = rows * count
    taps = kernel.shape[1]
    half = 9 * rows // 2
    main, _ = packed_rows(half)
    sds = jax.ShapeDtypeStruct
    block_shape = sds((rows, length), BF16)
    term_shape = sds((main, channels), BF16)
    stack_shape = sds((half, 2 * length), BF16)
    rhs = pltpu.VMEM((channels, 2 * length), BF16)

    def swap(x, far):
        return lax.ppermute(x, "chan", [(z, z ^ far) for z in range(count)])

    weights = jnp.transpose(kernel, (1, 0, 2)).reshape(taps * rows, channels)
    hbm = pl.BlockSpec(memory_space=pltpu.HBM)
    cot_other = rotate(cotangent, "tm", 1)
    activation, flat_own = run(
        activate_kernel,
        (in_place(features), in_place(cotangent)),
        in_specs=[hbm] * 2,
        out_shape=(block_shape, sds((rows, length), F32)),
        out_specs=(whole(),) * 2,
        scratch_shapes=[
            pltpu.VMEM(features.shape, BF16),
            pltpu.VMEM(features.shape, BF16),
            pltpu.SemaphoreType.DMA((2, 3)),
        ],
        name="activate",
    )
    other = rotate(activation, "tm", 1)
    near, far = swap(activation, 1), swap(activation, 2)
    own_term, stack, flat, weights = run(
        functools.partial(own_terms_kernel, pixels),
        (activation, other, flat_own, cot_other, in_place(weights)),
        in_specs=[whole()] * 4 + [hbm],
        out_shape=(
            term_shape,
            stack_shape,
            sds((rows, 2 * length), F32),
            sds(weights.shape, BF16),
        ),
        out_specs=(whole(),) * 4,
        scratch_shapes=[rhs, pltpu.SemaphoreType.DMA((1,))],
        name="own_terms",
    )
    terms, got = [own_term], [rotate(own_term, "dp", 1)]
    blocks = [activation, other]

    def terms_of(k, here, there, waits=()):
        blocks.extend((here, there))
        term = run(
            functools.partial(terms_kernel, pixels, k),
            (stack, *blocks[-2:]),
            waits=waits,
            out_shape=term_shape,
            out_specs=whole(),
            scratch_shapes=[rhs],
            name=f"terms_{k}",
        )
        terms.append(term)
        got.append(rotate(term, "dp", 1))
        return term

    own_share, kept, near_share, passed_share = run(
        functools.partial(share_kernel, pixels),
        (weights, flat, stack),
        waits=(own_term,),
        out_shape=(
            sds((rows, length), F32),
            sds((rows, length), F32),
            block_shape,
            block_shape,
        ),
        out_specs=(whole(),) * 4,
        scratch_shapes=[
            pltpu.VMEM((half, (frames + 2) * pixels), BF16),
            pltpu.VMEM((half, (frames + 2) * pixels), BF16),
            pltpu.VMEM((channels, length), F32),
        ],
        name="shares",
    )
    near = after(near, own_share, flops=NEAR_COST)
    far, message = run(
        pack_kernel,
        (far, passed_share),
        out_shape=(block_shape, sds((2, rows, length), BF16)),
        out_specs=(whole(),) * 2,
        cost_estimate=cost(FAR_COST),
        name="pack",
    )
    message = swap(message, 1)
    term = terms_of(1, near, rotate(near, "tm", 1), (own_share, far, got[0]))
    term = terms_of(2, far, rotate(far, "tm", 1), (term,))
    slope = run(
        functools.partial(slope_kernel, pixels),
        (features,),
        waits=(term,),
        out_shape=sds((rows, length), F32),
        out_specs=whole(),
        name="slope",
    )
    last, passed_share = run(
        unpack_kernel,
        (message,),
        waits=(slope, got[1]),
        out_shape=(block_shape, block_shape),
        out_specs=(whole(),) * 2,
        name="unpack",
    )
    carry = run(
        add_kernel,
        (kept, passed_share),
        out_shape=block_shape,
        out_specs=whole(),
        name="carry_share",
    )
    second_share = swap(carry, 2)
    term = terms_of(3, last, rotate(last, "tm", 1), (carry,))
    first_share = swap(after(near_share, term), 1)

    def sums(first, stop, waits=()):
        return run(
            functools.partial(sum_kernel, main),
            (*terms[first:stop], *got[first:stop]),
            waits=waits,
            out_shape=sds(((stop - first) * main, channels), BF16),
            out_specs=whole(),
            name=f"sums_{first}",
        )

    conv_out, token = run(
        functools.partial(conv_kernel, pixels),
        (weights, *blocks),
        waits=(term, got[2]),
        out_shape=(sds(features.shape, BF16), sds(TOKEN, F32)),
        out_specs=(whole(),) * 2,
        scratch_shapes=[pltpu.VMEM((channels, (frames + 2) * pixels), BF16)],
        name="conv",
    )
    early = sums(0, 2, (term,))
    gathered = run(
        gather_share_kernel,
        (own_share, second_share),
        waits=(token, early),
        out_shape=sds((rows, length), F32),
        out_specs=whole(),
        cost_estimate=cost(GATHER_COST),
        name="gather_share",
    )
    feature_grad, token = run(
        functools.partial(feature_kernel, pixels),
        (slope, gathered, first_share),
        out_shape=(sds(features.shape, BF16), sds(TOKEN, F32)),
        out_specs=(whole(),) * 2,
        cost_estimate=cost(FEATURE_COST),
        name="feature_grad",
    )
    late = sums(2, count, (token,))
    scale = 1.0 / math.sqrt(lax.axis_size("dp") * lax.axis_size("tm") * length)

    def finish(whose, sums, base=()):
        anywhere = pl.BlockSpec(memory_space=pl.ANY)
        return run(
            functools.partial(finish_kernel, scale, main, whose),
            (*sums, *base),
            in_specs=[whole()] * 2 + [anywhere] * len(base),
            out_shape=sds((3, 9 * rows, channels), F32),
            out_specs=anywhere,
            input_output_aliases={2: 0} if base else {},
            scratch_shapes=[pltpu.VMEM((3, half, channels), F32), pltpu.SemaphoreType.DMA((9,))],
            name=f"kernel_grad_{whose}",
        )

    kernel_grad = finish(0, (early, late))
    kernel_grad = finish(1, (rotate(early, "tm", 1), rotate(late, "tm", 1)), (kernel_grad,))
    kernel_grad = jnp.transpose(kernel_grad.reshape(taps, rows, channels), (1, 0, 2))
    return (conv_out, feature_grad, kernel_grad)


def local(features, kernel, cotangent):
    rows, clips, _, pixels = features.shape
    fits = (
        clips == 1
        and lax.axis_size("tm") == 2
        and lax.axis_size("dp") == 2
        and rows % (2 * SUB) == 0
        and pixels % 128 == 0
        and kernel.shape[1] == 27
        and lax.axis_size("chan") == 4
    )
    return (local_fast if fits else local_generic)(features, kernel, cotangent)


def solution(mesh):
    return jax.shard_map(
        local,
        mesh=mesh,
        in_specs=(
            P("chan", ("groups", "dp"), "tm", None),
            P("chan", None, None),
            P("chan", ("groups", "dp"), "tm", None),
        ),
        out_specs=(
            P("chan", ("groups", "dp"), "tm", None),
            P("chan", ("groups", "dp"), "tm", None),
            P(("groups", "chan"), None, None),
        ),
        check_vma=False,
    )
```
